32 devices in a mesh: ctx: 8 (over z, core), head: 4 (over y, x).
Axes of the slice: x: 2, y: 2, z: 4, core: 2. Of those that a mesh axis runs over, the one named last changes fastest.
Arguments:
- queries: bfloat16 [2048, 8192], P('ctx', 'head'), may hold values from -40 to 40
- keys: bfloat16 [2048, 1024], P('ctx', 'head'), may hold values from -4 to 4
- values: bfloat16 [2048, 1024], P('ctx', 'head'), may hold values from -6 to 6
- out_weight: bfloat16 [8192, 8192], P(None, 'head'), may hold values from -0.1796875 to 0.1796875
- doc_lengths: int32 [16], replicated, may hold values from 1 to 512, 2048 in all
- owners: int32 [64, 1], replicated, may hold values from 0 to 7; in each aligned block of 8 rows (0 to 7, 8 to 15, ...) no two rows name the same one
Outputs:
- attended: bfloat16 [8192, 2048], P('head', 'ctx')
The draws below stay inside these ranges and needn't reach their ends.
Inputs may be any that keep to these rules, and one draw needn't show every extreme that they name: `owners`: among the 8 pieces loaded by one index of ctx (aligned blocks of 8 rows) every owner appears at most once. `doc_lengths`: the lengths sum to 2048; the longest is exactly 512.
All inputs are finite; a program needn't handle non-finite values.
Results may differ from the reference program's by a relative error of at most 0.018.
Values may be sent and summed in bfloat16 or wider, within the bound.
No kernel may reach another device: no remote copies, remote signals or barrier semaphores. Data moves between devices by JAX's collectives and lax.ppermute only.
A program may use at most 128 MiB of HBM per device.

```python
import math
import jax
import jax.numpy as jnp
import numpy as np
from jax import lax

D = 8192
QUERY_HEAD_COUNT = 64
KEY_VALUE_HEADS = 8
HEAD_SIZE = 128
PIECES = 8
NDOC = 16
PACKED_TOKENS = 2048
PIECE = 32
QW = 8192
KW = 1024
N_CTX = 8
N_HEAD = 4


def closing_keys(key):
    start_offset = jax.random.fold_in(key, 7)
    lookup_grid = jnp.clip(jax.random.normal(start_offset, (PACKED_TOKENS, KW), jnp.float32), -4.0, 4.0)
    return lookup_grid


def draw_keys(key, part):
    return closing_keys(key).astype(jnp.bfloat16)


def draw_queries(key, part):
    group_length = QUERY_HEAD_COUNT // KEY_VALUE_HEADS
    start_offset = jax.random.fold_in(key, 5)
    lookup_grid = jnp.clip(1.5 * jax.random.normal(start_offset, (PACKED_TOKENS, KEY_VALUE_HEADS, group_length, HEAD_SIZE), jnp.float32), -6.0, 6.0)
    return lookup_grid.reshape(PACKED_TOKENS, QUERY_HEAD_COUNT * HEAD_SIZE).astype(jnp.bfloat16)


def steps_of(stream_key, extent, pieces, smallest, high):
    gain, own = 1.0, jax.random.fold_in(stream_key, 6)
    for axis_at, blocks in pieces:
        heights = jnp.exp(jax.random.uniform(jax.random.fold_in(own, axis_at), (blocks,), jnp.float32, smallest / len(pieces), high / len(pieces)))
        gain = gain * jnp.repeat(heights, extent[axis_at] // blocks).reshape([-1 if axis == axis_at else 1 for axis in range(len(extent))])
    return gain


def profile(number_of, total, limit, skew):
    weights = [(1 << 20) // math.isqrt(grade ** skew) + 1 for grade in range(2, number_of + 1)]
    rest, counts = total - limit - (number_of - 1), [1] * (number_of - 1)
    while rest > 0:
        movable = [i for i in range(number_of - 1) if counts[i] < limit]
        whole, budget = sum([weights[i] for i in movable]), rest
        for i in movable:
            more = min(limit - counts[i], max(1, budget * weights[i] // whole), rest)
            counts[i] = counts[i] + more
            rest = rest - more
    return np.array([limit] + counts)


def ragged_sizes(own_key, amount, total, reach, skew):
    if amount == 2:
        one = jax.random.randint(own_key, (), max(1, total - reach), min(reach, total - 1) + 1)
        return jnp.stack([one, total - one])
    lengths = jnp.asarray(profile(amount, total, reach, skew), jnp.int32)
    couples = (amount - 1) // 2
    source_of, sink = lengths[1:1 + 2 * couples:2], lengths[2:2 + 2 * couples:2]
    room = jnp.minimum(source_of - 1, reach - sink)
    moved = jax.random.randint(jax.random.fold_in(own_key, 1), (couples,), 0, 1 << 20) % (room + 1)
    lengths = lengths.at[1:1 + 2 * couples:2].set(source_of - moved).at[2:2 + 2 * couples:2].set(sink + moved)
    return lengths[jax.random.permutation(jax.random.fold_in(own_key, 2), amount)]


def assign_block(rng, own, number, rows, amount, top, most, skew):
    ranking = jax.random.permutation(rng, amount)
    crowded, ordinary = portions_of(amount, rows * top, most, skew, True), portions_of(amount, rows * top, most, skew, False)
    places = jnp.arange(amount)

    def named(sizes, offset_by):
        used = int((sizes > 0).sum())
        fixed = max(1, used // 4)
        moved = fixed + (places - fixed + offset_by * (used - fixed)) % max(1, amount - fixed)
        return jnp.zeros((amount,), jnp.int32).at[ranking[jnp.where(places < fixed, places, moved)]].set(jnp.asarray(sizes, jnp.int32))

    sizes = jnp.where(number % 4 == 0, named(crowded, number // 4), named(ordinary, number - number // 4 - 1))
    mixed = jax.random.permutation(jax.random.fold_in(own, 3), amount)
    source_of, taker = mixed[0:amount // 2 * 2:2], mixed[1:amount // 2 * 2:2]
    margin = jnp.minimum(sizes[source_of] - 1, most - sizes[taker]) // 2
    margin = jnp.where((source_of == ranking[0]) | (taker == ranking[0]) | (sizes[taker] == 0), 0, jnp.maximum(margin, 0))
    moved = jax.random.randint(jax.random.fold_in(own, 4), (amount // 2,), 0, 1 << 20) % (margin + 1)
    sizes = sizes.at[source_of].add(-moved).at[taker].add(moved)
    members = jnp.searchsorted(jnp.cumsum(sizes), jnp.arange(rows * top), side="right").astype(jnp.int32)
    listing = members.reshape(top, rows).T
    listing = listing[jax.random.permutation(jax.random.fold_in(own, 1), rows)]
    offset_by = jax.random.randint(jax.random.fold_in(own, 2), (rows, 1), 0, top)
    return jnp.take_along_axis(listing, (jnp.arange(top)[None, :] + offset_by) % top, axis=1)


def portions_of(number_of, total, limit, lean, full):
    portions = [(1 << 20) // math.isqrt(standing ** lean) + 1 for standing in range(1, number_of + 1)]
    largest = limit if full else min(limit, max(-(-total // number_of), total * portions[0] // sum(portions)))
    least = 1 if total - largest >= number_of - 1 else 0
    holding, rest = [largest] + [least] * (number_of - 1), total - largest - least * (number_of - 1)
    while rest > 0:
        movable = [i for i in range(1, number_of) if holding[i] < largest] or [i for i in range(1, number_of) if holding[i] < limit]
        pool, left = sum([portions[i] for i in movable]), rest
        for i in movable:
            more = min(limit - holding[i], max(1, left * portions[i] // pool), rest)
            holding[i] = holding[i] + more
            rest = rest - more
    return np.array(holding)


def gaussian(rng, shape, deviation, limit, pieces=(), held_as=jnp.bfloat16):
    entries = deviation * jax.random.normal(rng, shape, jnp.float32)
    if pieces:
        entries = entries * steps_of(rng, shape, pieces, -0.22, 0.18)
    return jnp.clip(entries, -limit, limit).astype(held_as)


def setup_inputs(seed: int = 0) -> dict:
    key_of = jax.random.split(jax.random.key(seed), 7)
    queries = draw_queries(jax.random.fold_in(key_of[6], 71), 0)
    keys = draw_keys(jax.random.fold_in(key_of[6], 71), 0)
    values = gaussian(key_of[2], (PACKED_TOKENS, KW), 1.0, 6.0, ((0, 8), (1, 4)))
    out_weight = gaussian(key_of[3], (D, QW), 0.03, 0.1796875, ((1, 4),))
    doc_lengths = ragged_sizes(key_of[4], NDOC, PACKED_TOKENS, PACKED_TOKENS // 4, 2).astype(jnp.int32)
    owners_keys = jax.random.split(jax.random.fold_in(key_of[5], 1), (PIECES * N_CTX) // PIECES)
    owners_turns = jax.random.permutation(jax.random.fold_in(key_of[5], 3), (PIECES * N_CTX) // PIECES)
    owners = jax.vmap(lambda own, number: assign_block(jax.random.fold_in(key_of[5], 2), own, number, PIECES, N_CTX, 1, 1, 2))(owners_keys, owners_turns).reshape((PIECES * N_CTX, 1))
    return {"queries": queries, "keys": keys, "values": values, "out_weight": out_weight, "doc_lengths": doc_lengths, "owners": owners}


MASKED = -1e+30

def document_index(positions, doc_starts):
    return lax.optimization_barrier(jnp.sum((positions[:, None] >= doc_starts[None, :]).astype(jnp.int32), axis=1)) - 1

def reference(queries, keys, values, out_weight, doc_lengths, owners):
    total_rows = queries.shape[0]
    group_length = QUERY_HEAD_COUNT // KEY_VALUE_HEADS
    positions = jnp.arange(total_rows, dtype=jnp.int32)
    doc_ends = jnp.cumsum(doc_lengths).astype(jnp.int32)
    doc_starts = doc_ends - doc_lengths
    doc_ids = document_index(positions, doc_starts)
    allowed = (doc_ids[:, None] == doc_ids[None, :]) & (positions[None, :] <= positions[:, None])
    score_scale = 1.0 / math.sqrt(HEAD_SIZE)

    def one_head(head):
        query_head = lax.dynamic_slice_in_dim(queries, head * HEAD_SIZE, HEAD_SIZE, 1)
        key_head = lax.dynamic_slice_in_dim(keys, head // group_length * HEAD_SIZE, HEAD_SIZE, 1)
        value_head = lax.dynamic_slice_in_dim(values, head // group_length * HEAD_SIZE, HEAD_SIZE, 1)
        scores = lax.dot_general(query_head, key_head, (((1,), (1,)), ((), ())), preferred_element_type=jnp.float32) * score_scale
        scores = jnp.where(allowed, scores, MASKED)
        shifted = jnp.exp(scores - lax.optimization_barrier(jnp.max(scores, axis=1, keepdims=True)))
        shifted = jnp.where(allowed, shifted, 0.0)
        weights = (shifted / lax.optimization_barrier(jnp.sum(shifted, axis=1, keepdims=True))).astype(jnp.bfloat16)
        return jnp.dot(weights, value_head, preferred_element_type=jnp.float32).astype(jnp.bfloat16)
    heads_out = lax.map(one_head, jnp.arange(QUERY_HEAD_COUNT, dtype=jnp.int32))
    context = jnp.transpose(heads_out, (1, 0, 2)).reshape(total_rows, QUERY_HEAD_COUNT * HEAD_SIZE)
    group_width = QUERY_HEAD_COUNT * HEAD_SIZE // N_HEAD

    def add_group(summed, group_index):
        context_part = lax.dynamic_slice_in_dim(context, group_index * group_width, group_width, 1)
        weight_part = lax.dynamic_slice_in_dim(out_weight, group_index * group_width, group_width, 1)
        partial_sum = lax.dot_general(weight_part, context_part, (((1,), (1,)), ((), ())), preferred_element_type=jnp.float32)
        rounded = lax.optimization_barrier(partial_sum.astype(jnp.bfloat16))
        return (summed + rounded.astype(jnp.float32), None)
    summed, unused = lax.scan(add_group, jnp.zeros((D, total_rows), jnp.float32), jnp.arange(N_HEAD, dtype=jnp.int32))
    projected = summed.astype(jnp.bfloat16)
    owner_table = owners[:, 0].reshape(N_CTX, PIECES)
    owner_ids = jnp.arange(N_CTX, dtype=jnp.int32)
    slot_hits = (owner_table[None, :, :] == owner_ids[:, None, None]).astype(jnp.int32)
    slot_live = lax.optimization_barrier(jnp.sum(slot_hits, axis=2)) > 0
    picked = lax.optimization_barrier(jnp.sum(slot_hits * jnp.arange(PIECES, dtype=jnp.int32)[None, None, :], axis=2))
    column = (owner_ids[None, :, None] * PIECES + picked[:, :, None]) * PIECE + jnp.arange(PIECE, dtype=jnp.int32)[None, None, :]
    gathered = jnp.take(projected, column.reshape(-1).astype(jnp.int32), axis=1)
    live_columns = jnp.broadcast_to(slot_live[:, :, None], column.shape).reshape(-1)
    return jnp.where(live_columns[None, :], gathered, jnp.zeros((), jnp.bfloat16))
```

```python
import functools
import math

import jax
import jax.numpy as jnp
from jax import lax
from jax.experimental import pallas as pl
from jax.experimental.pallas import tpu as pltpu
from jax.sharding import PartitionSpec as P

HEAD_SIZE = 128
PIECES = 8
N_FAST_HEAD = 4


MASKED = -1e30


def document_index(positions, doc_starts):
    return jnp.sum((positions[:, None] >= doc_starts[None, :]).astype(jnp.int32), axis=1) - 1


def attend(query_rows, query_pos, keys, values, doc_starts):
    row_count = query_rows.shape[0]
    key_heads = keys.shape[1] // HEAD_SIZE
    group_length = query_rows.shape[1] // keys.shape[1]
    query_heads = query_rows.reshape(row_count, key_heads, group_length, HEAD_SIZE)
    query_doc = document_index(query_pos, doc_starts)
    score_scale = 1.0 / math.sqrt(HEAD_SIZE)
    initial = (
        jnp.full((row_count, key_heads, group_length), MASKED, jnp.float32),
        jnp.zeros((row_count, key_heads, group_length), jnp.float32),
        jnp.zeros((row_count, key_heads, group_length, HEAD_SIZE), jnp.float32),
    )
    key_piece = lax.all_gather(keys, "ctx", axis=0, tiled=True)
    value_piece = lax.all_gather(values, "ctx", axis=0, tiled=True)
    piece_rows = key_piece.shape[0]
    tile_rows = math.gcd(piece_rows, 512)

    def one_tile(tile_index, running):
        tile_start = tile_index * tile_rows
        key_block = lax.dynamic_slice_in_dim(key_piece, tile_start, tile_rows, 0).reshape(
            tile_rows, key_heads, HEAD_SIZE
        )
        value_block = lax.dynamic_slice_in_dim(value_piece, tile_start, tile_rows, 0).reshape(
            tile_rows, key_heads, HEAD_SIZE
        )
        key_pos = tile_start + jnp.arange(tile_rows, dtype=jnp.int32)
        key_doc = document_index(key_pos, doc_starts)
        allowed = (query_doc[:, None] == key_doc[None, :]) & (
            key_pos[None, :] <= query_pos[:, None]
        )
        running_max, running_sum, weighted = running
        scores = (
            jnp.einsum("rkgd,nkd->rkgn", query_heads, key_block, preferred_element_type=jnp.float32)
            * score_scale
        )
        allowed_all = allowed[:, None, None, :]
        scores = jnp.where(allowed_all, scores, MASKED)
        new_max = jnp.maximum(running_max, jnp.max(scores, axis=-1))
        factor = jnp.exp(running_max - new_max)
        weights = jnp.where(allowed_all, jnp.exp(scores - new_max[..., None]), 0.0)
        new_sum = running_sum * factor + jnp.sum(weights, axis=-1)
        new_weighted = weighted * factor[..., None] + jnp.einsum(
            "rkgn,nkd->rkgd",
            weights.astype(jnp.bfloat16),
            value_block,
            preferred_element_type=jnp.float32,
        )
        return (new_max, new_sum, new_weighted)

    final_max, final_sum, weighted = lax.fori_loop(0, piece_rows // tile_rows, one_tile, initial)
    result = weighted / jnp.maximum(final_sum, 1.0)[..., None]
    return result.reshape(row_count, key_heads * group_length * HEAD_SIZE).astype(jnp.bfloat16)


def project(context, out_weight):
    return lax.psum_scatter(
        lax.dot_general(
            out_weight, context, (((1,), (1,)), ((), ())), preferred_element_type=jnp.float32
        ).astype(jnp.bfloat16),
        "head",
        scatter_dimension=0,
        tiled=True,
    )


def per_device(queries, keys, values, out_weight, doc_lengths, owners):
    place_count = lax.axis_size("ctx")
    own_index = lax.axis_index("ctx")
    token_count = queries.shape[0]
    block_rows = token_count // PIECES
    doc_ends = jnp.cumsum(doc_lengths)
    doc_starts = doc_ends - doc_lengths
    owner_table = owners[:, 0].reshape(place_count, PIECES)
    own_owners = lax.dynamic_index_in_dim(owner_table, own_index, 0, keepdims=False)
    place_ids = jnp.arange(place_count, dtype=jnp.int32)
    send_pick = (own_owners[None, :] == place_ids[:, None]).astype(jnp.bfloat16)
    grouped = queries.reshape(PIECES, block_rows, queries.shape[1])
    outgoing = jnp.einsum(
        "oc,chw->ohw", send_pick, grouped, preferred_element_type=jnp.float32
    ).astype(jnp.bfloat16)
    arrived = lax.all_to_all(outgoing, "ctx", split_axis=0, concat_axis=0, tiled=True)
    slot_hits = (owner_table == own_index).astype(jnp.int32)
    slot_live = jnp.sum(slot_hits, axis=1)
    picked = jnp.sum(slot_hits * jnp.arange(PIECES, dtype=jnp.int32)[None, :], axis=1)
    slot_pos = (place_ids[:, None] * PIECES + picked[:, None]) * block_rows + jnp.arange(
        block_rows, dtype=jnp.int32
    )[None, :]
    query_pos = jnp.where(slot_live[:, None] > 0, slot_pos, -1).reshape(-1)
    context = attend(
        arrived.reshape(place_count * block_rows, queries.shape[1]),
        query_pos,
        keys,
        values,
        doc_starts,
    )
    return project(context, out_weight)


def _find_piece(owners_ref, source, owner):
    piece = jnp.int32(0)
    for i in range(PIECES):
        piece = jnp.where(owners_ref[source * PIECES + i, 0] == owner, jnp.int32(i), piece)
    return piece


def _queries_for_other_core(meta_ref, owners_ref, queries_ref, out_ref, sems):
    c = meta_ref[0]
    core = lax.rem(c, 2)
    copies = []
    for j in range(PIECES // 2):
        piece = _find_piece(owners_ref, c, 2 * j + 1 - core)
        rows = queries_ref.shape[0] // PIECES
        copies.append(
            pltpu.make_async_copy(
                queries_ref.at[pl.ds(pl.multiple_of(piece * rows, rows), rows)],
                out_ref.at[pl.ds(j * rows, rows)],
                sems.at[j],
            )
        )
    for copy in copies:
        copy.start()
    for copy in copies:
        copy.wait()


def _attend_kernel(
    groups, meta_ref, owners_ref, lengths_ref, queries_ref, other_ref,
    k0_ref, k1_ref, k2_ref, k3_ref, v0_ref, v1_ref, v2_ref, v3_ref,
    *rest,
):
    out_refs, (kbuf, vbuf, qbuf, ctxbuf, kv_sems, q_sems) = rest[: len(groups)], rest[len(groups):]
    c = meta_ref[0]
    core = lax.rem(c, 2)
    z = lax.div(c, 2)
    rows = k0_ref.shape[0]
    piece_rows = rows // PIECES
    tile = 128
    slots = (2 + core, 3 - core, core, 1 - core)
    copies = []
    for b, (k_ref, v_ref) in enumerate(((k0_ref, v0_ref), (k1_ref, v1_ref), (k2_ref, v2_ref), (k3_ref, v3_ref))):
        at = pl.ds(pl.multiple_of(slots[b] * rows, rows), rows)
        copies.append(pltpu.make_async_copy(k_ref, kbuf.at[at], kv_sems.at[2 * b]))
        copies.append(pltpu.make_async_copy(v_ref, vbuf.at[at], kv_sems.at[2 * b + 1]))
    starts = []
    for n, k in enumerate(groups):
        zdest = z ^ k
        owner = 2 * zdest + core
        mine = _find_piece(owners_ref, c, owner)
        theirs = _find_piece(owners_ref, c + 1 - 2 * core, owner)
        mine_at = 2 * n + core
        copies.append(pltpu.make_async_copy(
            queries_ref.at[pl.ds(pl.multiple_of(mine * piece_rows, piece_rows), piece_rows)],
            qbuf.at[mine_at], q_sems.at[2 * n]))
        copies.append(pltpu.make_async_copy(
            other_ref.at[pl.ds(pl.multiple_of(zdest * piece_rows, piece_rows), piece_rows)],
            qbuf.at[2 * n + 1 - core], q_sems.at[2 * n + 1]))
        at0 = jnp.where(core == 0, mine, theirs)
        at1 = jnp.where(core == 0, theirs, mine)
        starts.append((at0 * piece_rows, rows + at1 * piece_rows))
    for copy in copies:
        copy.start()
    doc_start = []
    running = jnp.int32(0)
    for d in range(lengths_ref.shape[0]):
        doc_start.append(running)
        running = running + lengths_ref[d]
    for copy in copies:
        copy.wait()
    base = 2 * rows * (z - 1)
    heads = k0_ref.shape[1] // HEAD_SIZE
    group = queries_ref.shape[1] // k0_ref.shape[1]
    scale = math.log2(math.e) / math.sqrt(HEAD_SIZE)
    span = 5 * tile

    def one_piece(n, p0):
        first = lax.div(p0, tile) * tile + 2 * rows - 4 * tile
        first = pl.multiple_of(first, tile)
        lane = lax.broadcasted_iota(jnp.int32, (1, tile), 1)
        pos = 2 * rows * z + p0 + lax.rem(lane, piece_rows)
        low = jnp.zeros((1, tile), jnp.int32)
        for start in doc_start:
            low = jnp.where(pos >= start, start, low)
        key_pos = base + first + lax.broadcasted_iota(jnp.int32, (span, tile), 0)
        allowed = (key_pos >= low) & (key_pos <= pos)
        allowed = jnp.concatenate([allowed] * (group * piece_rows // tile), axis=1)
        for kv in range(heads):
            cols = pl.ds(kv * HEAD_SIZE, HEAD_SIZE)
            q = jnp.concatenate(
                [qbuf[n, :, pl.ds((kv * group + g) * HEAD_SIZE, HEAD_SIZE)] for g in range(group)], axis=0)
            k = kbuf[pl.ds(first, span), cols]
            v = vbuf[pl.ds(first, span), cols]
            s = lax.dot_general(k, q, (((1,), (1,)), ((), ())), preferred_element_type=jnp.float32) * scale
            s = jnp.where(allowed, s, MASKED)
            top = jnp.max(s, axis=0, keepdims=True)
            w = jnp.exp2(s - top)
            total = jnp.sum(w, axis=0, keepdims=True)
            o = lax.dot_general(v, w.astype(jnp.bfloat16), (((0,), (0,)), ((), ())),
                                preferred_element_type=jnp.float32)
            o = (o / total).T.astype(jnp.bfloat16)
            for g in range(group):
                ctxbuf[n, :, pl.ds((kv * group + g) * HEAD_SIZE, HEAD_SIZE)] = o[g * piece_rows:(g + 1) * piece_rows]

    def step(n, carry):
        p0 = starts[0][0]
        for m in range(1, 2 * len(groups)):
            p0 = jnp.where(n == m, starts[m // 2][m % 2], p0)
        one_piece(n, p0)
        return carry

    lax.fori_loop(0, 2 * len(groups), step, 0)
    for n, out_ref in enumerate(out_refs):
        out_ref[...] = ctxbuf[2 * n:2 * n + 2].reshape(out_ref.shape)


def _attend_groups(groups, meta, owners, lengths, queries, other, kv):
    piece = queries.shape[0] // PIECES
    rows = kv[0].shape[0]
    smem = pl.BlockSpec(memory_space=pltpu.SMEM)
    hbm = pl.BlockSpec(memory_space=pl.ANY)
    vmem = pl.BlockSpec(memory_space=pltpu.VMEM)
    return pl.pallas_call(
        functools.partial(_attend_kernel, groups),
        out_shape=[jax.ShapeDtypeStruct((2 * piece, queries.shape[1]), jnp.bfloat16) for _ in groups],
        in_specs=[smem] * 3 + [hbm] * 10,
        out_specs=[vmem] * len(groups),
        scratch_shapes=[
            pltpu.VMEM((4 * rows, kv[0].shape[1]), jnp.bfloat16),
            pltpu.VMEM((4 * rows, kv[0].shape[1]), jnp.bfloat16),
            pltpu.VMEM((2 * len(groups), piece, queries.shape[1]), jnp.bfloat16),
            pltpu.VMEM((2 * len(groups), piece, queries.shape[1]), jnp.bfloat16),
            pltpu.SemaphoreType.DMA((8,)),
            pltpu.SemaphoreType.DMA((2 * len(groups),)),
        ],
        compiler_params=pltpu.CompilerParams(vmem_limit_bytes=32 * 2**20),
        cost_estimate=pl.CostEstimate(flops=4 * 10**8, bytes_accessed=3 * 2**20, transcendentals=10**6),
        name="attend_groups",
    )(meta, owners, lengths, queries, other, *kv)


def _project_kernel(parts, block, meta_ref, a_ref, b_ref, w_ref, out_ref, wbuf, catbuf, ctxbuf, sems):
    h = meta_ref[1]
    second = lax.rem(lax.div(meta_ref[0], 2), 2)
    half = w_ref.shape[0] // (2 * N_FAST_HEAD)
    per = half // block
    copies = []
    for i, (flip, side) in enumerate(parts):
        for j in range(per):
            row = pl.multiple_of((h ^ flip) * (2 * half) + side * half + j * block, block)
            n = i * per + j
            copies.append(pltpu.make_async_copy(w_ref.at[pl.ds(row, block)], wbuf.at[n], sems.at[n]))
    for copy in copies:
        copy.start()
    mid = a_ref.shape[0]
    catbuf[pl.ds(pl.multiple_of(second * mid, mid), mid)] = a_ref[...]
    catbuf[pl.ds(pl.multiple_of((1 - second) * mid, mid), mid)] = b_ref[...]
    ctxbuf[...] = catbuf[...].T
    for n, copy in enumerate(copies):
        copy.wait()
        out_ref[pl.ds(n * block, block)] = jnp.dot(
            wbuf[n], ctxbuf[...], preferred_element_type=jnp.float32).astype(out_ref.dtype)


def _project_rows(parts, meta, a, b, out_weight, dtype=jnp.bfloat16):
    block = 256
    half = out_weight.shape[0] // (2 * N_FAST_HEAD)
    rows, tokens = half * len(parts), a.shape[0] + b.shape[0]
    steps = rows // block
    vmem = pl.BlockSpec(memory_space=pltpu.VMEM)
    return pl.pallas_call(
        functools.partial(_project_kernel, parts, block),
        out_shape=jax.ShapeDtypeStruct((rows, tokens), dtype),
        in_specs=[pl.BlockSpec(memory_space=pltpu.SMEM), vmem, vmem, pl.BlockSpec(memory_space=pl.ANY)],
        out_specs=vmem,
        scratch_shapes=[
            pltpu.VMEM((steps, block, out_weight.shape[1]), jnp.bfloat16),
            pltpu.VMEM((tokens, out_weight.shape[1]), jnp.bfloat16),
            pltpu.VMEM((out_weight.shape[1], tokens), jnp.bfloat16),
            pltpu.SemaphoreType.DMA((steps,)),
        ],
        compiler_params=pltpu.CompilerParams(vmem_limit_bytes=40 * 2**20),
        cost_estimate=pl.CostEstimate(
            flops=2 * rows * tokens * out_weight.shape[1],
            bytes_accessed=2 * rows * (out_weight.shape[1] + tokens), transcendentals=0),
        name="project_rows",
    )(meta, a, b, out_weight)


def _add_halves_kernel(a_ref, b_ref, out_ref):
    out_ref[...] = (a_ref[...].astype(jnp.float32) + b_ref[...].astype(jnp.float32)).astype(out_ref.dtype)


def _add_halves(a, a_half, b, b_half):
    rows, tokens = a.shape[0] // 2, a.shape[1]
    return pl.pallas_call(
        _add_halves_kernel,
        out_shape=jax.ShapeDtypeStruct((rows, tokens), jnp.bfloat16),
        grid=(1,),
        in_specs=[
            pl.BlockSpec((rows, tokens), lambda i: (a_half, 0)),
            pl.BlockSpec((rows, tokens), lambda i: (b_half, 0)),
        ],
        out_specs=pl.BlockSpec((rows, tokens), lambda i: (0, 0)),
        cost_estimate=pl.CostEstimate(flops=rows * tokens, bytes_accessed=6 * rows * tokens, transcendentals=0),
        name="add_halves",
    )(a, b)


def _finish_kernel(far, meta_ref, keep_ref, x1_ref, y1_ref, y2_ref, x2_ref, *rest):
    out_ref = rest[-1]
    half = x1_ref.shape[0]
    f32 = jnp.float32
    out_ref[:half] = (
        keep_ref[:half].astype(f32) + x1_ref[...].astype(f32) + y2_ref[...].astype(f32)
    ).astype(out_ref.dtype)
    out_ref[half:] = (
        keep_ref[half:].astype(f32) + y1_ref[...].astype(f32) + x2_ref[...].astype(f32)
    ).astype(out_ref.dtype)


def _finish(far, meta, keep, x1, y1, y2, x2, out=None):
    rows, tokens = keep.shape
    half = rows // 2

    def place(i, meta_ref):
        upper = lax.div(meta_ref[0], 4)
        return (0, 1 - upper if far else upper)

    zero = lambda i, meta_ref: (0, 0)
    specs = [pl.BlockSpec((rows, tokens), zero)] + [pl.BlockSpec((half, tokens), zero)] * 4
    operands = [keep, x1, y1, y2, x2]
    if out is not None:
        specs.append(pl.BlockSpec(memory_space=pl.ANY))
        operands.append(out)
    return pl.pallas_call(
        functools.partial(_finish_kernel, far),
        out_shape=jax.ShapeDtypeStruct((rows, 2 * tokens), jnp.bfloat16),
        grid_spec=pltpu.PrefetchScalarGridSpec(
            num_scalar_prefetch=1, grid=(1,), in_specs=specs,
            out_specs=pl.BlockSpec((rows, tokens), place),
        ),
        input_output_aliases={6: 0} if out is not None else {},
        cost_estimate=pl.CostEstimate(flops=2 * rows * tokens, bytes_accessed=10 * rows * tokens, transcendentals=0),
        name="finish",
    )(meta, *operands)


def _flip(x, axis, bits):
    n = lax.axis_size(axis)
    return lax.ppermute(x, axis, [(i, i ^ bits) for i in range(n)])


def _reduce_chunk(meta, a, b, out_weight, far, out):
    xmsg = _project_rows([(1, 0), (3, 0)], meta, a, b, out_weight)
    x1 = _flip(xmsg, "head", 1)
    ymsg = _project_rows([(2, 1), (3, 1)], meta, a, b, out_weight)
    y1 = _flip(ymsg, "head", 2)
    pass_on = _project_rows([(2, 0), (1, 1)], meta, a, b, out_weight)
    keep = _project_rows([(0, 0), (0, 1)], meta, a, b, out_weight)
    y2 = _flip(_add_halves(pass_on, 0, x1, 1), "head", 2)
    x2 = _flip(_add_halves(pass_on, 1, y1, 1), "head", 1)
    return _finish(far, meta, keep, x1, y1, y2, x2, out)


def per_device_fast(queries, keys, values, out_weight, doc_lengths, owners):
    places = lax.axis_size("ctx")
    meta = jnp.stack([lax.axis_index("ctx"), lax.axis_index("head")]).astype(jnp.int32)
    before = [(i, i + 2) for i in range(places - 2)]
    k2 = lax.ppermute(keys, "ctx", before)
    v2 = lax.ppermute(values, "ctx", before)
    k1, v1 = _flip(keys, "ctx", 1), _flip(values, "ctx", 1)
    smem = pl.BlockSpec(memory_space=pltpu.SMEM)
    hbm = pl.BlockSpec(memory_space=pl.ANY)
    leaving = pl.pallas_call(
        _queries_for_other_core,
        out_shape=jax.ShapeDtypeStruct((queries.shape[0] // 2, queries.shape[1]), jnp.bfloat16),
        in_specs=[smem, smem, hbm],
        out_specs=hbm,
        scratch_shapes=[pltpu.SemaphoreType.DMA((PIECES // 2,))],
        name="queries_for_other_core",
    )(meta, owners, queries)
    other = _flip(leaving, "ctx", 1)
    k3, v3 = _flip(k2, "ctx", 1), _flip(v2, "ctx", 1)
    kv = (keys, k1, k2, k3, values, v1, v2, v3)
    near1, far3 = _attend_groups((1, 3), meta, owners, doc_lengths, queries, other, kv)
    near1, far3 = _flip(near1, "ctx", 2), _flip(far3, "ctx", 6)
    far2, near0 = _attend_groups((2, 0), meta, owners, doc_lengths, queries, other, kv)
    far2 = _flip(far2, "ctx", 4)
    out = _reduce_chunk(meta, near0, near1, out_weight, False, None)
    return _reduce_chunk(meta, far2, far3, out_weight, True, out)


def solution(mesh):
    in_specs = (P("ctx", "head"), P("ctx", "head"), P("ctx", "head"), P(None, "head"), P(), P())
    out_specs = P("head", "ctx")
    fast = mesh.shape["ctx"] == PIECES and mesh.shape["head"] == N_FAST_HEAD
    return jax.shard_map(
        per_device_fast if fast else per_device, mesh=mesh, in_specs=in_specs, out_specs=out_specs, check_vma=False
    )
```

```python
import functools
import math

import jax
import jax.numpy as jnp
from jax import lax
from jax.experimental import pallas as pl
from jax.experimental.pallas import tpu as pltpu
from jax.sharding import PartitionSpec as P

HEAD_SIZE = 128
PIECES = 8
N_FAST_HEAD = 4


MASKED = -1e30


def document_index(positions, doc_starts):
    return jnp.sum((positions[:, None] >= doc_starts[None, :]).astype(jnp.int32), axis=1) - 1


def attend(query_rows, query_pos, keys, values, doc_starts):
    row_count = query_rows.shape[0]
    key_heads = keys.shape[1] // HEAD_SIZE
    group_length = query_rows.shape[1] // keys.shape[1]
    query_heads = query_rows.reshape(row_count, key_heads, group_length, HEAD_SIZE)
    query_doc = document_index(query_pos, doc_starts)
    score_scale = 1.0 / math.sqrt(HEAD_SIZE)
    initial = (
        jnp.full((row_count, key_heads, group_length), MASKED, jnp.float32),
        jnp.zeros((row_count, key_heads, group_length), jnp.float32),
        jnp.zeros((row_count, key_heads, group_length, HEAD_SIZE), jnp.float32),
    )
    key_piece = lax.all_gather(keys, "ctx", axis=0, tiled=True)
    value_piece = lax.all_gather(values, "ctx", axis=0, tiled=True)
    piece_rows = key_piece.shape[0]
    tile_rows = math.gcd(piece_rows, 512)

    def one_tile(tile_index, running):
        tile_start = tile_index * tile_rows
        key_block = lax.dynamic_slice_in_dim(key_piece, tile_start, tile_rows, 0).reshape(
            tile_rows, key_heads, HEAD_SIZE
        )
        value_block = lax.dynamic_slice_in_dim(value_piece, tile_start, tile_rows, 0).reshape(
            tile_rows, key_heads, HEAD_SIZE
        )
        key_pos = tile_start + jnp.arange(tile_rows, dtype=jnp.int32)
        key_doc = document_index(key_pos, doc_starts)
        allowed = (query_doc[:, None] == key_doc[None, :]) & (
            key_pos[None, :] <= query_pos[:, None]
        )
        running_max, running_sum, weighted = running
        scores = (
            jnp.einsum("rkgd,nkd->rkgn", query_heads, key_block, preferred_element_type=jnp.float32)
            * score_scale
        )
        allowed_all = allowed[:, None, None, :]
        scores = jnp.where(allowed_all, scores, MASKED)
        new_max = jnp.maximum(running_max, jnp.max(scores, axis=-1))
        factor = jnp.exp(running_max - new_max)
        weights = jnp.where(allowed_all, jnp.exp(scores - new_max[..., None]), 0.0)
        new_sum = running_sum * factor + jnp.sum(weights, axis=-1)
        new_weighted = weighted * factor[..., None] + jnp.einsum(
            "rkgn,nkd->rkgd",
            weights.astype(jnp.bfloat16),
            value_block,
            preferred_element_type=jnp.float32,
        )
        return (new_max, new_sum, new_weighted)

    final_max, final_sum, weighted = lax.fori_loop(0, piece_rows // tile_rows, one_tile, initial)
    result = weighted / jnp.maximum(final_sum, 1.0)[..., None]
    return result.reshape(row_count, key_heads * group_length * HEAD_SIZE).astype(jnp.bfloat16)


def project(context, out_weight):
    return lax.psum_scatter(
        lax.dot_general(
            out_weight, context, (((1,), (1,)), ((), ())), preferred_element_type=jnp.float32
        ).astype(jnp.bfloat16),
        "head",
        scatter_dimension=0,
        tiled=True,
    )


def per_device(queries, keys, values, out_weight, doc_lengths, owners):
    place_count = lax.axis_size("ctx")
    own_index = lax.axis_index("ctx")
    token_count = queries.shape[0]
    block_rows = token_count // PIECES
    doc_ends = jnp.cumsum(doc_lengths)
    doc_starts = doc_ends - doc_lengths
    owner_table = owners[:, 0].reshape(place_count, PIECES)
    own_owners = lax.dynamic_index_in_dim(owner_table, own_index, 0, keepdims=False)
    place_ids = jnp.arange(place_count, dtype=jnp.int32)
    send_pick = (own_owners[None, :] == place_ids[:, None]).astype(jnp.bfloat16)
    grouped = queries.reshape(PIECES, block_rows, queries.shape[1])
    outgoing = jnp.einsum(
        "oc,chw->ohw", send_pick, grouped, preferred_element_type=jnp.float32
    ).astype(jnp.bfloat16)
    arrived = lax.all_to_all(outgoing, "ctx", split_axis=0, concat_axis=0, tiled=True)
    slot_hits = (owner_table == own_index).astype(jnp.int32)
    slot_live = jnp.sum(slot_hits, axis=1)
    picked = jnp.sum(slot_hits * jnp.arange(PIECES, dtype=jnp.int32)[None, :], axis=1)
    slot_pos = (place_ids[:, None] * PIECES + picked[:, None]) * block_rows + jnp.arange(
        block_rows, dtype=jnp.int32
    )[None, :]
    query_pos = jnp.where(slot_live[:, None] > 0, slot_pos, -1).reshape(-1)
    context = attend(
        arrived.reshape(place_count * block_rows, queries.shape[1]),
        query_pos,
        keys,
        values,
        doc_starts,
    )
    return project(context, out_weight)


SMEM = pl.BlockSpec(memory_space=pltpu.SMEM)
VMEM = pl.BlockSpec(memory_space=pltpu.VMEM)
HBM = pl.BlockSpec(memory_space=pltpu.HBM)
ANY = pl.BlockSpec(memory_space=pl.ANY)


OWNERS_AT = 2


def _find_piece(table_ref, source, owner):
    piece = jnp.int32(0)
    for i in range(PIECES):
        piece = jnp.where(table_ref[OWNERS_AT + source * PIECES + i] == owner, jnp.int32(i), piece)
    return piece


def _rows(start, size):
    return pl.ds(pl.multiple_of(start, size), size)


def _queries_for_other_core(meta_ref, queries_ref, out_ref):
    c = meta_ref[0]
    core = lax.rem(c, 2)
    rows = queries_ref.shape[0] // PIECES
    for j in range(PIECES // 2):
        piece = _find_piece(meta_ref, c, 2 * j + 1 - core)
        out_ref[j * rows:(j + 1) * rows] = queries_ref[_rows(piece * rows, rows)]


QUARTERS = {
    "x": ((1, 0), (3, 0)),
    "y": ((2, 1), (3, 1)),
    "pass": ((2, 0), (1, 1)),
    "keep": ((0, 0), (0, 1)),
}


def _weight_copies(names, meta_ref, w_ref, out_refs, sems):
    half = w_ref.shape[0] // (2 * N_FAST_HEAD)
    copies = []
    for n, name in enumerate(names):
        for i, (flip, side) in enumerate(QUARTERS[name]):
            row = (meta_ref[1] ^ flip) * (2 * half) + side * half
            copies.append(pltpu.make_async_copy(
                w_ref.at[_rows(row, half)], out_refs[n].at[pl.ds(i * half, half)], sems.at[2 * n + i]))
    return copies


def _stage_kernel(names, meta_ref, w_ref, *rest):
    copies = _weight_copies(names, meta_ref, w_ref, rest[:-1], rest[-1])
    for copy in copies:
        copy.start()
    for copy in copies:
        copy.wait()


def _quarter(out_weight):
    return jax.ShapeDtypeStruct((out_weight.shape[0] // N_FAST_HEAD, out_weight.shape[1]), out_weight.dtype)


def _stage_weights(names, meta, out_weight):
    return pl.pallas_call(
        functools.partial(_stage_kernel, names),
        out_shape=[_quarter(out_weight) for _ in names],
        in_specs=[SMEM, HBM],
        out_specs=[VMEM] * len(names),
        scratch_shapes=[pltpu.SemaphoreType.DMA((2 * len(names),))],
        compiler_params=pltpu.CompilerParams(vmem_limit_bytes=36 * 2**20),
        cost_estimate=pl.CostEstimate(
            flops=0, bytes_accessed=len(names) * out_weight.size, transcendentals=0),
        name="stage_weights",
    )(meta, out_weight)


def _attend_kernel(
    groups, names, meta_ref, queries_ref, other_ref,
    k0_ref, k1_ref, k2_ref, k3_ref, v0_ref, v1_ref, v2_ref, v3_ref, w_ref, after_ref,
    *rest,
):
    count = len(groups)
    out_refs, w_out = rest[:count], rest[count:count + len(names)]
    kbuf, vbuf, qbuf, ctxbuf, w_sems = rest[count + len(names):]
    w_copies = _weight_copies(names, meta_ref, w_ref, w_out, w_sems)
    for copy in w_copies:
        copy.start()
    c = meta_ref[0]
    core = lax.rem(c, 2)
    z = lax.div(c, 2)
    rows = k0_ref.shape[0]
    piece_rows = rows // PIECES
    tile = 128
    slots = (2 + core, 3 - core, core, 1 - core)
    for b, (k_ref, v_ref) in enumerate(((k0_ref, v0_ref), (k1_ref, v1_ref), (k2_ref, v2_ref), (k3_ref, v3_ref))):
        kbuf[_rows(slots[b] * rows, rows)] = k_ref[...]
        vbuf[_rows(slots[b] * rows, rows)] = v_ref[...]
    starts = []
    for n, k in enumerate(groups):
        zdest = z ^ k
        owner = 2 * zdest + core
        mine = _find_piece(meta_ref, c, owner)
        theirs = _find_piece(meta_ref, c + 1 - 2 * core, owner)
        qbuf[2 * n + core] = queries_ref[_rows(mine * piece_rows, piece_rows)]
        qbuf[2 * n + 1 - core] = other_ref[_rows(zdest * piece_rows, piece_rows)]
        at0 = jnp.where(core == 0, mine, theirs)
        at1 = jnp.where(core == 0, theirs, mine)
        starts.append((at0 * piece_rows, rows + at1 * piece_rows))
    doc_start = []
    running = jnp.int32(0)
    lengths_at = OWNERS_AT + PIECES * PIECES
    for d in range(lengths_at, meta_ref.shape[0]):
        doc_start.append(running)
        running = running + meta_ref[d]
    base = 2 * rows * (z - 1)
    heads = k0_ref.shape[1] // HEAD_SIZE
    group = queries_ref.shape[1] // k0_ref.shape[1]
    scale = math.log2(math.e) / math.sqrt(HEAD_SIZE)
    span = 5 * tile

    def one_piece(n, p0):
        first = lax.div(p0, tile) * tile + 2 * rows - 4 * tile
        first = pl.multiple_of(first, tile)
        lane = lax.broadcasted_iota(jnp.int32, (1, tile), 1)
        pos = 2 * rows * z + p0 + lax.rem(lane, piece_rows)
        low = jnp.zeros((1, tile), jnp.int32)
        for start in doc_start:
            low = jnp.where(pos >= start, start, low)
        key_pos = base + first + lax.broadcasted_iota(jnp.int32, (span, tile), 0)
        allowed = (key_pos >= low) & (key_pos <= pos)
        allowed = jnp.concatenate([allowed] * (group * piece_rows // tile), axis=1)
        for kv in range(heads):
            cols = pl.ds(kv * HEAD_SIZE, HEAD_SIZE)
            q = jnp.concatenate(
                [qbuf[n, :, pl.ds((kv * group + g) * HEAD_SIZE, HEAD_SIZE)] for g in range(group)], axis=0)
            k = kbuf[pl.ds(first, span), cols]
            v = vbuf[pl.ds(first, span), cols]
            s = lax.dot_general(k, q, (((1,), (1,)), ((), ())), preferred_element_type=jnp.float32) * scale
            s = jnp.where(allowed, s, MASKED)
            top = jnp.max(s, axis=0, keepdims=True)
            w = jnp.exp2(s - top)
            total = jnp.sum(w, axis=0, keepdims=True)
            o = lax.dot_general(v, w.astype(jnp.bfloat16), (((0,), (0,)), ((), ())),
                                preferred_element_type=jnp.float32)
            o = (o / total).T.astype(jnp.bfloat16)
            for g in range(group):
                ctxbuf[n, :, pl.ds((kv * group + g) * HEAD_SIZE, HEAD_SIZE)] = o[g * piece_rows:(g + 1) * piece_rows]

    def step(n, carry):
        p0 = starts[0][0]
        for m in range(1, 2 * count):
            p0 = jnp.where(n == m, starts[m // 2][m % 2], p0)
        one_piece(n, p0)
        return carry

    lax.fori_loop(0, 2 * count, step, 0)
    for n, out_ref in enumerate(out_refs):
        out_ref[...] = ctxbuf[2 * n:2 * n + 2].reshape(out_ref.shape)
    for copy in w_copies:
        copy.wait()


def _attend_groups(groups, names, meta, queries, other, kv, out_weight, after):
    piece = queries.shape[0] // PIECES
    rows = kv[0].shape[0]
    return pl.pallas_call(
        functools.partial(_attend_kernel, groups, names),
        out_shape=[jax.ShapeDtypeStruct((2 * piece, queries.shape[1]), jnp.bfloat16) for _ in groups]
        + [_quarter(out_weight) for _ in names],
        in_specs=[SMEM] + [VMEM] * 10 + [HBM, ANY],
        out_specs=[VMEM] * (len(groups) + len(names)),
        scratch_shapes=[
            pltpu.VMEM((4 * rows, kv[0].shape[1]), jnp.bfloat16),
            pltpu.VMEM((4 * rows, kv[0].shape[1]), jnp.bfloat16),
            pltpu.VMEM((2 * len(groups), piece, queries.shape[1]), jnp.bfloat16),
            pltpu.VMEM((2 * len(groups), piece, queries.shape[1]), jnp.bfloat16),
            pltpu.SemaphoreType.DMA((2 * len(names),)),
        ],
        compiler_params=pltpu.CompilerParams(vmem_limit_bytes=12 * 2**20),
        cost_estimate=pl.CostEstimate(flops=10**9, bytes_accessed=10 * 2**20, transcendentals=10**6),
        name="attend_groups",
    )(meta, queries, other, *kv, out_weight, after)


def _join_kernel(meta_ref, a_ref, b_ref, w_ref, out_ref, joined_ref, catbuf):
    second = lax.rem(lax.div(meta_ref[0], 2), 2)
    mid = a_ref.shape[0]
    catbuf[_rows(second * mid, mid)] = a_ref[...]
    catbuf[_rows((1 - second) * mid, mid)] = b_ref[...]
    joined = catbuf[...].T
    joined_ref[...] = joined
    out_ref[...] = jnp.dot(w_ref[...], joined, preferred_element_type=jnp.float32).astype(out_ref.dtype)


def _project_kernel(joined_ref, w_ref, out_ref):
    out_ref[...] = jnp.dot(w_ref[...], joined_ref[...], preferred_element_type=jnp.float32).astype(out_ref.dtype)


def _cost(rows, depth, tokens):
    return pl.CostEstimate(
        flops=2 * rows * depth * tokens, bytes_accessed=2 * (rows * depth + tokens * (rows + depth)), transcendentals=0)


def _join_and_project(meta, a, b, weight):
    (rows, depth), tokens = weight.shape, a.shape[0] + b.shape[0]
    return pl.pallas_call(
        _join_kernel,
        out_shape=[jax.ShapeDtypeStruct((rows, tokens), jnp.bfloat16), jax.ShapeDtypeStruct((depth, tokens), jnp.bfloat16)],
        in_specs=[SMEM] + [VMEM] * 3,
        out_specs=[VMEM] * 2,
        scratch_shapes=[pltpu.VMEM((tokens, depth), jnp.bfloat16)],
        compiler_params=pltpu.CompilerParams(vmem_limit_bytes=8 * 2**20),
        cost_estimate=_cost(rows, depth, tokens),
        name="join_and_project",
    )(meta, a, b, weight)


def _project_rows(joined, weight):
    (rows, depth), tokens = weight.shape, joined.shape[1]
    return pl.pallas_call(
        _project_kernel,
        out_shape=jax.ShapeDtypeStruct((rows, tokens), jnp.bfloat16),
        in_specs=[VMEM] * 2,
        out_specs=VMEM,
        compiler_params=pltpu.CompilerParams(vmem_limit_bytes=8 * 2**20),
        cost_estimate=_cost(rows, depth, tokens),
        name="project_rows",
    )(joined, weight)


def _add_halves_kernel(a_half, b_half, a_ref, b_ref, out_ref):
    rows = out_ref.shape[0]
    a = a_ref[a_half * rows:(a_half + 1) * rows].astype(jnp.float32)
    b = b_ref[b_half * rows:(b_half + 1) * rows].astype(jnp.float32)
    out_ref[...] = (a + b).astype(out_ref.dtype)


def _add_halves(a, a_half, b, b_half):
    rows, tokens = a.shape[0] // 2, a.shape[1]
    return pl.pallas_call(
        functools.partial(_add_halves_kernel, a_half, b_half),
        out_shape=jax.ShapeDtypeStruct((rows, tokens), jnp.bfloat16),
        in_specs=[VMEM] * 2,
        out_specs=VMEM,
        compiler_params=pltpu.CompilerParams(vmem_limit_bytes=2 * 2**20),
        cost_estimate=pl.CostEstimate(flops=rows * tokens, bytes_accessed=6 * rows * tokens, transcendentals=0),
        name="add_halves",
    )(a, b)


def _sum_parts(keep_ref, x1_ref, y1_ref, y2_ref, x2_ref):
    half = y2_ref.shape[0]
    f32 = jnp.float32
    first = keep_ref[:half].astype(f32) + x1_ref[:half].astype(f32) + y2_ref[...].astype(f32)
    second = keep_ref[half:].astype(f32) + y1_ref[:half].astype(f32) + x2_ref[...].astype(f32)
    return first.astype(jnp.bfloat16), second.astype(jnp.bfloat16)


def _finish_kernel(meta_ref, keep_ref, x1_ref, y1_ref, y2_ref, x2_ref, out_ref):
    half = y2_ref.shape[0]
    out_ref[:half], out_ref[half:] = _sum_parts(keep_ref, x1_ref, y1_ref, y2_ref, x2_ref)


def _finish_both_kernel(meta_ref, near_ref, keep_ref, x1_ref, y1_ref, y2_ref, x2_ref, out_ref):
    half, tokens = y2_ref.shape
    upper = lax.div(meta_ref[0], 4)
    first, second = _sum_parts(keep_ref, x1_ref, y1_ref, y2_ref, x2_ref)
    at = _rows((1 - upper) * tokens, tokens)
    out_ref[:half, at] = first
    out_ref[half:, at] = second
    out_ref[:, _rows(upper * tokens, tokens)] = near_ref[...]


def _finish(meta, keep, x1, y1, y2, x2, near=None):
    rows, tokens = keep.shape
    operands = [meta] + ([] if near is None else [near]) + [keep, x1, y1, y2, x2]
    return pl.pallas_call(
        _finish_kernel if near is None else _finish_both_kernel,
        out_shape=jax.ShapeDtypeStruct((rows, tokens if near is None else 2 * tokens), jnp.bfloat16),
        in_specs=[SMEM] + [VMEM] * (len(operands) - 1),
        out_specs=VMEM,
        compiler_params=pltpu.CompilerParams(vmem_limit_bytes=4 * 2**20),
        cost_estimate=pl.CostEstimate(flops=2 * rows * tokens, bytes_accessed=10 * rows * tokens, transcendentals=0),
        name="finish",
    )(*operands)


def _flip(x, axis, bits):
    n = lax.axis_size(axis)
    return lax.ppermute(x, axis, [(i, i ^ bits) for i in range(n)])


def _reduce_chunk(meta, a, b, weights, near):
    xmsg, joined = _join_and_project(meta, a, b, weights["x"])
    x1 = _flip(xmsg, "head", 1)
    y1 = _flip(_project_rows(joined, weights["y"]), "head", 2)
    pass_on = _project_rows(joined, weights["pass"])
    keep = _project_rows(joined, weights["keep"])
    y2 = _flip(_add_halves(pass_on, 0, x1, 1), "head", 2)
    x2 = _flip(_add_halves(pass_on, 1, y1, 1), "head", 1)
    return _finish(meta, keep, x1, y1, y2, x2, near)


def per_device_fast(queries, keys, values, out_weight, doc_lengths, owners):
    places = lax.axis_size("ctx")
    before = [(i, i + 2) for i in range(places - 2)]
    k2 = lax.ppermute(keys, "ctx", before)
    v2 = lax.ppermute(values, "ctx", before)
    meta = jnp.concatenate([
        lax.axis_index("ctx").reshape(1), lax.axis_index("head").reshape(1), owners.reshape(-1), doc_lengths,
    ]).astype(jnp.int32)
    k1, v1 = _flip(keys, "ctx", 1), _flip(values, "ctx", 1)
    leaving = pl.pallas_call(
        _queries_for_other_core,
        out_shape=jax.ShapeDtypeStruct((queries.shape[0] // 2, queries.shape[1]), jnp.bfloat16),
        in_specs=[SMEM, VMEM],
        out_specs=VMEM,
        compiler_params=pltpu.CompilerParams(vmem_limit_bytes=2 * 2**20),
        name="queries_for_other_core",
    )(meta, queries)
    other = _flip(leaving, "ctx", 1)
    weights = dict(zip(("x", "y"), _stage_weights(("x", "y"), meta, out_weight)))
    k3, v3 = _flip(k2, "ctx", 1), _flip(v2, "ctx", 1)
    kv = (keys, k1, k2, k3, values, v1, v2, v3)
    near1, far3, weights["pass"] = _attend_groups(
        (1, 3), ("pass",), meta, queries, other, kv, out_weight, weights["x"])
    near1, far3 = _flip(near1, "ctx", 2), _flip(far3, "ctx", 6)
    far2, near0, weights["keep"] = _attend_groups(
        (2, 0), ("keep",), meta, queries, other, kv, out_weight, weights["pass"])
    far2 = _flip(far2, "ctx", 4)
    near = _reduce_chunk(meta, near0, near1, weights, None)
    return _reduce_chunk(meta, far2, far3, weights, near)


def solution(mesh):
    in_specs = (P("ctx", "head"), P("ctx", "head"), P("ctx", "head"), P(None, "head"), P(), P())
    out_specs = P("head", "ctx")
    fast = mesh.shape["ctx"] == PIECES and mesh.shape["head"] == N_FAST_HEAD
    return jax.shard_map(
        per_device_fast if fast else per_device, mesh=mesh, in_specs=in_specs, out_specs=out_specs, check_vma=False
    )
```

```python
import functools
import math

import jax
import jax.numpy as jnp
from jax import lax
from jax.experimental import pallas as pl
from jax.experimental.pallas import tpu as pltpu
from jax.sharding import PartitionSpec as P

HEAD_SIZE = 128
PIECES = 8
N_FAST_HEAD = 4


MASKED = -1e30


def document_index(positions, doc_starts):
    return jnp.sum((positions[:, None] >= doc_starts[None, :]).astype(jnp.int32), axis=1) - 1


def attend(query_rows, query_pos, keys, values, doc_starts):
    row_count = query_rows.shape[0]
    key_heads = keys.shape[1] // HEAD_SIZE
    group_length = query_rows.shape[1] // keys.shape[1]
    query_heads = query_rows.reshape(row_count, key_heads, group_length, HEAD_SIZE)
    query_doc = document_index(query_pos, doc_starts)
    score_scale = 1.0 / math.sqrt(HEAD_SIZE)
    initial = (
        jnp.full((row_count, key_heads, group_length), MASKED, jnp.float32),
        jnp.zeros((row_count, key_heads, group_length), jnp.float32),
        jnp.zeros((row_count, key_heads, group_length, HEAD_SIZE), jnp.float32),
    )
    key_piece = lax.all_gather(keys, "ctx", axis=0, tiled=True)
    value_piece = lax.all_gather(values, "ctx", axis=0, tiled=True)
    piece_rows = key_piece.shape[0]
    tile_rows = math.gcd(piece_rows, 512)

    def one_tile(tile_index, running):
        tile_start = tile_index * tile_rows
        key_block = lax.dynamic_slice_in_dim(key_piece, tile_start, tile_rows, 0).reshape(
            tile_rows, key_heads, HEAD_SIZE
        )
        value_block = lax.dynamic_slice_in_dim(value_piece, tile_start, tile_rows, 0).reshape(
            tile_rows, key_heads, HEAD_SIZE
        )
        key_pos = tile_start + jnp.arange(tile_rows, dtype=jnp.int32)
        key_doc = document_index(key_pos, doc_starts)
        allowed = (query_doc[:, None] == key_doc[None, :]) & (
            key_pos[None, :] <= query_pos[:, None]
        )
        running_max, running_sum, weighted = running
        scores = (
            jnp.einsum("rkgd,nkd->rkgn", query_heads, key_block, preferred_element_type=jnp.float32)
            * score_scale
        )
        allowed_all = allowed[:, None, None, :]
        scores = jnp.where(allowed_all, scores, MASKED)
        new_max = jnp.maximum(running_max, jnp.max(scores, axis=-1))
        factor = jnp.exp(running_max - new_max)
        weights = jnp.where(allowed_all, jnp.exp(scores - new_max[..., None]), 0.0)
        new_sum = running_sum * factor + jnp.sum(weights, axis=-1)
        new_weighted = weighted * factor[..., None] + jnp.einsum(
            "rkgn,nkd->rkgd",
            weights.astype(jnp.bfloat16),
            value_block,
            preferred_element_type=jnp.float32,
        )
        return (new_max, new_sum, new_weighted)

    final_max, final_sum, weighted = lax.fori_loop(0, piece_rows // tile_rows, one_tile, initial)
    result = weighted / jnp.maximum(final_sum, 1.0)[..., None]
    return result.reshape(row_count, key_heads * group_length * HEAD_SIZE).astype(jnp.bfloat16)


def project(context, out_weight):
    return lax.psum_scatter(
        lax.dot_general(
            out_weight, context, (((1,), (1,)), ((), ())), preferred_element_type=jnp.float32
        ).astype(jnp.bfloat16),
        "head",
        scatter_dimension=0,
        tiled=True,
    )


def per_device(queries, keys, values, out_weight, doc_lengths, owners):
    place_count = lax.axis_size("ctx")
    own_index = lax.axis_index("ctx")
    token_count = queries.shape[0]
    block_rows = token_count // PIECES
    doc_ends = jnp.cumsum(doc_lengths)
    doc_starts = doc_ends - doc_lengths
    owner_table = owners[:, 0].reshape(place_count, PIECES)
    own_owners = lax.dynamic_index_in_dim(owner_table, own_index, 0, keepdims=False)
    place_ids = jnp.arange(place_count, dtype=jnp.int32)
    send_pick = (own_owners[None, :] == place_ids[:, None]).astype(jnp.bfloat16)
    grouped = queries.reshape(PIECES, block_rows, queries.shape[1])
    outgoing = jnp.einsum(
        "oc,chw->ohw", send_pick, grouped, preferred_element_type=jnp.float32
    ).astype(jnp.bfloat16)
    arrived = lax.all_to_all(outgoing, "ctx", split_axis=0, concat_axis=0, tiled=True)
    slot_hits = (owner_table == own_index).astype(jnp.int32)
    slot_live = jnp.sum(slot_hits, axis=1)
    picked = jnp.sum(slot_hits * jnp.arange(PIECES, dtype=jnp.int32)[None, :], axis=1)
    slot_pos = (place_ids[:, None] * PIECES + picked[:, None]) * block_rows + jnp.arange(
        block_rows, dtype=jnp.int32
    )[None, :]
    query_pos = jnp.where(slot_live[:, None] > 0, slot_pos, -1).reshape(-1)
    context = attend(
        arrived.reshape(place_count * block_rows, queries.shape[1]),
        query_pos,
        keys,
        values,
        doc_starts,
    )
    return project(context, out_weight)


SMEM = pl.BlockSpec(memory_space=pltpu.SMEM)
VMEM = pl.BlockSpec(memory_space=pltpu.VMEM)
HBM = pl.BlockSpec(memory_space=pltpu.HBM)


OWNERS_AT = 2


def _find_piece(table_ref, source, owner):
    piece = jnp.int32(0)
    for i in range(PIECES):
        piece = jnp.where(table_ref[OWNERS_AT + source * PIECES + i] == owner, jnp.int32(i), piece)
    return piece


def _rows(start, size):
    return pl.ds(pl.multiple_of(start, size), size)


def _join_keys_values_kernel(keys_ref, values_ref, out_ref):
    rows = keys_ref.shape[0]
    out_ref[:rows] = keys_ref[...]
    out_ref[rows:] = values_ref[...]


def _join_keys_values(keys, values):
    return pl.pallas_call(
        _join_keys_values_kernel,
        out_shape=jax.ShapeDtypeStruct((2 * keys.shape[0], keys.shape[1]), keys.dtype),
        in_specs=[VMEM] * 2,
        out_specs=VMEM,
        compiler_params=pltpu.CompilerParams(vmem_limit_bytes=2 * 2**20),
        cost_estimate=pl.CostEstimate(flops=1, bytes_accessed=1, transcendentals=0),
        name="join_keys_values",
    )(keys, values)


def _queries_for_other_core_kernel(meta_ref, queries_ref, out_ref, kept_ref):
    c = meta_ref[0]
    core = lax.rem(c, 2)
    rows = queries_ref.shape[0] // PIECES
    for j in range(PIECES // 2):
        piece = _find_piece(meta_ref, c, 2 * j + 1 - core)
        out_ref[j * rows:(j + 1) * rows] = queries_ref[_rows(piece * rows, rows)]
    kept_ref[...] = queries_ref[...]


def _queries_for_other_core(meta, queries):
    return pl.pallas_call(
        _queries_for_other_core_kernel,
        out_shape=[
            jax.ShapeDtypeStruct((queries.shape[0] // 2, queries.shape[1]), queries.dtype),
            jax.ShapeDtypeStruct(queries.shape, queries.dtype),
        ],
        in_specs=[SMEM, VMEM],
        out_specs=[VMEM] * 2,
        compiler_params=pltpu.CompilerParams(vmem_limit_bytes=2 * 2**20),
        cost_estimate=pl.CostEstimate(flops=1, bytes_accessed=1, transcendentals=0),
        name="queries_for_other_core",
    )(meta, queries)


QUARTERS = {
    "x": ((1, 0), (3, 0)),
    "y": ((2, 1), (3, 1)),
    "pass": ((2, 0), (1, 1)),
    "keep": ((0, 0), (0, 1)),
}


def _weight_copies(names, meta_ref, w_ref, out_refs, sems):
    half = w_ref.shape[0] // (2 * N_FAST_HEAD)
    copies = []
    for n, name in enumerate(names):
        for i, (flip, side) in enumerate(QUARTERS[name]):
            row = (meta_ref[1] ^ flip) * (2 * half) + side * half
            copies.append(pltpu.make_async_copy(
                w_ref.at[_rows(row, half)], out_refs[n].at[pl.ds(i * half, half)], sems.at[2 * n + i]))
    return copies


def _quarter(out_weight):
    return jax.ShapeDtypeStruct((out_weight.shape[0] // N_FAST_HEAD, out_weight.shape[1]), out_weight.dtype)


def _stage_kernel(names, meta_ref, w_ref, *rest):
    copies = _weight_copies(names, meta_ref, w_ref, rest[:-1], rest[-1])
    for copy in copies:
        copy.start()
    for copy in copies:
        copy.wait()


def _stage_weights(names, meta, out_weight, room):
    return pl.pallas_call(
        functools.partial(_stage_kernel, names),
        out_shape=[_quarter(out_weight) for _ in names],
        in_specs=[SMEM, HBM],
        out_specs=[VMEM] * len(names),
        scratch_shapes=[pltpu.SemaphoreType.DMA((2 * len(names),))],
        compiler_params=pltpu.CompilerParams(vmem_limit_bytes=room * 2**20),
        cost_estimate=pl.CostEstimate(flops=1, bytes_accessed=1, transcendentals=0),
        name="stage_weights",
    )(meta, out_weight)


def _attend_kernel(
    groups, names, meta_ref, queries_ref, other_ref,
    kv0_ref, kv1_ref, kv2_ref, kv3_ref, w_ref,
    *rest,
):
    count = len(groups)
    out_refs, w_out = rest[:count], rest[count:count + len(names)]
    kbuf, vbuf, qbuf, ctxbuf, w_sems = rest[count + len(names):]
    w_copies = _weight_copies(names, meta_ref, w_ref, w_out, w_sems)
    for copy in w_copies:
        copy.start()
    c = meta_ref[0]
    core = lax.rem(c, 2)
    z = lax.div(c, 2)
    rows = kv0_ref.shape[0] // 2
    piece_rows = rows // PIECES
    tile = 128
    heads = kv0_ref.shape[1] // HEAD_SIZE
    slots = (2 + core, 3 - core, core, 1 - core)
    for b, kv_ref in enumerate((kv0_ref, kv1_ref, kv2_ref, kv3_ref)):
        at = _rows(slots[b] * rows, rows)
        kbuf[at] = kv_ref[:rows]
        for kv in range(heads):
            vbuf[at, 2 * kv * HEAD_SIZE:(2 * kv + 1) * HEAD_SIZE] = (
                kv_ref[rows:, kv * HEAD_SIZE:(kv + 1) * HEAD_SIZE])
            vbuf[at, (2 * kv + 1) * HEAD_SIZE:(2 * kv + 2) * HEAD_SIZE] = jnp.ones((rows, HEAD_SIZE), jnp.bfloat16)
    starts = []
    for n, k in enumerate(groups):
        zdest = z ^ k
        owner = 2 * zdest + core
        mine = _find_piece(meta_ref, c, owner)
        theirs = _find_piece(meta_ref, c + 1 - 2 * core, owner)
        qbuf[2 * n + core] = queries_ref[_rows(mine * piece_rows, piece_rows)]
        qbuf[2 * n + 1 - core] = other_ref[_rows(zdest * piece_rows, piece_rows)]
        at0 = jnp.where(core == 0, mine, theirs)
        at1 = jnp.where(core == 0, theirs, mine)
        starts.append((at0 * piece_rows, rows + at1 * piece_rows))
    doc_start = []
    running = jnp.int32(0)
    lengths_at = OWNERS_AT + PIECES * PIECES
    for d in range(lengths_at, meta_ref.shape[0]):
        doc_start.append(running)
        running = running + meta_ref[d]
    base = 2 * rows * (z - 1)
    group = queries_ref.shape[1] // kv0_ref.shape[1]
    scale = math.log2(math.e) / math.sqrt(HEAD_SIZE)
    span = 5 * tile

    def piece_keys(p0):
        first = pl.multiple_of(lax.div(p0, tile) * tile + 2 * rows - 4 * tile, tile)
        pos = 2 * rows * z + p0 + lax.broadcasted_iota(jnp.int32, (piece_rows, 1), 0)
        low = jnp.zeros((piece_rows, 1), jnp.int32)
        for start in doc_start:
            low = jnp.where(pos >= start, start, low)
        key_pos = base + first + lax.broadcasted_iota(jnp.int32, (piece_rows, span), 1)
        return first, (key_pos >= low) & (key_pos <= pos)

    def some_pieces(pieces):
        units, scores, weights = [], [], []
        for n, p0 in pieces:
            first, allowed = piece_keys(p0)
            units += [(n, kv, first, allowed) for kv in range(heads)]
        for n, kv, first, allowed in units:
            q = jnp.concatenate(
                [qbuf[n, :, pl.ds((kv * group + g) * HEAD_SIZE, HEAD_SIZE)] for g in range(group)], axis=0)
            k = kbuf[pl.ds(first, span), pl.ds(kv * HEAD_SIZE, HEAD_SIZE)]
            scores.append(lax.dot_general(q, k, (((1,), (1,)), ((), ())), preferred_element_type=jnp.float32))
        for (n, kv, first, allowed), s in zip(units, scores):
            s = jnp.where(allowed[None], s.reshape(group, piece_rows, span), MASKED)
            w = jnp.exp2((s - jnp.max(s, axis=2, keepdims=True)) * scale)
            weights.append(w.astype(jnp.bfloat16).reshape(group * piece_rows, span))
        for (n, kv, first, allowed), w in zip(units, weights):
            o = jnp.dot(w, vbuf[pl.ds(first, span), pl.ds(kv * 2 * HEAD_SIZE, 2 * HEAD_SIZE)],
                        preferred_element_type=jnp.float32)
            o = (o[:, :HEAD_SIZE] / o[:, HEAD_SIZE:]).astype(jnp.bfloat16)
            for g in range(group):
                ctxbuf[n, :, pl.ds((kv * group + g) * HEAD_SIZE, HEAD_SIZE)] = o[g * piece_rows:(g + 1) * piece_rows]

    together = 2

    def step(i, carry):
        pieces = []
        for j in range(together):
            n = i * together + j
            p0 = starts[0][0]
            for m in range(1, 2 * count):
                p0 = jnp.where(n == m, starts[m // 2][m % 2], p0)
            pieces.append((n, p0))
        some_pieces(pieces)
        return carry

    lax.fori_loop(0, 2 * count // together, step, 0)
    for n, out_ref in enumerate(out_refs):
        out_ref[...] = ctxbuf[2 * n:2 * n + 2].reshape(out_ref.shape)
    for copy in w_copies:
        copy.wait()


def _attend_groups(groups, names, meta, queries, other, kv, out_weight):
    piece = queries.shape[0] // PIECES
    rows = kv[0].shape[0] // 2
    return pl.pallas_call(
        functools.partial(_attend_kernel, groups, names),
        out_shape=[jax.ShapeDtypeStruct((2 * piece, queries.shape[1]), jnp.bfloat16) for _ in groups]
        + [_quarter(out_weight) for _ in names],
        in_specs=[SMEM] + [VMEM] * 6 + [HBM],
        out_specs=[VMEM] * (len(groups) + len(names)),
        scratch_shapes=[
            pltpu.VMEM((4 * rows, kv[0].shape[1]), jnp.bfloat16),
            pltpu.VMEM((4 * rows, 2 * kv[0].shape[1]), jnp.bfloat16),
            pltpu.VMEM((2 * len(groups), piece, queries.shape[1]), jnp.bfloat16),
            pltpu.VMEM((2 * len(groups), piece, queries.shape[1]), jnp.bfloat16),
            pltpu.SemaphoreType.DMA((2 * len(names),)),
        ],
        compiler_params=pltpu.CompilerParams(vmem_limit_bytes=12 * 2**20),
        cost_estimate=pl.CostEstimate(flops=1, bytes_accessed=1, transcendentals=0),
        name="attend_groups",
    )(meta, queries, other, *kv, out_weight)


def _dot_to(out_ref, weight_ref, tokens):
    out_ref[...] = jnp.dot(weight_ref[...], tokens, preferred_element_type=jnp.float32).astype(out_ref.dtype)


def _leaving_rows_kernel(meta_ref, a_ref, b_ref, wx_ref, wy_ref, x_ref, y_ref, joined_ref, catbuf):
    second = lax.rem(lax.div(meta_ref[0], 2), 2)
    mid = a_ref.shape[0]
    catbuf[_rows(second * mid, mid)] = a_ref[...]
    catbuf[_rows((1 - second) * mid, mid)] = b_ref[...]
    joined = catbuf[...].T
    joined_ref[...] = joined
    _dot_to(x_ref, wx_ref, joined)
    _dot_to(y_ref, wy_ref, joined)


def _pass_rows_kernel(joined_ref, w_ref, out_ref):
    _dot_to(out_ref, w_ref, joined_ref[...])


def _keep_rows_kernel(near_ref, far_ref, w_ref, near_out, far_out):
    tokens = near_ref.shape[1]
    both = jnp.concatenate([near_ref[...], far_ref[...]], axis=1)
    out = jnp.dot(w_ref[...], both, preferred_element_type=jnp.float32).astype(near_out.dtype)
    near_out[...] = out[:, :tokens]
    far_out[...] = out[:, tokens:]


def _leaving_rows(meta, a, b, w_x, w_y):
    (rows, depth), tokens = w_x.shape, a.shape[0] + b.shape[0]
    part = jax.ShapeDtypeStruct((rows, tokens), jnp.bfloat16)
    return pl.pallas_call(
        _leaving_rows_kernel,
        out_shape=[part, part, jax.ShapeDtypeStruct((depth, tokens), jnp.bfloat16)],
        in_specs=[SMEM] + [VMEM] * 4,
        out_specs=[VMEM] * 3,
        scratch_shapes=[pltpu.VMEM((tokens, depth), jnp.bfloat16)],
        compiler_params=pltpu.CompilerParams(vmem_limit_bytes=8 * 2**20),
        cost_estimate=pl.CostEstimate(flops=1, bytes_accessed=1, transcendentals=0),
        name="leaving_rows",
    )(meta, a, b, w_x, w_y)


def _pass_rows(joined, weight):
    return pl.pallas_call(
        _pass_rows_kernel,
        out_shape=jax.ShapeDtypeStruct((weight.shape[0], joined.shape[1]), jnp.bfloat16),
        in_specs=[VMEM] * 2,
        out_specs=VMEM,
        compiler_params=pltpu.CompilerParams(vmem_limit_bytes=8 * 2**20),
        cost_estimate=pl.CostEstimate(flops=1, bytes_accessed=1, transcendentals=0),
        name="pass_rows",
    )(joined, weight)


def _keep_rows(near, far, weight):
    part = jax.ShapeDtypeStruct((weight.shape[0], near.shape[1]), jnp.bfloat16)
    return pl.pallas_call(
        _keep_rows_kernel,
        out_shape=[part, part],
        in_specs=[VMEM] * 3,
        out_specs=[VMEM] * 2,
        compiler_params=pltpu.CompilerParams(vmem_limit_bytes=8 * 2**20),
        cost_estimate=pl.CostEstimate(flops=1, bytes_accessed=1, transcendentals=0),
        name="keep_rows",
    )(near, far, weight)


def _add_halves_kernel(a_half, b_half, a_ref, b_ref, out_ref):
    rows = out_ref.shape[0]
    a = a_ref[a_half * rows:(a_half + 1) * rows].astype(jnp.float32)
    b = b_ref[b_half * rows:(b_half + 1) * rows].astype(jnp.float32)
    out_ref[...] = (a + b).astype(out_ref.dtype)


def _add_halves(a, a_half, b, b_half):
    rows, tokens = a.shape[0] // 2, a.shape[1]
    return pl.pallas_call(
        functools.partial(_add_halves_kernel, a_half, b_half),
        out_shape=jax.ShapeDtypeStruct((rows, tokens), jnp.bfloat16),
        in_specs=[VMEM] * 2,
        out_specs=VMEM,
        compiler_params=pltpu.CompilerParams(vmem_limit_bytes=2 * 2**20),
        cost_estimate=pl.CostEstimate(flops=1, bytes_accessed=1, transcendentals=0),
        name="add_halves",
    )(a, b)


def _sum_parts(keep_ref, x1_ref, y1_ref, y2_ref, x2_ref):
    half = y2_ref.shape[0]
    f32 = jnp.float32
    first = keep_ref[:half].astype(f32) + x1_ref[:half].astype(f32) + y2_ref[...].astype(f32)
    second = keep_ref[half:].astype(f32) + y1_ref[:half].astype(f32) + x2_ref[...].astype(f32)
    return first.astype(jnp.bfloat16), second.astype(jnp.bfloat16)


def _finish_kernel(meta_ref, keep_ref, x1_ref, y1_ref, y2_ref, x2_ref, out_ref):
    half = y2_ref.shape[0]
    out_ref[:half], out_ref[half:] = _sum_parts(keep_ref, x1_ref, y1_ref, y2_ref, x2_ref)


def _finish_both_kernel(meta_ref, near_ref, keep_ref, x1_ref, y1_ref, y2_ref, x2_ref, out_ref):
    half, tokens = y2_ref.shape
    upper = lax.div(meta_ref[0], 4)
    first, second = _sum_parts(keep_ref, x1_ref, y1_ref, y2_ref, x2_ref)
    at = _rows((1 - upper) * tokens, tokens)
    out_ref[:half, at] = first
    out_ref[half:, at] = second
    out_ref[:, _rows(upper * tokens, tokens)] = near_ref[...]


def _finish(meta, keep, x1, y1, y2, x2, near=None):
    rows, tokens = keep.shape
    operands = [meta] + ([] if near is None else [near]) + [keep, x1, y1, y2, x2]
    return pl.pallas_call(
        _finish_kernel if near is None else _finish_both_kernel,
        out_shape=jax.ShapeDtypeStruct((rows, tokens if near is None else 2 * tokens), jnp.bfloat16),
        in_specs=[SMEM] + [VMEM] * (len(operands) - 1),
        out_specs=VMEM,
        compiler_params=pltpu.CompilerParams(vmem_limit_bytes=4 * 2**20),
        cost_estimate=pl.CostEstimate(flops=1, bytes_accessed=1, transcendentals=0),
        name="finish",
    )(*operands)


def _flip(x, axis, bits):
    n = lax.axis_size(axis)
    return lax.ppermute(x, axis, [(i, i ^ bits) for i in range(n)])


def per_device_fast(queries, keys, values, out_weight, doc_lengths, owners):
    places = lax.axis_size("ctx")
    kv0 = _join_keys_values(keys, values)
    kv2 = lax.ppermute(kv0, "ctx", [(i, i + 2) for i in range(places - 2)])
    kv1 = _flip(kv0, "ctx", 1)
    meta = jnp.concatenate([
        lax.axis_index("ctx").reshape(1), lax.axis_index("head").reshape(1), owners.reshape(-1), doc_lengths,
    ]).astype(jnp.int32)
    leaving, queries = _queries_for_other_core(meta, queries)
    other = _flip(leaving, "ctx", 1)
    (w_x,) = _stage_weights(("x",), meta, out_weight, 36)
    kv2, w_x = lax.optimization_barrier((kv2, w_x))
    kv = (kv0, kv1, kv2, _flip(kv2, "ctx", 1))
    near1, far3, w_y = _attend_groups((1, 3), ("y",), meta, queries, other, kv, out_weight)
    near1, far3 = _flip(near1, "ctx", 2), _flip(far3, "ctx", 6)
    far2, near0, w_pass = _attend_groups((2, 0), ("pass",), meta, queries, other, kv, out_weight)
    far2 = _flip(far2, "ctx", 4)

    xmsg, ymsg, near = _leaving_rows(meta, near0, near1, w_x, w_y)
    xmsg, ymsg, far3 = lax.optimization_barrier((xmsg, ymsg, far3))
    near_x1, near_y1 = _flip(xmsg, "head", 1), _flip(ymsg, "head", 2)
    near_pass = _pass_rows(near, w_pass)
    near_pass, keep_meta = lax.optimization_barrier((near_pass, meta))
    (w_keep,) = _stage_weights(("keep",), keep_meta, out_weight, 8)
    near_pass, w_keep = lax.optimization_barrier((near_pass, w_keep))
    ymsg, xmsg = _add_halves(near_pass, 0, near_x1, 1), _add_halves(near_pass, 1, near_y1, 1)
    meta, ymsg, xmsg = lax.optimization_barrier((meta, ymsg, xmsg))
    near_y2, near_x2 = _flip(ymsg, "head", 2), _flip(xmsg, "head", 1)

    xmsg, ymsg, far = _leaving_rows(meta, far2, far3, w_x, w_y)
    xmsg, ymsg, near_y2, near_x2 = lax.optimization_barrier((xmsg, ymsg, near_y2, near_x2))
    far_x1, far_y1 = _flip(xmsg, "head", 1), _flip(ymsg, "head", 2)
    far_pass = _pass_rows(far, w_pass)
    near_keep, far_keep = _keep_rows(near, far, w_keep)
    near = _finish(meta, near_keep, near_x1, near_y1, near_y2, near_x2)
    far_pass, near, far_keep = lax.optimization_barrier((far_pass, near, far_keep))
    far_y2 = _flip(_add_halves(far_pass, 0, far_x1, 1), "head", 2)
    far_x2 = _flip(_add_halves(far_pass, 1, far_y1, 1), "head", 1)
    return _finish(meta, far_keep, far_x1, far_y1, far_y2, far_x2, near)


def solution(mesh):
    in_specs = (P("ctx", "head"), P("ctx", "head"), P("ctx", "head"), P(None, "head"), P(), P())
    out_specs = P("head", "ctx")
    fast = mesh.shape["ctx"] == PIECES and mesh.shape["head"] == N_FAST_HEAD
    return jax.shard_map(
        per_device_fast if fast else per_device, mesh=mesh, in_specs=in_specs, out_specs=out_specs, check_vma=False
    )
```

```python
import functools
import math

import jax
import jax.numpy as jnp
from jax import lax
from jax.experimental import pallas as pl
from jax.experimental.pallas import tpu as pltpu
from jax.sharding import PartitionSpec as P

HEAD_SIZE = 128
PIECES = 8
N_FAST_HEAD = 4


MASKED = -1e30


def document_index(positions, doc_starts):
    return jnp.sum((positions[:, None] >= doc_starts[None, :]).astype(jnp.int32), axis=1) - 1


def attend(query_rows, query_pos, keys, values, doc_starts):
    row_count = query_rows.shape[0]
    key_heads = keys.shape[1] // HEAD_SIZE
    group_length = query_rows.shape[1] // keys.shape[1]
    query_heads = query_rows.reshape(row_count, key_heads, group_length, HEAD_SIZE)
    query_doc = document_index(query_pos, doc_starts)
    score_scale = 1.0 / math.sqrt(HEAD_SIZE)
    initial = (
        jnp.full((row_count, key_heads, group_length), MASKED, jnp.float32),
        jnp.zeros((row_count, key_heads, group_length), jnp.float32),
        jnp.zeros((row_count, key_heads, group_length, HEAD_SIZE), jnp.float32),
    )
    key_piece = lax.all_gather(keys, "ctx", axis=0, tiled=True)
    value_piece = lax.all_gather(values, "ctx", axis=0, tiled=True)
    piece_rows = key_piece.shape[0]
    tile_rows = math.gcd(piece_rows, 512)

    def one_tile(tile_index, running):
        tile_start = tile_index * tile_rows
        key_block = lax.dynamic_slice_in_dim(key_piece, tile_start, tile_rows, 0).reshape(
            tile_rows, key_heads, HEAD_SIZE
        )
        value_block = lax.dynamic_slice_in_dim(value_piece, tile_start, tile_rows, 0).reshape(
            tile_rows, key_heads, HEAD_SIZE
        )
        key_pos = tile_start + jnp.arange(tile_rows, dtype=jnp.int32)
        key_doc = document_index(key_pos, doc_starts)
        allowed = (query_doc[:, None] == key_doc[None, :]) & (
            key_pos[None, :] <= query_pos[:, None]
        )
        running_max, running_sum, weighted = running
        scores = (
            jnp.einsum("rkgd,nkd->rkgn", query_heads, key_block, preferred_element_type=jnp.float32)
            * score_scale
        )
        allowed_all = allowed[:, None, None, :]
        scores = jnp.where(allowed_all, scores, MASKED)
        new_max = jnp.maximum(running_max, jnp.max(scores, axis=-1))
        factor = jnp.exp(running_max - new_max)
        weights = jnp.where(allowed_all, jnp.exp(scores - new_max[..., None]), 0.0)
        new_sum = running_sum * factor + jnp.sum(weights, axis=-1)
        new_weighted = weighted * factor[..., None] + jnp.einsum(
            "rkgn,nkd->rkgd",
            weights.astype(jnp.bfloat16),
            value_block,
            preferred_element_type=jnp.float32,
        )
        return (new_max, new_sum, new_weighted)

    final_max, final_sum, weighted = lax.fori_loop(0, piece_rows // tile_rows, one_tile, initial)
    result = weighted / jnp.maximum(final_sum, 1.0)[..., None]
    return result.reshape(row_count, key_heads * group_length * HEAD_SIZE).astype(jnp.bfloat16)


def project(context, out_weight):
    return lax.psum_scatter(
        lax.dot_general(
            out_weight, context, (((1,), (1,)), ((), ())), preferred_element_type=jnp.float32
        ).astype(jnp.bfloat16),
        "head",
        scatter_dimension=0,
        tiled=True,
    )


def per_device(queries, keys, values, out_weight, doc_lengths, owners):
    place_count = lax.axis_size("ctx")
    own_index = lax.axis_index("ctx")
    token_count = queries.shape[0]
    block_rows = token_count // PIECES
    doc_ends = jnp.cumsum(doc_lengths)
    doc_starts = doc_ends - doc_lengths
    owner_table = owners[:, 0].reshape(place_count, PIECES)
    own_owners = lax.dynamic_index_in_dim(owner_table, own_index, 0, keepdims=False)
    place_ids = jnp.arange(place_count, dtype=jnp.int32)
    send_pick = (own_owners[None, :] == place_ids[:, None]).astype(jnp.bfloat16)
    grouped = queries.reshape(PIECES, block_rows, queries.shape[1])
    outgoing = jnp.einsum(
        "oc,chw->ohw", send_pick, grouped, preferred_element_type=jnp.float32
    ).astype(jnp.bfloat16)
    arrived = lax.all_to_all(outgoing, "ctx", split_axis=0, concat_axis=0, tiled=True)
    slot_hits = (owner_table == own_index).astype(jnp.int32)
    slot_live = jnp.sum(slot_hits, axis=1)
    picked = jnp.sum(slot_hits * jnp.arange(PIECES, dtype=jnp.int32)[None, :], axis=1)
    slot_pos = (place_ids[:, None] * PIECES + picked[:, None]) * block_rows + jnp.arange(
        block_rows, dtype=jnp.int32
    )[None, :]
    query_pos = jnp.where(slot_live[:, None] > 0, slot_pos, -1).reshape(-1)
    context = attend(
        arrived.reshape(place_count * block_rows, queries.shape[1]),
        query_pos,
        keys,
        values,
        doc_starts,
    )
    return project(context, out_weight)


SMEM = pl.BlockSpec(memory_space=pltpu.SMEM)
VMEM = pl.BlockSpec(memory_space=pltpu.VMEM)
HBM = pl.BlockSpec(memory_space=pltpu.HBM)


OWNERS_AT = 2


def _find_piece(table_ref, source, owner):
    piece = jnp.int32(0)
    for i in range(PIECES):
        piece = jnp.where(table_ref[OWNERS_AT + source * PIECES + i] == owner, jnp.int32(i), piece)
    return piece


def _rows(start, size):
    return pl.ds(pl.multiple_of(start, size), size)


def _join_keys_values_kernel(keys_ref, values_ref, out_ref, sems):
    rows = keys_ref.shape[0]
    copies = [
        pltpu.make_async_copy(keys_ref, out_ref.at[pl.ds(0, rows)], sems.at[0]),
        pltpu.make_async_copy(values_ref, out_ref.at[pl.ds(rows, rows)], sems.at[1]),
    ]
    for copy in copies:
        copy.start()
    for copy in copies:
        copy.wait()


def _join_keys_values(keys, values):
    return pl.pallas_call(
        _join_keys_values_kernel,
        out_shape=jax.ShapeDtypeStruct((2 * keys.shape[0], keys.shape[1]), keys.dtype),
        in_specs=[HBM] * 2,
        out_specs=VMEM,
        scratch_shapes=[pltpu.SemaphoreType.DMA((2,))],
        compiler_params=pltpu.CompilerParams(vmem_limit_bytes=2 * 2**20),
        cost_estimate=pl.CostEstimate(flops=1, bytes_accessed=1, transcendentals=0),
        name="join_keys_values",
    )(keys, values)


def _queries_for_other_core_kernel(meta_ref, queries_ref, out_ref, kept_ref, sem):
    copy = pltpu.make_async_copy(queries_ref, kept_ref, sem)
    copy.start()
    copy.wait()
    c = meta_ref[0]
    core = lax.rem(c, 2)
    rows = queries_ref.shape[0] // PIECES
    for j in range(PIECES // 2):
        piece = _find_piece(meta_ref, c, 2 * j + 1 - core)
        out_ref[j * rows:(j + 1) * rows] = kept_ref[_rows(piece * rows, rows)]


def _queries_for_other_core(meta, queries):
    return pl.pallas_call(
        _queries_for_other_core_kernel,
        out_shape=[
            jax.ShapeDtypeStruct((queries.shape[0] // 2, queries.shape[1]), queries.dtype),
            jax.ShapeDtypeStruct(queries.shape, queries.dtype),
        ],
        in_specs=[SMEM, HBM],
        out_specs=[VMEM] * 2,
        scratch_shapes=[pltpu.SemaphoreType.DMA],
        compiler_params=pltpu.CompilerParams(vmem_limit_bytes=2 * 2**20),
        cost_estimate=pl.CostEstimate(flops=1, bytes_accessed=1, transcendentals=0),
        name="queries_for_other_core",
    )(meta, queries)


QUARTERS = {
    "x": ((1, 0), (3, 0)),
    "y": ((2, 1), (3, 1)),
    "pass": ((2, 0), (1, 1)),
    "keep": ((0, 0), (0, 1)),
}


def _weight_copies(names, meta_ref, w_ref, out_refs, sems):
    half = w_ref.shape[0] // (2 * N_FAST_HEAD)
    copies = []
    for n, name in enumerate(names):
        for i, (flip, side) in enumerate(QUARTERS[name]):
            row = (meta_ref[1] ^ flip) * (2 * half) + side * half
            copies.append(pltpu.make_async_copy(
                w_ref.at[_rows(row, half)], out_refs[n].at[pl.ds(i * half, half)], sems.at[2 * n + i]))
    return copies


def _quarter(out_weight):
    return jax.ShapeDtypeStruct((out_weight.shape[0] // N_FAST_HEAD, out_weight.shape[1]), out_weight.dtype)


def _stage_kernel(names, meta_ref, w_ref, *rest):
    copies = _weight_copies(names, meta_ref, w_ref, rest[:-1], rest[-1])
    for copy in copies:
        copy.start()
    for copy in copies:
        copy.wait()


def _stage_weights(names, meta, out_weight, room):
    return pl.pallas_call(
        functools.partial(_stage_kernel, names),
        out_shape=[_quarter(out_weight) for _ in names],
        in_specs=[SMEM, HBM],
        out_specs=[VMEM] * len(names),
        scratch_shapes=[pltpu.SemaphoreType.DMA((2 * len(names),))],
        compiler_params=pltpu.CompilerParams(vmem_limit_bytes=room * 2**20),
        cost_estimate=pl.CostEstimate(flops=1, bytes_accessed=1, transcendentals=0),
        name="stage_weights",
    )(meta, out_weight)


def _attend_kernel(
    groups, names, meta_ref, queries_ref, other_ref,
    kv0_ref, kv1_ref, kv2_ref, kv3_ref, w_ref,
    *rest,
):
    count = len(groups)
    out_refs, w_out = rest[:count], rest[count:count + len(names)]
    kbuf, vbuf, qbuf, ctxbuf, w_sems = rest[count + len(names):]
    w_copies = _weight_copies(names, meta_ref, w_ref, w_out, w_sems)
    for copy in w_copies:
        copy.start()
    c = meta_ref[0]
    core = lax.rem(c, 2)
    z = lax.div(c, 2)
    rows = kv0_ref.shape[0] // 2
    piece_rows = rows // PIECES
    tile = 128
    heads = kv0_ref.shape[1] // HEAD_SIZE
    slots = (2 + core, 3 - core, core, 1 - core)
    for b, kv_ref in enumerate((kv0_ref, kv1_ref, kv2_ref, kv3_ref)):
        at = _rows(slots[b] * rows, rows)
        kbuf[at] = kv_ref[:rows]
        for kv in range(heads):
            vbuf[at, 2 * kv * HEAD_SIZE:(2 * kv + 1) * HEAD_SIZE] = (
                kv_ref[rows:, kv * HEAD_SIZE:(kv + 1) * HEAD_SIZE])
            vbuf[at, (2 * kv + 1) * HEAD_SIZE:(2 * kv + 2) * HEAD_SIZE] = jnp.ones((rows, HEAD_SIZE), jnp.bfloat16)
    starts = []
    for n, k in enumerate(groups):
        zdest = z ^ k
        owner = 2 * zdest + core
        mine = _find_piece(meta_ref, c, owner)
        theirs = _find_piece(meta_ref, c + 1 - 2 * core, owner)
        qbuf[2 * n + core] = queries_ref[_rows(mine * piece_rows, piece_rows)]
        qbuf[2 * n + 1 - core] = other_ref[_rows(zdest * piece_rows, piece_rows)]
        at0 = jnp.where(core == 0, mine, theirs)
        at1 = jnp.where(core == 0, theirs, mine)
        starts.append((at0 * piece_rows, rows + at1 * piece_rows))
    doc_start = []
    running = jnp.int32(0)
    lengths_at = OWNERS_AT + PIECES * PIECES
    for d in range(lengths_at, meta_ref.shape[0]):
        doc_start.append(running)
        running = running + meta_ref[d]
    base = 2 * rows * (z - 1)
    group = queries_ref.shape[1] // kv0_ref.shape[1]
    scale = math.log2(math.e) / math.sqrt(HEAD_SIZE)
    span = 5 * tile

    def piece_keys(p0):
        first = pl.multiple_of(lax.div(p0, tile) * tile + 2 * rows - 4 * tile, tile)
        pos = 2 * rows * z + p0 + lax.broadcasted_iota(jnp.int32, (piece_rows, 1), 0)
        low = jnp.zeros((piece_rows, 1), jnp.int32)
        for start in doc_start:
            low = jnp.where(pos >= start, start, low)
        key_pos = base + first + lax.broadcasted_iota(jnp.int32, (piece_rows, span), 1)
        return first, (key_pos >= low) & (key_pos <= pos)

    def some_pieces(pieces):
        units, scores, weights = [], [], []
        for n, p0 in pieces:
            first, allowed = piece_keys(p0)
            units += [(n, kv, first, allowed) for kv in range(heads)]
        for n, kv, first, allowed in units:
            q = jnp.concatenate(
                [qbuf[n, :, pl.ds((kv * group + g) * HEAD_SIZE, HEAD_SIZE)] for g in range(group)], axis=0)
            k = kbuf[pl.ds(first, span), pl.ds(kv * HEAD_SIZE, HEAD_SIZE)]
            scores.append(lax.dot_general(q, k, (((1,), (1,)), ((), ())), preferred_element_type=jnp.float32))
        for (n, kv, first, allowed), s in zip(units, scores):
            s = jnp.where(allowed[None], s.reshape(group, piece_rows, span), MASKED)
            w = jnp.exp2((s - jnp.max(s, axis=2, keepdims=True)) * scale)
            weights.append(w.astype(jnp.bfloat16).reshape(group * piece_rows, span))
        for (n, kv, first, allowed), w in zip(units, weights):
            o = jnp.dot(w, vbuf[pl.ds(first, span), pl.ds(kv * 2 * HEAD_SIZE, 2 * HEAD_SIZE)],
                        preferred_element_type=jnp.float32)
            o = (o[:, :HEAD_SIZE] / o[:, HEAD_SIZE:]).astype(jnp.bfloat16)
            for g in range(group):
                ctxbuf[n, :, pl.ds((kv * group + g) * HEAD_SIZE, HEAD_SIZE)] = o[g * piece_rows:(g + 1) * piece_rows]

    together = 2

    def step(i, carry):
        pieces = []
        for j in range(together):
            n = i * together + j
            p0 = starts[0][0]
            for m in range(1, 2 * count):
                p0 = jnp.where(n == m, starts[m // 2][m % 2], p0)
            pieces.append((n, p0))
        some_pieces(pieces)
        return carry

    lax.fori_loop(0, 2 * count // together, step, 0)
    for n, out_ref in enumerate(out_refs):
        out_ref[...] = ctxbuf[2 * n:2 * n + 2].reshape(out_ref.shape)
    for copy in w_copies:
        copy.wait()


def _attend_groups(groups, names, meta, queries, other, kv, out_weight):
    piece = queries.shape[0] // PIECES
    rows = kv[0].shape[0] // 2
    return pl.pallas_call(
        functools.partial(_attend_kernel, groups, names),
        out_shape=[jax.ShapeDtypeStruct((2 * piece, queries.shape[1]), jnp.bfloat16) for _ in groups]
        + [_quarter(out_weight) for _ in names],
        in_specs=[SMEM] + [VMEM] * 6 + [HBM],
        out_specs=[VMEM] * (len(groups) + len(names)),
        scratch_shapes=[
            pltpu.VMEM((4 * rows, kv[0].shape[1]), jnp.bfloat16),
            pltpu.VMEM((4 * rows, 2 * kv[0].shape[1]), jnp.bfloat16),
            pltpu.VMEM((2 * len(groups), piece, queries.shape[1]), jnp.bfloat16),
            pltpu.VMEM((2 * len(groups), piece, queries.shape[1]), jnp.bfloat16),
            pltpu.SemaphoreType.DMA((2 * len(names),)),
        ],
        compiler_params=pltpu.CompilerParams(vmem_limit_bytes=12 * 2**20),
        cost_estimate=pl.CostEstimate(flops=1, bytes_accessed=1, transcendentals=0),
        name="attend_groups",
    )(meta, queries, other, *kv, out_weight)


def _dot_to(out_ref, weight_ref, tokens):
    out_ref[...] = jnp.dot(weight_ref[...], tokens, preferred_element_type=jnp.float32).astype(out_ref.dtype)


def _leaving_rows_kernel(meta_ref, a_ref, b_ref, wx_ref, wy_ref, x_ref, y_ref, joined_ref, catbuf):
    second = lax.rem(lax.div(meta_ref[0], 2), 2)
    mid = a_ref.shape[0]
    catbuf[_rows(second * mid, mid)] = a_ref[...]
    catbuf[_rows((1 - second) * mid, mid)] = b_ref[...]
    joined = catbuf[...].T
    joined_ref[...] = joined
    _dot_to(x_ref, wx_ref, joined)
    _dot_to(y_ref, wy_ref, joined)


def _pass_rows_kernel(joined_ref, w_ref, out_ref):
    _dot_to(out_ref, w_ref, joined_ref[...])


def _keep_rows_kernel(near_ref, far_ref, w_ref, near_out, far_out):
    tokens = near_ref.shape[1]
    both = jnp.concatenate([near_ref[...], far_ref[...]], axis=1)
    out = jnp.dot(w_ref[...], both, preferred_element_type=jnp.float32).astype(near_out.dtype)
    near_out[...] = out[:, :tokens]
    far_out[...] = out[:, tokens:]


def _leaving_rows(meta, a, b, w_x, w_y):
    (rows, depth), tokens = w_x.shape, a.shape[0] + b.shape[0]
    part = jax.ShapeDtypeStruct((rows, tokens), jnp.bfloat16)
    return pl.pallas_call(
        _leaving_rows_kernel,
        out_shape=[part, part, jax.ShapeDtypeStruct((depth, tokens), jnp.bfloat16)],
        in_specs=[SMEM] + [VMEM] * 4,
        out_specs=[VMEM] * 3,
        scratch_shapes=[pltpu.VMEM((tokens, depth), jnp.bfloat16)],
        compiler_params=pltpu.CompilerParams(vmem_limit_bytes=8 * 2**20),
        cost_estimate=pl.CostEstimate(flops=1, bytes_accessed=1, transcendentals=0),
        name="leaving_rows",
    )(meta, a, b, w_x, w_y)


def _pass_rows(joined, weight):
    return pl.pallas_call(
        _pass_rows_kernel,
        out_shape=jax.ShapeDtypeStruct((weight.shape[0], joined.shape[1]), jnp.bfloat16),
        in_specs=[VMEM] * 2,
        out_specs=VMEM,
        compiler_params=pltpu.CompilerParams(vmem_limit_bytes=8 * 2**20),
        cost_estimate=pl.CostEstimate(flops=1, bytes_accessed=1, transcendentals=0),
        name="pass_rows",
    )(joined, weight)


def _keep_rows(near, far, weight):
    part = jax.ShapeDtypeStruct((weight.shape[0], near.shape[1]), jnp.bfloat16)
    return pl.pallas_call(
        _keep_rows_kernel,
        out_shape=[part, part],
        in_specs=[VMEM] * 3,
        out_specs=[VMEM] * 2,
        compiler_params=pltpu.CompilerParams(vmem_limit_bytes=8 * 2**20),
        cost_estimate=pl.CostEstimate(flops=1, bytes_accessed=1, transcendentals=0),
        name="keep_rows",
    )(near, far, weight)


def _add_halves_kernel(a_half, b_half, a_ref, b_ref, out_ref):
    rows = out_ref.shape[0]
    a = a_ref[a_half * rows:(a_half + 1) * rows].astype(jnp.float32)
    b = b_ref[b_half * rows:(b_half + 1) * rows].astype(jnp.float32)
    out_ref[...] = (a + b).astype(out_ref.dtype)


def _add_halves(a, a_half, b, b_half):
    rows, tokens = a.shape[0] // 2, a.shape[1]
    return pl.pallas_call(
        functools.partial(_add_halves_kernel, a_half, b_half),
        out_shape=jax.ShapeDtypeStruct((rows, tokens), jnp.bfloat16),
        in_specs=[VMEM] * 2,
        out_specs=VMEM,
        compiler_params=pltpu.CompilerParams(vmem_limit_bytes=2 * 2**20),
        cost_estimate=pl.CostEstimate(flops=1, bytes_accessed=1, transcendentals=0),
        name="add_halves",
    )(a, b)


def _sum_parts(keep_ref, x1_ref, y1_ref, y2_ref, x2_ref):
    half = y2_ref.shape[0]
    f32 = jnp.float32
    first = keep_ref[:half].astype(f32) + x1_ref[:half].astype(f32) + y2_ref[...].astype(f32)
    second = keep_ref[half:].astype(f32) + y1_ref[:half].astype(f32) + x2_ref[...].astype(f32)
    return first.astype(jnp.bfloat16), second.astype(jnp.bfloat16)


def _finish_kernel(meta_ref, keep_ref, x1_ref, y1_ref, y2_ref, x2_ref, out_ref):
    half = y2_ref.shape[0]
    out_ref[:half], out_ref[half:] = _sum_parts(keep_ref, x1_ref, y1_ref, y2_ref, x2_ref)


def _finish_both_kernel(meta_ref, near_ref, keep_ref, x1_ref, y1_ref, y2_ref, x2_ref, out_ref):
    half, tokens = y2_ref.shape
    upper = lax.div(meta_ref[0], 4)
    first, second = _sum_parts(keep_ref, x1_ref, y1_ref, y2_ref, x2_ref)
    at = _rows((1 - upper) * tokens, tokens)
    out_ref[:half, at] = first
    out_ref[half:, at] = second
    out_ref[:, _rows(upper * tokens, tokens)] = near_ref[...]


def _finish(meta, keep, x1, y1, y2, x2, near=None):
    rows, tokens = keep.shape
    operands = [meta] + ([] if near is None else [near]) + [keep, x1, y1, y2, x2]
    return pl.pallas_call(
        _finish_kernel if near is None else _finish_both_kernel,
        out_shape=jax.ShapeDtypeStruct((rows, tokens if near is None else 2 * tokens), jnp.bfloat16),
        in_specs=[SMEM] + [VMEM] * (len(operands) - 1),
        out_specs=VMEM,
        compiler_params=pltpu.CompilerParams(vmem_limit_bytes=4 * 2**20),
        cost_estimate=pl.CostEstimate(flops=1, bytes_accessed=1, transcendentals=0),
        name="finish",
    )(*operands)


def _flip(x, axis, bits):
    n = lax.axis_size(axis)
    return lax.ppermute(x, axis, [(i, i ^ bits) for i in range(n)])


def per_device_fast(queries, keys, values, out_weight, doc_lengths, owners):
    places = lax.axis_size("ctx")
    queries, keys, values, out_weight = (
        pltpu.with_memory_space_constraint(x, pltpu.HBM) for x in (queries, keys, values, out_weight))
    kv0 = _join_keys_values(keys, values)
    kv2 = lax.ppermute(kv0, "ctx", [(i, i + 2) for i in range(places - 2)])
    kv1 = _flip(kv0, "ctx", 1)
    meta = jnp.concatenate([
        lax.axis_index("ctx").reshape(1), lax.axis_index("head").reshape(1), owners.reshape(-1), doc_lengths,
    ]).astype(jnp.int32)
    leaving, queries = _queries_for_other_core(meta, queries)
    other = _flip(leaving, "ctx", 1)
    (w_x,) = _stage_weights(("x",), meta, out_weight, 8)
    kv2, w_x = lax.optimization_barrier((kv2, w_x))
    kv = (kv0, kv1, kv2, _flip(kv2, "ctx", 1))
    near1, far3, w_y = _attend_groups((1, 3), ("y",), meta, queries, other, kv, out_weight)
    near1, far3 = _flip(near1, "ctx", 2), _flip(far3, "ctx", 6)
    far2, near0, w_pass = _attend_groups((2, 0), ("pass",), meta, queries, other, kv, out_weight)
    far2 = _flip(far2, "ctx", 4)

    xmsg, ymsg, near = _leaving_rows(meta, near0, near1, w_x, w_y)
    xmsg, ymsg, far3 = lax.optimization_barrier((xmsg, ymsg, far3))
    near_x1, near_y1 = _flip(xmsg, "head", 1), _flip(ymsg, "head", 2)
    near_pass = _pass_rows(near, w_pass)
    near_pass, keep_meta = lax.optimization_barrier((near_pass, meta))
    (w_keep,) = _stage_weights(("keep",), keep_meta, out_weight, 8)
    near_pass, w_keep = lax.optimization_barrier((near_pass, w_keep))
    ymsg, xmsg = _add_halves(near_pass, 0, near_x1, 1), _add_halves(near_pass, 1, near_y1, 1)
    meta, ymsg, xmsg = lax.optimization_barrier((meta, ymsg, xmsg))
    near_y2, near_x2 = _flip(ymsg, "head", 2), _flip(xmsg, "head", 1)

    xmsg, ymsg, far = _leaving_rows(meta, far2, far3, w_x, w_y)
    xmsg, ymsg, near_y2, near_x2 = lax.optimization_barrier((xmsg, ymsg, near_y2, near_x2))
    far_x1, far_y1 = _flip(xmsg, "head", 1), _flip(ymsg, "head", 2)
    far_pass = _pass_rows(far, w_pass)
    near_keep, far_keep = _keep_rows(near, far, w_keep)
    near = _finish(meta, near_keep, near_x1, near_y1, near_y2, near_x2)
    far_pass, near, far_keep = lax.optimization_barrier((far_pass, near, far_keep))
    far_y2 = _flip(_add_halves(far_pass, 0, far_x1, 1), "head", 2)
    far_x2 = _flip(_add_halves(far_pass, 1, far_y1, 1), "head", 1)
    return _finish(meta, far_keep, far_x1, far_y1, far_y2, far_x2, near)


def solution(mesh):
    in_specs = (P("ctx", "head"), P("ctx", "head"), P("ctx", "head"), P(None, "head"), P(), P())
    out_specs = P("head", "ctx")
    fast = mesh.shape["ctx"] == PIECES and mesh.shape["head"] == N_FAST_HEAD
    return jax.shard_map(
        per_device_fast if fast else per_device, mesh=mesh, in_specs=in_specs, out_specs=out_specs, check_vma=False
    )
```

```python
import functools
import math

import jax
import jax.numpy as jnp
from jax import lax
from jax.experimental import pallas as pl
from jax.experimental.pallas import tpu as pltpu
from jax.sharding import PartitionSpec as P

HEAD_SIZE = 128
PIECES = 8
N_FAST_HEAD = 4


MASKED = -1e30


def document_index(positions, doc_starts):
    return jnp.sum((positions[:, None] >= doc_starts[None, :]).astype(jnp.int32), axis=1) - 1


def attend(query_rows, query_pos, keys, values, doc_starts):
    row_count = query_rows.shape[0]
    key_heads = keys.shape[1] // HEAD_SIZE
    group_length = query_rows.shape[1] // keys.shape[1]
    query_heads = query_rows.reshape(row_count, key_heads, group_length, HEAD_SIZE)
    query_doc = document_index(query_pos, doc_starts)
    score_scale = 1.0 / math.sqrt(HEAD_SIZE)
    initial = (
        jnp.full((row_count, key_heads, group_length), MASKED, jnp.float32),
        jnp.zeros((row_count, key_heads, group_length), jnp.float32),
        jnp.zeros((row_count, key_heads, group_length, HEAD_SIZE), jnp.float32),
    )
    key_piece = lax.all_gather(keys, "ctx", axis=0, tiled=True)
    value_piece = lax.all_gather(values, "ctx", axis=0, tiled=True)
    piece_rows = key_piece.shape[0]
    tile_rows = math.gcd(piece_rows, 512)

    def one_tile(tile_index, running):
        tile_start = tile_index * tile_rows
        key_block = lax.dynamic_slice_in_dim(key_piece, tile_start, tile_rows, 0).reshape(
            tile_rows, key_heads, HEAD_SIZE
        )
        value_block = lax.dynamic_slice_in_dim(value_piece, tile_start, tile_rows, 0).reshape(
            tile_rows, key_heads, HEAD_SIZE
        )
        key_pos = tile_start + jnp.arange(tile_rows, dtype=jnp.int32)
        key_doc = document_index(key_pos, doc_starts)
        allowed = (query_doc[:, None] == key_doc[None, :]) & (
            key_pos[None, :] <= query_pos[:, None]
        )
        running_max, running_sum, weighted = running
        scores = (
            jnp.einsum("rkgd,nkd->rkgn", query_heads, key_block, preferred_element_type=jnp.float32)
            * score_scale
        )
        allowed_all = allowed[:, None, None, :]
        scores = jnp.where(allowed_all, scores, MASKED)
        new_max = jnp.maximum(running_max, jnp.max(scores, axis=-1))
        factor = jnp.exp(running_max - new_max)
        weights = jnp.where(allowed_all, jnp.exp(scores - new_max[..., None]), 0.0)
        new_sum = running_sum * factor + jnp.sum(weights, axis=-1)
        new_weighted = weighted * factor[..., None] + jnp.einsum(
            "rkgn,nkd->rkgd",
            weights.astype(jnp.bfloat16),
            value_block,
            preferred_element_type=jnp.float32,
        )
        return (new_max, new_sum, new_weighted)

    final_max, final_sum, weighted = lax.fori_loop(0, piece_rows // tile_rows, one_tile, initial)
    result = weighted / jnp.maximum(final_sum, 1.0)[..., None]
    return result.reshape(row_count, key_heads * group_length * HEAD_SIZE).astype(jnp.bfloat16)


def project(context, out_weight):
    return lax.psum_scatter(
        lax.dot_general(
            out_weight, context, (((1,), (1,)), ((), ())), preferred_element_type=jnp.float32
        ).astype(jnp.bfloat16),
        "head",
        scatter_dimension=0,
        tiled=True,
    )


def per_device(queries, keys, values, out_weight, doc_lengths, owners):
    place_count = lax.axis_size("ctx")
    own_index = lax.axis_index("ctx")
    token_count = queries.shape[0]
    block_rows = token_count // PIECES
    doc_ends = jnp.cumsum(doc_lengths)
    doc_starts = doc_ends - doc_lengths
    owner_table = owners[:, 0].reshape(place_count, PIECES)
    own_owners = lax.dynamic_index_in_dim(owner_table, own_index, 0, keepdims=False)
    place_ids = jnp.arange(place_count, dtype=jnp.int32)
    send_pick = (own_owners[None, :] == place_ids[:, None]).astype(jnp.bfloat16)
    grouped = queries.reshape(PIECES, block_rows, queries.shape[1])
    outgoing = jnp.einsum(
        "oc,chw->ohw", send_pick, grouped, preferred_element_type=jnp.float32
    ).astype(jnp.bfloat16)
    arrived = lax.all_to_all(outgoing, "ctx", split_axis=0, concat_axis=0, tiled=True)
    slot_hits = (owner_table == own_index).astype(jnp.int32)
    slot_live = jnp.sum(slot_hits, axis=1)
    picked = jnp.sum(slot_hits * jnp.arange(PIECES, dtype=jnp.int32)[None, :], axis=1)
    slot_pos = (place_ids[:, None] * PIECES + picked[:, None]) * block_rows + jnp.arange(
        block_rows, dtype=jnp.int32
    )[None, :]
    query_pos = jnp.where(slot_live[:, None] > 0, slot_pos, -1).reshape(-1)
    context = attend(
        arrived.reshape(place_count * block_rows, queries.shape[1]),
        query_pos,
        keys,
        values,
        doc_starts,
    )
    return project(context, out_weight)


SMEM = pl.BlockSpec(memory_space=pltpu.SMEM)
VMEM = pl.BlockSpec(memory_space=pltpu.VMEM)
HBM = pl.BlockSpec(memory_space=pltpu.HBM)


OWNERS_AT = 2


def _find_piece(table_ref, source, owner):
    piece = jnp.int32(0)
    for i in range(PIECES):
        piece = jnp.where(table_ref[OWNERS_AT + source * PIECES + i] == owner, jnp.int32(i), piece)
    return piece


def _rows(start, size):
    return pl.ds(pl.multiple_of(start, size), size)


def _join_keys_values_kernel(keys_ref, values_ref, out_ref, sems):
    rows = keys_ref.shape[0]
    copies = [
        pltpu.make_async_copy(keys_ref, out_ref.at[pl.ds(0, rows)], sems.at[0]),
        pltpu.make_async_copy(values_ref, out_ref.at[pl.ds(rows, rows)], sems.at[1]),
    ]
    for copy in copies:
        copy.start()
    for copy in copies:
        copy.wait()


def _join_keys_values(keys, values):
    return pl.pallas_call(
        _join_keys_values_kernel,
        out_shape=jax.ShapeDtypeStruct((2 * keys.shape[0], keys.shape[1]), keys.dtype),
        in_specs=[HBM] * 2,
        out_specs=VMEM,
        scratch_shapes=[pltpu.SemaphoreType.DMA((2,))],
        compiler_params=pltpu.CompilerParams(vmem_limit_bytes=2 * 2**20),
        cost_estimate=pl.CostEstimate(flops=1, bytes_accessed=1, transcendentals=0),
        name="join_keys_values",
    )(keys, values)


def _queries_for_other_core_kernel(meta_ref, queries_ref, out_ref, kept_ref, sem):
    copy = pltpu.make_async_copy(queries_ref, kept_ref, sem)
    copy.start()
    copy.wait()
    c = meta_ref[0]
    core = lax.rem(c, 2)
    rows = queries_ref.shape[0] // PIECES
    for j in range(PIECES // 2):
        piece = _find_piece(meta_ref, c, 2 * j + 1 - core)
        out_ref[j * rows:(j + 1) * rows] = kept_ref[_rows(piece * rows, rows)]


def _queries_for_other_core(meta, queries):
    return pl.pallas_call(
        _queries_for_other_core_kernel,
        out_shape=[
            jax.ShapeDtypeStruct((queries.shape[0] // 2, queries.shape[1]), queries.dtype),
            jax.ShapeDtypeStruct(queries.shape, queries.dtype),
        ],
        in_specs=[SMEM, HBM],
        out_specs=[VMEM] * 2,
        scratch_shapes=[pltpu.SemaphoreType.DMA],
        compiler_params=pltpu.CompilerParams(vmem_limit_bytes=2 * 2**20),
        cost_estimate=pl.CostEstimate(flops=1, bytes_accessed=1, transcendentals=0),
        name="queries_for_other_core",
    )(meta, queries)


QUARTERS = {
    "x": ((1, 0), (3, 0)),
    "y": ((2, 1), (3, 1)),
    "pass": ((2, 0), (1, 1)),
    "keep": ((0, 0), (0, 1)),
}


def _weight_copies(names, meta_ref, w_ref, out_refs, sems):
    half = w_ref.shape[0] // (2 * N_FAST_HEAD)
    copies = []
    for n, name in enumerate(names):
        for i, (flip, side) in enumerate(QUARTERS[name]):
            row = (meta_ref[1] ^ flip) * (2 * half) + side * half
            copies.append(pltpu.make_async_copy(
                w_ref.at[_rows(row, half)], out_refs[n].at[pl.ds(i * half, half)], sems.at[2 * n + i]))
    return copies


def _quarter(out_weight):
    return jax.ShapeDtypeStruct((out_weight.shape[0] // N_FAST_HEAD, out_weight.shape[1]), out_weight.dtype)


def _stage_kernel(names, meta_ref, w_ref, *rest):
    copies = _weight_copies(names, meta_ref, w_ref, rest[:-1], rest[-1])
    for copy in copies:
        copy.start()
    for copy in copies:
        copy.wait()


def _stage_weights(names, meta, out_weight, room):
    return pl.pallas_call(
        functools.partial(_stage_kernel, names),
        out_shape=[_quarter(out_weight) for _ in names],
        in_specs=[SMEM, HBM],
        out_specs=[VMEM] * len(names),
        scratch_shapes=[pltpu.SemaphoreType.DMA((2 * len(names),))],
        compiler_params=pltpu.CompilerParams(vmem_limit_bytes=room * 2**20),
        cost_estimate=pl.CostEstimate(flops=1, bytes_accessed=1, transcendentals=0),
        name="stage_weights",
    )(meta, out_weight)


def _attend_kernel(
    groups, names, meta_ref, queries_ref, other_ref,
    kv0_ref, kv1_ref, kv2_ref, kv3_ref, w_ref,
    *rest,
):
    count = len(groups)
    out_refs, w_out = rest[:count], rest[count:count + len(names)]
    kbuf, vbuf, qbuf, ctxbuf, w_sems = rest[count + len(names):]
    w_copies = _weight_copies(names, meta_ref, w_ref, w_out, w_sems)
    for copy in w_copies:
        copy.start()
    c = meta_ref[0]
    core = lax.rem(c, 2)
    z = lax.div(c, 2)
    rows = kv0_ref.shape[0] // 2
    piece_rows = rows // PIECES
    tile = 128
    heads = kv0_ref.shape[1] // HEAD_SIZE
    slots = (2 + core, 3 - core, core, 1 - core)
    for b, kv_ref in enumerate((kv0_ref, kv1_ref, kv2_ref, kv3_ref)):
        at = _rows(slots[b] * rows, rows)
        kbuf[at] = kv_ref[:rows]
        for kv in range(heads):
            vbuf[at, 2 * kv * HEAD_SIZE:(2 * kv + 1) * HEAD_SIZE] = (
                kv_ref[rows:, kv * HEAD_SIZE:(kv + 1) * HEAD_SIZE])
            vbuf[at, (2 * kv + 1) * HEAD_SIZE:(2 * kv + 2) * HEAD_SIZE] = jnp.ones((rows, HEAD_SIZE), jnp.bfloat16)
    starts = []
    for n, k in enumerate(groups):
        zdest = z ^ k
        owner = 2 * zdest + core
        mine = _find_piece(meta_ref, c, owner)
        theirs = _find_piece(meta_ref, c + 1 - 2 * core, owner)
        qbuf[2 * n + core] = queries_ref[_rows(mine * piece_rows, piece_rows)]
        qbuf[2 * n + 1 - core] = other_ref[_rows(zdest * piece_rows, piece_rows)]
        at0 = jnp.where(core == 0, mine, theirs)
        at1 = jnp.where(core == 0, theirs, mine)
        starts.append((at0 * piece_rows, rows + at1 * piece_rows))
    doc_start = []
    running = jnp.int32(0)
    lengths_at = OWNERS_AT + PIECES * PIECES
    for d in range(lengths_at, meta_ref.shape[0]):
        doc_start.append(running)
        running = running + meta_ref[d]
    base = 2 * rows * (z - 1)
    group = queries_ref.shape[1] // kv0_ref.shape[1]
    scale = math.log2(math.e) / math.sqrt(HEAD_SIZE)
    span = 5 * tile

    def piece_keys(p0):
        first = pl.multiple_of(lax.div(p0, tile) * tile + 2 * rows - 4 * tile, tile)
        pos = 2 * rows * z + p0 + lax.broadcasted_iota(jnp.int32, (piece_rows, 1), 0)
        low = jnp.zeros((piece_rows, 1), jnp.int32)
        for start in doc_start:
            low = jnp.where(pos >= start, start, low)
        key_pos = base + first + lax.broadcasted_iota(jnp.int32, (piece_rows, span), 1)
        return first, (key_pos >= low) & (key_pos <= pos)

    def some_pieces(pieces):
        units, scores, weights = [], [], []
        for n, p0 in pieces:
            first, allowed = piece_keys(p0)
            units += [(n, kv, first, allowed) for kv in range(heads)]
        for n, kv, first, allowed in units:
            q = jnp.concatenate(
                [qbuf[n, :, pl.ds((kv * group + g) * HEAD_SIZE, HEAD_SIZE)] for g in range(group)], axis=0)
            k = kbuf[pl.ds(first, span), pl.ds(kv * HEAD_SIZE, HEAD_SIZE)]
            scores.append(lax.dot_general(q, k, (((1,), (1,)), ((), ())), preferred_element_type=jnp.float32))
        for (n, kv, first, allowed), s in zip(units, scores):
            s = jnp.where(allowed[None], s.reshape(group, piece_rows, span), MASKED)
            w = jnp.exp2((s - jnp.max(s, axis=2, keepdims=True)) * scale)
            weights.append(w.astype(jnp.bfloat16).reshape(group * piece_rows, span))
        for (n, kv, first, allowed), w in zip(units, weights):
            o = jnp.dot(w, vbuf[pl.ds(first, span), pl.ds(kv * 2 * HEAD_SIZE, 2 * HEAD_SIZE)],
                        preferred_element_type=jnp.float32)
            o = (o[:, :HEAD_SIZE] / o[:, HEAD_SIZE:]).astype(jnp.bfloat16)
            for g in range(group):
                ctxbuf[n, :, pl.ds((kv * group + g) * HEAD_SIZE, HEAD_SIZE)] = o[g * piece_rows:(g + 1) * piece_rows]

    together = 2

    def step(i, carry):
        pieces = []
        for j in range(together):
            n = i * together + j
            p0 = starts[0][0]
            for m in range(1, 2 * count):
                p0 = jnp.where(n == m, starts[m // 2][m % 2], p0)
            pieces.append((n, p0))
        some_pieces(pieces)
        return carry

    lax.fori_loop(0, 2 * count // together, step, 0)
    for n, out_ref in enumerate(out_refs):
        out_ref[...] = ctxbuf[2 * n:2 * n + 2].reshape(out_ref.shape)
    for copy in w_copies:
        copy.wait()


def _attend_groups(groups, names, meta, queries, other, kv, out_weight):
    piece = queries.shape[0] // PIECES
    rows = kv[0].shape[0] // 2
    return pl.pallas_call(
        functools.partial(_attend_kernel, groups, names),
        out_shape=[jax.ShapeDtypeStruct((2 * piece, queries.shape[1]), jnp.bfloat16) for _ in groups]
        + [_quarter(out_weight) for _ in names],
        in_specs=[SMEM] + [VMEM] * 6 + [HBM],
        out_specs=[VMEM] * (len(groups) + len(names)),
        scratch_shapes=[
            pltpu.VMEM((4 * rows, kv[0].shape[1]), jnp.bfloat16),
            pltpu.VMEM((4 * rows, 2 * kv[0].shape[1]), jnp.bfloat16),
            pltpu.VMEM((2 * len(groups), piece, queries.shape[1]), jnp.bfloat16),
            pltpu.VMEM((2 * len(groups), piece, queries.shape[1]), jnp.bfloat16),
            pltpu.SemaphoreType.DMA((2 * len(names),)),
        ],
        compiler_params=pltpu.CompilerParams(vmem_limit_bytes=12 * 2**20),
        cost_estimate=pl.CostEstimate(flops=1, bytes_accessed=1, transcendentals=0),
        name="attend_groups",
    )(meta, queries, other, *kv, out_weight)


def _dot_to(out_ref, weight_ref, tokens):
    out_ref[...] = jnp.dot(weight_ref[...], tokens, preferred_element_type=jnp.float32).astype(out_ref.dtype)


def _leaving_rows_kernel(meta_ref, a_ref, b_ref, wx_ref, wy_ref, x_ref, y_ref, joined_ref, catbuf):
    second = lax.rem(lax.div(meta_ref[0], 2), 2)
    mid = a_ref.shape[0]
    catbuf[_rows(second * mid, mid)] = a_ref[...]
    catbuf[_rows((1 - second) * mid, mid)] = b_ref[...]
    joined = catbuf[...].T
    joined_ref[...] = joined
    _dot_to(x_ref, wx_ref, joined)
    _dot_to(y_ref, wy_ref, joined)


def _pass_rows_kernel(joined_ref, w_ref, out_ref):
    _dot_to(out_ref, w_ref, joined_ref[...])


def _keep_rows_kernel(near_ref, far_ref, w_ref, near_out, far_out):
    tokens = near_ref.shape[1]
    both = jnp.concatenate([near_ref[...], far_ref[...]], axis=1)
    out = jnp.dot(w_ref[...], both, preferred_element_type=jnp.float32).astype(near_out.dtype)
    near_out[...] = out[:, :tokens]
    far_out[...] = out[:, tokens:]


def _leaving_rows(meta, a, b, w_x, w_y):
    (rows, depth), tokens = w_x.shape, a.shape[0] + b.shape[0]
    part = jax.ShapeDtypeStruct((rows, tokens), jnp.bfloat16)
    return pl.pallas_call(
        _leaving_rows_kernel,
        out_shape=[part, part, jax.ShapeDtypeStruct((depth, tokens), jnp.bfloat16)],
        in_specs=[SMEM] + [VMEM] * 4,
        out_specs=[VMEM] * 3,
        scratch_shapes=[pltpu.VMEM((tokens, depth), jnp.bfloat16)],
        compiler_params=pltpu.CompilerParams(vmem_limit_bytes=8 * 2**20),
        cost_estimate=pl.CostEstimate(flops=1, bytes_accessed=1, transcendentals=0),
        name="leaving_rows",
    )(meta, a, b, w_x, w_y)


def _pass_rows(joined, weight):
    return pl.pallas_call(
        _pass_rows_kernel,
        out_shape=jax.ShapeDtypeStruct((weight.shape[0], joined.shape[1]), jnp.bfloat16),
        in_specs=[VMEM] * 2,
        out_specs=VMEM,
        compiler_params=pltpu.CompilerParams(vmem_limit_bytes=8 * 2**20),
        cost_estimate=pl.CostEstimate(flops=1, bytes_accessed=1, transcendentals=0),
        name="pass_rows",
    )(joined, weight)


def _keep_rows(near, far, weight):
    part = jax.ShapeDtypeStruct((weight.shape[0], near.shape[1]), jnp.bfloat16)
    return pl.pallas_call(
        _keep_rows_kernel,
        out_shape=[part, part],
        in_specs=[VMEM] * 3,
        out_specs=[VMEM] * 2,
        compiler_params=pltpu.CompilerParams(vmem_limit_bytes=8 * 2**20),
        cost_estimate=pl.CostEstimate(flops=1, bytes_accessed=1, transcendentals=0),
        name="keep_rows",
    )(near, far, weight)


def _add_halves_kernel(a_half, b_half, a_ref, b_ref, out_ref):
    rows = out_ref.shape[0]
    a = a_ref[a_half * rows:(a_half + 1) * rows].astype(jnp.float32)
    b = b_ref[b_half * rows:(b_half + 1) * rows].astype(jnp.float32)
    out_ref[...] = (a + b).astype(out_ref.dtype)


def _add_halves(a, a_half, b, b_half):
    rows, tokens = a.shape[0] // 2, a.shape[1]
    return pl.pallas_call(
        functools.partial(_add_halves_kernel, a_half, b_half),
        out_shape=jax.ShapeDtypeStruct((rows, tokens), jnp.bfloat16),
        in_specs=[VMEM] * 2,
        out_specs=VMEM,
        compiler_params=pltpu.CompilerParams(vmem_limit_bytes=2 * 2**20),
        cost_estimate=pl.CostEstimate(flops=1, bytes_accessed=1, transcendentals=0),
        name="add_halves",
    )(a, b)


def _sum_parts(keep_ref, x1_ref, y1_ref, y2_ref, x2_ref):
    half = y2_ref.shape[0]
    f32 = jnp.float32
    first = keep_ref[:half].astype(f32) + x1_ref[:half].astype(f32) + y2_ref[...].astype(f32)
    second = keep_ref[half:].astype(f32) + y1_ref[:half].astype(f32) + x2_ref[...].astype(f32)
    return first, second


def _own_half(meta_ref, rows, tokens):
    lane = lax.broadcasted_iota(jnp.int32, (rows, tokens), 1)
    return lax.div(lane, tokens // 2) == lax.rem(lax.div(meta_ref[0], 2), 2)


def _finish_first_kernel(meta_ref, keep_ref, x1_ref, y1_ref, y2_ref, x2_ref, out_ref, away_ref):
    half, tokens = y2_ref.shape
    top, bottom = _sum_parts(keep_ref, x1_ref, y1_ref, y2_ref, x2_ref)
    out_ref[:half] = top.astype(out_ref.dtype)
    out_ref[half:] = bottom.astype(out_ref.dtype)
    own = _own_half(meta_ref, half, tokens)
    away_ref[...] = jnp.where(own, pltpu.roll(bottom, tokens // 2, 1), top).astype(away_ref.dtype)


def _finish_second_kernel(meta_ref, first_ref, away_ref, keep_ref, x1_ref, y1_ref, y2_ref, x2_ref, out_ref):
    half, tokens = y2_ref.shape
    upper = lax.div(meta_ref[0], 4)
    own = _own_half(meta_ref, half, tokens)
    mine, others = _rows(upper * tokens, tokens), _rows((1 - upper) * tokens, tokens)
    away = away_ref[...].astype(jnp.float32)
    sums = _sum_parts(keep_ref, x1_ref, y1_ref, y2_ref, x2_ref)
    arrived = (pltpu.roll(away, tokens // 2, 1), away)
    for i in range(2):
        at = pl.ds(i * half, half)
        first = first_ref[at].astype(jnp.float32)
        out_ref[at, mine] = jnp.where(own, first, pltpu.roll(sums[i], tokens // 2, 1)).astype(out_ref.dtype)
        out_ref[at, others] = jnp.where(own, arrived[i], sums[i]).astype(out_ref.dtype)


def _finish(kernel, out_shape, operands):
    return pl.pallas_call(
        kernel,
        out_shape=out_shape,
        in_specs=[SMEM] + [VMEM] * (len(operands) - 1),
        out_specs=jax.tree.map(lambda _: VMEM, out_shape),
        compiler_params=pltpu.CompilerParams(vmem_limit_bytes=8 * 2**20),
        cost_estimate=pl.CostEstimate(flops=1, bytes_accessed=1, transcendentals=0),
        name="finish",
    )(*operands)


def _flip(x, axis, bits):
    n = lax.axis_size(axis)
    return lax.ppermute(x, axis, [(i, i ^ bits) for i in range(n)])


def per_device_fast(queries, keys, values, out_weight, doc_lengths, owners):
    places = lax.axis_size("ctx")
    queries, keys, values, out_weight = (
        pltpu.with_memory_space_constraint(x, pltpu.HBM) for x in (queries, keys, values, out_weight))
    kv0 = _join_keys_values(keys, values)
    kv2 = lax.ppermute(kv0, "ctx", [(i, i + 2) for i in range(places - 2)])
    kv1 = _flip(kv0, "ctx", 1)
    meta = jnp.concatenate([
        lax.axis_index("ctx").reshape(1), lax.axis_index("head").reshape(1), owners.reshape(-1), doc_lengths,
    ]).astype(jnp.int32)
    leaving, queries = _queries_for_other_core(meta, queries)
    other = _flip(leaving, "ctx", 1)
    (w_x,) = _stage_weights(("x",), meta, out_weight, 8)
    kv2, w_x = lax.optimization_barrier((kv2, w_x))
    kv = (kv0, kv1, kv2, _flip(kv2, "ctx", 1))
    ctx0, ctx2, ctx1, ctx3, w_y, w_pass = _attend_groups(
        (0, 2, 1, 3), ("y", "pass"), meta, queries, other, kv, out_weight)
    ctx1, ctx3 = _flip(ctx1, "ctx", 2), _flip(ctx3, "ctx", 6)

    xmsg, ymsg, joined = _leaving_rows(meta, ctx0, ctx2, w_x, w_y)
    x1, y1 = _flip(xmsg, "head", 1), _flip(ymsg, "head", 2)
    pass_on = _pass_rows(joined, w_pass)
    pass_on, keep_meta = lax.optimization_barrier((pass_on, meta))
    (w_keep,) = _stage_weights(("keep",), keep_meta, out_weight, 8)
    pass_on, w_keep = lax.optimization_barrier((pass_on, w_keep))
    ymsg, xmsg = _add_halves(pass_on, 0, x1, 1), _add_halves(pass_on, 1, y1, 1)
    meta, ymsg, xmsg = lax.optimization_barrier((meta, ymsg, xmsg))
    y2, x2 = _flip(ymsg, "head", 2), _flip(xmsg, "head", 1)

    xmsg, ymsg, joined2 = _leaving_rows(meta, ctx1, ctx3, w_x, w_y)
    xmsg, ymsg, y2, x2 = lax.optimization_barrier((xmsg, ymsg, y2, x2))
    next_x1, next_y1 = _flip(xmsg, "head", 1), _flip(ymsg, "head", 2)
    keep, next_keep = _keep_rows(joined, joined2, w_keep)
    rows, tokens = keep.shape
    first, away = _finish(_finish_first_kernel, [
        jax.ShapeDtypeStruct((rows, tokens), jnp.bfloat16),
        jax.ShapeDtypeStruct((rows // 2, tokens), jnp.bfloat16),
    ], (meta, keep, x1, y1, y2, x2))
    joined2, away_sent = lax.optimization_barrier((joined2, away))
    pass_on = _pass_rows(joined2, w_pass)
    ymsg, xmsg = _add_halves(pass_on, 0, next_x1, 1), _add_halves(pass_on, 1, next_y1, 1)
    away = _flip(away_sent, "ctx", 4)
    y2, x2 = _flip(ymsg, "head", 2), _flip(xmsg, "head", 1)
    return _finish(_finish_second_kernel, jax.ShapeDtypeStruct((rows, 2 * tokens), jnp.bfloat16),
                   (meta, first, away, next_keep, next_x1, next_y1, y2, x2))


def solution(mesh):
    in_specs = (P("ctx", "head"), P("ctx", "head"), P("ctx", "head"), P(None, "head"), P(), P())
    out_specs = P("head", "ctx")
    fast = mesh.shape["ctx"] == PIECES and mesh.shape["head"] == N_FAST_HEAD
    return jax.shard_map(
        per_device_fast if fast else per_device, mesh=mesh, in_specs=in_specs, out_specs=out_specs, check_vma=False
    )
```

```python
import functools
import math

import jax
import jax.numpy as jnp
from jax import lax
from jax.experimental import pallas as pl
from jax.experimental.pallas import tpu as pltpu
from jax.sharding import PartitionSpec as P

HEAD_SIZE = 128
PIECES = 8
N_FAST_HEAD = 4


MASKED = -1e30


def document_index(positions, doc_starts):
    return jnp.sum((positions[:, None] >= doc_starts[None, :]).astype(jnp.int32), axis=1) - 1


def attend(query_rows, query_pos, keys, values, doc_starts):
    row_count = query_rows.shape[0]
    key_heads = keys.shape[1] // HEAD_SIZE
    group_length = query_rows.shape[1] // keys.shape[1]
    query_heads = query_rows.reshape(row_count, key_heads, group_length, HEAD_SIZE)
    query_doc = document_index(query_pos, doc_starts)
    score_scale = 1.0 / math.sqrt(HEAD_SIZE)
    initial = (
        jnp.full((row_count, key_heads, group_length), MASKED, jnp.float32),
        jnp.zeros((row_count, key_heads, group_length), jnp.float32),
        jnp.zeros((row_count, key_heads, group_length, HEAD_SIZE), jnp.float32),
    )
    key_piece = lax.all_gather(keys, "ctx", axis=0, tiled=True)
    value_piece = lax.all_gather(values, "ctx", axis=0, tiled=True)
    piece_rows = key_piece.shape[0]
    tile_rows = math.gcd(piece_rows, 512)

    def one_tile(tile_index, running):
        tile_start = tile_index * tile_rows
        key_block = lax.dynamic_slice_in_dim(key_piece, tile_start, tile_rows, 0).reshape(
            tile_rows, key_heads, HEAD_SIZE
        )
        value_block = lax.dynamic_slice_in_dim(value_piece, tile_start, tile_rows, 0).reshape(
            tile_rows, key_heads, HEAD_SIZE
        )
        key_pos = tile_start + jnp.arange(tile_rows, dtype=jnp.int32)
        key_doc = document_index(key_pos, doc_starts)
        allowed = (query_doc[:, None] == key_doc[None, :]) & (
            key_pos[None, :] <= query_pos[:, None]
        )
        running_max, running_sum, weighted = running
        scores = (
            jnp.einsum("rkgd,nkd->rkgn", query_heads, key_block, preferred_element_type=jnp.float32)
            * score_scale
        )
        allowed_all = allowed[:, None, None, :]
        scores = jnp.where(allowed_all, scores, MASKED)
        new_max = jnp.maximum(running_max, jnp.max(scores, axis=-1))
        factor = jnp.exp(running_max - new_max)
        weights = jnp.where(allowed_all, jnp.exp(scores - new_max[..., None]), 0.0)
        new_sum = running_sum * factor + jnp.sum(weights, axis=-1)
        new_weighted = weighted * factor[..., None] + jnp.einsum(
            "rkgn,nkd->rkgd",
            weights.astype(jnp.bfloat16),
            value_block,
            preferred_element_type=jnp.float32,
        )
        return (new_max, new_sum, new_weighted)

    final_max, final_sum, weighted = lax.fori_loop(0, piece_rows // tile_rows, one_tile, initial)
    result = weighted / jnp.maximum(final_sum, 1.0)[..., None]
    return result.reshape(row_count, key_heads * group_length * HEAD_SIZE).astype(jnp.bfloat16)


def project(context, out_weight):
    return lax.psum_scatter(
        lax.dot_general(
            out_weight, context, (((1,), (1,)), ((), ())), preferred_element_type=jnp.float32
        ).astype(jnp.bfloat16),
        "head",
        scatter_dimension=0,
        tiled=True,
    )


def per_device(queries, keys, values, out_weight, doc_lengths, owners):
    place_count = lax.axis_size("ctx")
    own_index = lax.axis_index("ctx")
    token_count = queries.shape[0]
    block_rows = token_count // PIECES
    doc_ends = jnp.cumsum(doc_lengths)
    doc_starts = doc_ends - doc_lengths
    owner_table = owners[:, 0].reshape(place_count, PIECES)
    own_owners = lax.dynamic_index_in_dim(owner_table, own_index, 0, keepdims=False)
    place_ids = jnp.arange(place_count, dtype=jnp.int32)
    send_pick = (own_owners[None, :] == place_ids[:, None]).astype(jnp.bfloat16)
    grouped = queries.reshape(PIECES, block_rows, queries.shape[1])
    outgoing = jnp.einsum(
        "oc,chw->ohw", send_pick, grouped, preferred_element_type=jnp.float32
    ).astype(jnp.bfloat16)
    arrived = lax.all_to_all(outgoing, "ctx", split_axis=0, concat_axis=0, tiled=True)
    slot_hits = (owner_table == own_index).astype(jnp.int32)
    slot_live = jnp.sum(slot_hits, axis=1)
    picked = jnp.sum(slot_hits * jnp.arange(PIECES, dtype=jnp.int32)[None, :], axis=1)
    slot_pos = (place_ids[:, None] * PIECES + picked[:, None]) * block_rows + jnp.arange(
        block_rows, dtype=jnp.int32
    )[None, :]
    query_pos = jnp.where(slot_live[:, None] > 0, slot_pos, -1).reshape(-1)
    context = attend(
        arrived.reshape(place_count * block_rows, queries.shape[1]),
        query_pos,
        keys,
        values,
        doc_starts,
    )
    return project(context, out_weight)


SMEM = pl.BlockSpec(memory_space=pltpu.SMEM)
VMEM = pl.BlockSpec(memory_space=pltpu.VMEM)
HBM = pl.BlockSpec(memory_space=pltpu.HBM)


OWNERS_AT = 2


def _find_piece(table_ref, source, owner):
    piece = jnp.int32(0)
    for i in range(PIECES):
        piece = jnp.where(table_ref[OWNERS_AT + source * PIECES + i] == owner, jnp.int32(i), piece)
    return piece


def _rows(start, size):
    return pl.ds(pl.multiple_of(start, size), size)


def _join_keys_values_kernel(keys_ref, values_ref, out_ref, sems):
    rows = keys_ref.shape[0]
    copies = [
        pltpu.make_async_copy(keys_ref, out_ref.at[pl.ds(0, rows)], sems.at[0]),
        pltpu.make_async_copy(values_ref, out_ref.at[pl.ds(rows, rows)], sems.at[1]),
    ]
    for copy in copies:
        copy.start()
    for copy in copies:
        copy.wait()


def _join_keys_values(keys, values):
    return pl.pallas_call(
        _join_keys_values_kernel,
        out_shape=jax.ShapeDtypeStruct((2 * keys.shape[0], keys.shape[1]), keys.dtype),
        in_specs=[HBM] * 2,
        out_specs=VMEM,
        scratch_shapes=[pltpu.SemaphoreType.DMA((2,))],
        compiler_params=pltpu.CompilerParams(vmem_limit_bytes=2 * 2**20),
        cost_estimate=pl.CostEstimate(flops=1, bytes_accessed=1, transcendentals=0),
        name="join_keys_values",
    )(keys, values)


def _queries_for_other_core_kernel(names, meta_ref, queries_ref, w_ref, out_ref, kept_ref, *rest):
    *w_out, sem, w_sems = rest
    w_copies = _weight_copies(names, meta_ref, w_ref, w_out, w_sems)
    copy = pltpu.make_async_copy(queries_ref, kept_ref, sem)
    copy.start()
    for w_copy in w_copies:
        w_copy.start()
    copy.wait()
    c = meta_ref[0]
    core = lax.rem(c, 2)
    rows = queries_ref.shape[0] // PIECES
    for j in range(PIECES // 2):
        piece = _find_piece(meta_ref, c, 2 * j + 1 - core)
        out_ref[j * rows:(j + 1) * rows] = kept_ref[_rows(piece * rows, rows)]
    for w_copy in w_copies:
        w_copy.wait()


def _queries_for_other_core(names, meta, queries, out_weight):
    return pl.pallas_call(
        functools.partial(_queries_for_other_core_kernel, names),
        out_shape=[
            jax.ShapeDtypeStruct((queries.shape[0] // 2, queries.shape[1]), queries.dtype),
            jax.ShapeDtypeStruct(queries.shape, queries.dtype),
        ] + [_eighth(out_weight) for _ in names],
        in_specs=[SMEM, HBM, HBM],
        out_specs=[VMEM] * (2 + len(names)),
        scratch_shapes=[pltpu.SemaphoreType.DMA, pltpu.SemaphoreType.DMA((len(names),))],
        compiler_params=pltpu.CompilerParams(vmem_limit_bytes=2 * 2**20),
        cost_estimate=pl.CostEstimate(flops=1, bytes_accessed=1, transcendentals=0),
        name="queries_for_other_core",
    )(meta, queries, out_weight)


EIGHTHS = {
    "xf": (1, 0), "xp": (3, 0), "yf": (2, 1), "yp": (3, 1), "py": (2, 0), "px": (1, 1), "k0": (0, 0), "k1": (0, 1),
}


def _weight_copies(names, meta_ref, w_ref, out_refs, sems):
    half = w_ref.shape[0] // (2 * N_FAST_HEAD)
    copies = []
    for n, name in enumerate(names):
        flip, side = EIGHTHS[name]
        row = (meta_ref[1] ^ flip) * (2 * half) + side * half
        copies.append(pltpu.make_async_copy(w_ref.at[_rows(row, half)], out_refs[n], sems.at[n]))
    return copies


def _eighth(out_weight):
    return jax.ShapeDtypeStruct((out_weight.shape[0] // (2 * N_FAST_HEAD), out_weight.shape[1]), out_weight.dtype)


def _stage_kernel(names, meta_ref, w_ref, *rest):
    copies = _weight_copies(names, meta_ref, w_ref, rest[:-1], rest[-1])
    for copy in copies:
        copy.start()
    for copy in copies:
        copy.wait()


def _stage_weights(names, meta, out_weight):
    return pl.pallas_call(
        functools.partial(_stage_kernel, names),
        out_shape=[_eighth(out_weight) for _ in names],
        in_specs=[SMEM, HBM],
        out_specs=[VMEM] * len(names),
        scratch_shapes=[pltpu.SemaphoreType.DMA((len(names),))],
        compiler_params=pltpu.CompilerParams(vmem_limit_bytes=8 * 2**20),
        cost_estimate=pl.CostEstimate(flops=1, bytes_accessed=1, transcendentals=0),
        name="stage_weights",
    )(meta, out_weight)


def _attend_kernel(
    groups, names, meta_ref, queries_ref, other_ref,
    kv0_ref, kv1_ref, kv2_ref, kv3_ref, w_ref,
    *rest,
):
    count = len(groups)
    out_refs, w_out = rest[:count], rest[count:count + len(names)]
    kbuf, vbuf, qbuf, ctxbuf, w_sems = rest[count + len(names):]
    w_copies = _weight_copies(names, meta_ref, w_ref, w_out, w_sems)
    for copy in w_copies:
        copy.start()
    c = meta_ref[0]
    core = lax.rem(c, 2)
    z = lax.div(c, 2)
    rows = kv0_ref.shape[0] // 2
    piece_rows = rows // PIECES
    tile = 128
    heads = kv0_ref.shape[1] // HEAD_SIZE
    slots = (2 + core, 3 - core, core, 1 - core)
    for b, kv_ref in enumerate((kv0_ref, kv1_ref, kv2_ref, kv3_ref)):
        at = _rows(slots[b] * rows, rows)
        kbuf[at] = kv_ref[:rows]
        for kv in range(heads):
            vbuf[at, 2 * kv * HEAD_SIZE:(2 * kv + 1) * HEAD_SIZE] = (
                kv_ref[rows:, kv * HEAD_SIZE:(kv + 1) * HEAD_SIZE])
            vbuf[at, (2 * kv + 1) * HEAD_SIZE:(2 * kv + 2) * HEAD_SIZE] = jnp.ones((rows, HEAD_SIZE), jnp.bfloat16)
    starts = []
    for n, k in enumerate(groups):
        zdest = z ^ k
        owner = 2 * zdest + core
        mine = _find_piece(meta_ref, c, owner)
        theirs = _find_piece(meta_ref, c + 1 - 2 * core, owner)
        qbuf[2 * n + core] = queries_ref[_rows(mine * piece_rows, piece_rows)]
        qbuf[2 * n + 1 - core] = other_ref[_rows(zdest * piece_rows, piece_rows)]
        at0 = jnp.where(core == 0, mine, theirs)
        at1 = jnp.where(core == 0, theirs, mine)
        starts.append((at0 * piece_rows, rows + at1 * piece_rows))
    doc_start = []
    running = jnp.int32(0)
    lengths_at = OWNERS_AT + PIECES * PIECES
    for d in range(lengths_at, meta_ref.shape[0]):
        doc_start.append(running)
        running = running + meta_ref[d]
    base = 2 * rows * (z - 1)
    group = queries_ref.shape[1] // kv0_ref.shape[1]
    scale = math.log2(math.e) / math.sqrt(HEAD_SIZE)

    def tiles_needed(p0):
        low = jnp.int32(0)
        for start in doc_start:
            low = jnp.where(2 * rows * z + p0 >= start, start, low)
        return lax.div(2 * rows * z + p0, tile) - lax.div(low, tile) + 1

    def piece_keys(p0, span):
        first = pl.multiple_of(lax.div(p0, tile) * tile + 2 * rows + tile - span, tile)
        pos = 2 * rows * z + p0 + lax.broadcasted_iota(jnp.int32, (piece_rows, 1), 0)
        low = jnp.zeros((piece_rows, 1), jnp.int32)
        for start in doc_start:
            low = jnp.where(pos >= start, start, low)
        key_pos = base + first + lax.broadcasted_iota(jnp.int32, (piece_rows, span), 1)
        return first, (key_pos >= low) & (key_pos <= pos)

    def some_pieces(pieces, span):
        units, scores, weights = [], [], []
        for n, p0 in pieces:
            first, allowed = piece_keys(p0, span)
            units += [(n, kv, first, allowed) for kv in range(heads)]
        for n, kv, first, allowed in units:
            q = jnp.concatenate(
                [qbuf[n, :, pl.ds((kv * group + g) * HEAD_SIZE, HEAD_SIZE)] for g in range(group)], axis=0)
            k = kbuf[pl.ds(first, span), pl.ds(kv * HEAD_SIZE, HEAD_SIZE)]
            scores.append(lax.dot_general(q, k, (((1,), (1,)), ((), ())), preferred_element_type=jnp.float32))
        for (n, kv, first, allowed), s in zip(units, scores):
            s = jnp.where(allowed[None], s.reshape(group, piece_rows, span), MASKED)
            w = jnp.exp2((s - jnp.max(s, axis=2, keepdims=True)) * scale)
            weights.append(w.astype(jnp.bfloat16).reshape(group * piece_rows, span))
        for (n, kv, first, allowed), w in zip(units, weights):
            o = jnp.dot(w, vbuf[pl.ds(first, span), pl.ds(kv * 2 * HEAD_SIZE, 2 * HEAD_SIZE)],
                        preferred_element_type=jnp.float32)
            o = (o[:, :HEAD_SIZE] / o[:, HEAD_SIZE:]).astype(jnp.bfloat16)
            for g in range(group):
                ctxbuf[n, :, pl.ds((kv * group + g) * HEAD_SIZE, HEAD_SIZE)] = o[g * piece_rows:(g + 1) * piece_rows]

    together = 2
    most_tiles = 5

    def step(i, carry):
        pieces = []
        for j in range(together):
            n = i * together + j
            p0 = starts[0][0]
            for m in range(1, 2 * count):
                p0 = jnp.where(n == m, starts[m // 2][m % 2], p0)
            pieces.append((n, p0))
        needed = functools.reduce(jnp.maximum, [tiles_needed(p0) for n, p0 in pieces])
        least = 0
        for tiles in (2, 3, most_tiles):
            fits = needed > least if tiles == most_tiles else (needed > least) & (needed <= tiles)
            pl.when(fits)(functools.partial(some_pieces, pieces, tiles * tile))
            least = tiles
        return carry

    lax.fori_loop(0, 2 * count // together, step, 0)
    for n, out_ref in enumerate(out_refs):
        out_ref[...] = ctxbuf[2 * n:2 * n + 2].reshape(out_ref.shape)
    for copy in w_copies:
        copy.wait()


def _attend_groups(groups, names, meta, queries, other, kv, out_weight):
    piece = queries.shape[0] // PIECES
    rows = kv[0].shape[0] // 2
    return pl.pallas_call(
        functools.partial(_attend_kernel, groups, names),
        out_shape=[jax.ShapeDtypeStruct((2 * piece, queries.shape[1]), jnp.bfloat16) for _ in groups]
        + [_eighth(out_weight) for _ in names],
        in_specs=[SMEM] + [VMEM] * 6 + [HBM],
        out_specs=[VMEM] * (len(groups) + len(names)),
        scratch_shapes=[
            pltpu.VMEM((4 * rows, kv[0].shape[1]), jnp.bfloat16),
            pltpu.VMEM((4 * rows, 2 * kv[0].shape[1]), jnp.bfloat16),
            pltpu.VMEM((2 * len(groups), piece, queries.shape[1]), jnp.bfloat16),
            pltpu.VMEM((2 * len(groups), piece, queries.shape[1]), jnp.bfloat16),
            pltpu.SemaphoreType.DMA((len(names),)),
        ],
        compiler_params=pltpu.CompilerParams(vmem_limit_bytes=12 * 2**20),
        cost_estimate=pl.CostEstimate(flops=1, bytes_accessed=1, transcendentals=0),
        name="attend_groups",
    )(meta, queries, other, *kv, out_weight)


def _dot_to(out_ref, weight_ref, tokens):
    out_ref[...] = jnp.dot(weight_ref[...], tokens, preferred_element_type=jnp.float32).astype(out_ref.dtype)


def _leaving_rows_kernel(meta_ref, a_ref, b_ref, *rest):
    w_refs, out_refs, (joined_ref, catbuf) = rest[:4], rest[4:8], rest[8:]
    second = lax.rem(lax.div(meta_ref[0], 2), 2)
    mid = a_ref.shape[0]
    catbuf[_rows(second * mid, mid)] = a_ref[...]
    catbuf[_rows((1 - second) * mid, mid)] = b_ref[...]
    joined = catbuf[...].T
    joined_ref[...] = joined
    for w_ref, out_ref in zip(w_refs, out_refs):
        _dot_to(out_ref, w_ref, joined)


def _pass_rows_kernel(joined_ref, w0_ref, w1_ref, out0_ref, out1_ref):
    joined = joined_ref[...]
    _dot_to(out0_ref, w0_ref, joined)
    _dot_to(out1_ref, w1_ref, joined)


def _keep_rows_kernel(first_ref, second_ref, w0_ref, w1_ref, first_out, second_out):
    half, tokens = w0_ref.shape[0], first_ref.shape[1]
    both = jnp.concatenate([first_ref[...], second_ref[...]], axis=1)
    for i, w_ref in enumerate((w0_ref, w1_ref)):
        out = jnp.dot(w_ref[...], both, preferred_element_type=jnp.float32).astype(first_out.dtype)
        first_out[i * half:(i + 1) * half] = out[:, :tokens]
        second_out[i * half:(i + 1) * half] = out[:, tokens:]


def _project(kernel, name, out_shape, operands, scratch=(), scalars=()):
    return pl.pallas_call(
        kernel,
        out_shape=out_shape,
        in_specs=[SMEM] * len(scalars) + [VMEM] * len(operands),
        out_specs=[VMEM] * len(out_shape),
        scratch_shapes=scratch,
        compiler_params=pltpu.CompilerParams(vmem_limit_bytes=8 * 2**20),
        cost_estimate=pl.CostEstimate(flops=1, bytes_accessed=1, transcendentals=0),
        name=name,
    )(*scalars, *operands)


def _leaving_rows(meta, a, b, weights):
    (rows, depth), tokens = weights["xf"].shape, a.shape[0] + b.shape[0]
    part = jax.ShapeDtypeStruct((rows, tokens), jnp.bfloat16)
    return _project(
        _leaving_rows_kernel, "leaving_rows", [part] * 4 + [jax.ShapeDtypeStruct((depth, tokens), jnp.bfloat16)],
        (a, b) + tuple(weights[name] for name in ("xf", "xp", "yf", "yp")),
        [pltpu.VMEM((tokens, depth), jnp.bfloat16)], (meta,))


def _pass_rows(joined, weights):
    part = jax.ShapeDtypeStruct((weights["py"].shape[0], joined.shape[1]), jnp.bfloat16)
    return _project(_pass_rows_kernel, "pass_rows", [part] * 2, (joined, weights["py"], weights["px"]))


def _keep_rows(first, second, weights):
    part = jax.ShapeDtypeStruct((2 * weights["k0"].shape[0], first.shape[1]), jnp.bfloat16)
    return _project(_keep_rows_kernel, "keep_rows", [part] * 2, (first, second, weights["k0"], weights["k1"]))


def _add_kernel(a_ref, b_ref, out_ref):
    out_ref[...] = (a_ref[...].astype(jnp.float32) + b_ref[...].astype(jnp.float32)).astype(out_ref.dtype)


def _add(a, b):
    return _project(_add_kernel, "add", [jax.ShapeDtypeStruct(a.shape, jnp.bfloat16)], (a, b))[0]


def _sum_parts(keep_ref, x1_ref, y1_ref, y2_ref, x2_ref):
    half = y2_ref.shape[0]
    f32 = jnp.float32
    first = keep_ref[:half].astype(f32) + x1_ref[...].astype(f32) + y2_ref[...].astype(f32)
    second = keep_ref[half:].astype(f32) + y1_ref[...].astype(f32) + x2_ref[...].astype(f32)
    return first, second


def _own_half(meta_ref, rows, tokens):
    lane = lax.broadcasted_iota(jnp.int32, (rows, tokens), 1)
    return lax.div(lane, tokens // 2) == lax.rem(lax.div(meta_ref[0], 2), 2)


def _finish_first_kernel(meta_ref, keep_ref, x1_ref, y1_ref, y2_ref, x2_ref, out_ref, away_ref):
    half, tokens = y2_ref.shape
    top, bottom = _sum_parts(keep_ref, x1_ref, y1_ref, y2_ref, x2_ref)
    out_ref[:half] = top.astype(out_ref.dtype)
    out_ref[half:] = bottom.astype(out_ref.dtype)
    own = _own_half(meta_ref, half, tokens)
    away_ref[...] = jnp.where(own, pltpu.roll(bottom, tokens // 2, 1), top).astype(away_ref.dtype)


def _unpack_kernel(meta_ref, away_ref, out_ref):
    half, tokens = away_ref.shape
    out_ref[:half] = pltpu.roll(away_ref[...].astype(jnp.float32), tokens // 2, 1).astype(out_ref.dtype)
    out_ref[half:] = away_ref[...]


def _sum_first_step_kernel(meta_ref, keep_ref, x1_ref, y1_ref, out_ref):
    half = x1_ref.shape[0]
    for i, one_ref in enumerate((x1_ref, y1_ref)):
        at = pl.ds(i * half, half)
        out_ref[at] = keep_ref[at].astype(jnp.float32) + one_ref[...].astype(jnp.float32)


def _finish_second_kernel(meta_ref, first_ref, away_ref, sum_ref, y2_ref, x2_ref, out_ref, rows_ref, sems):
    half, tokens = y2_ref.shape
    part = half // 2
    upper = lax.div(meta_ref[0], 4)
    mine, others = _rows(upper * tokens, tokens), _rows((1 - upper) * tokens, tokens)
    own = _own_half(meta_ref, part, tokens)
    copies = []
    for i in range(4):
        at, inside = pl.ds(i * part, part), pl.ds(i % 2 * part, part)
        two_ref = y2_ref if i < 2 else x2_ref
        sums = sum_ref[at] + two_ref[inside].astype(jnp.float32)
        first, away = first_ref[at].astype(jnp.float32), away_ref[at].astype(jnp.float32)
        rows_ref[at, mine] = jnp.where(own, first, pltpu.roll(sums, tokens // 2, 1)).astype(rows_ref.dtype)
        rows_ref[at, others] = jnp.where(own, away, sums).astype(rows_ref.dtype)
        copies.append(pltpu.make_async_copy(rows_ref.at[at], out_ref.at[at], sems.at[i]))
        copies[-1].start()
    for copy in copies:
        copy.wait()


def _finish_second(meta, first, away, summed, y2, x2):
    rows, tokens = summed.shape
    return pl.pallas_call(
        _finish_second_kernel,
        out_shape=jax.ShapeDtypeStruct((rows, 2 * tokens), jnp.bfloat16),
        in_specs=[SMEM] + [VMEM] * 5,
        out_specs=HBM,
        scratch_shapes=[pltpu.VMEM((rows, 2 * tokens), jnp.bfloat16), pltpu.SemaphoreType.DMA((4,))],
        compiler_params=pltpu.CompilerParams(vmem_limit_bytes=8 * 2**20),
        cost_estimate=pl.CostEstimate(flops=1, bytes_accessed=1, transcendentals=0),
        name="finish_second",
    )(meta, first, away, summed, y2, x2)


def _finish(kernel, out_shape, operands):
    return pl.pallas_call(
        kernel,
        out_shape=out_shape,
        in_specs=[SMEM] + [VMEM] * (len(operands) - 1),
        out_specs=jax.tree.map(lambda _: VMEM, out_shape),
        compiler_params=pltpu.CompilerParams(vmem_limit_bytes=8 * 2**20),
        cost_estimate=pl.CostEstimate(flops=1, bytes_accessed=1, transcendentals=0),
        name="finish",
    )(*operands)


def _flip(x, axis, bits):
    n = lax.axis_size(axis)
    return lax.ppermute(x, axis, [(i, i ^ bits) for i in range(n)])


def per_device_fast(queries, keys, values, out_weight, doc_lengths, owners):
    places = lax.axis_size("ctx")
    queries, keys, values, out_weight = (
        pltpu.with_memory_space_constraint(x, pltpu.HBM) for x in (queries, keys, values, out_weight))
    kv0 = _join_keys_values(keys, values)
    kv2 = lax.ppermute(kv0, "ctx", [(i, i + 2) for i in range(places - 2)])
    kv1 = _flip(kv0, "ctx", 1)
    meta = jnp.concatenate([
        lax.axis_index("ctx").reshape(1), lax.axis_index("head").reshape(1), owners.reshape(-1), doc_lengths,
    ]).astype(jnp.int32)
    weights = {}
    leaving, queries, weights["xp"] = _queries_for_other_core(("xp",), meta, queries, out_weight)
    other = _flip(leaving, "ctx", 1)
    weights["yp"], weights["xf"] = _stage_weights(("yp", "xf"), meta, out_weight)
    kv2, weights["xf"] = lax.optimization_barrier((kv2, weights["xf"]))
    kv = (kv0, kv1, kv2, _flip(kv2, "ctx", 1))
    loaded = ("yf", "py", "px")
    ctx0, ctx2, ctx1, ctx3, *loads = _attend_groups((0, 2, 1, 3), loaded, meta, queries, other, kv, out_weight)
    weights.update(zip(loaded, loads))
    ctx1, ctx3 = _flip(ctx1, "ctx", 2), _flip(ctx3, "ctx", 6)

    xf, xp, yf, yp, joined = _leaving_rows(meta, ctx0, ctx2, weights)
    x1f, x1p, y1f, y1p = _flip(xf, "head", 1), _flip(xp, "head", 1), _flip(yf, "head", 2), _flip(yp, "head", 2)
    later_meta, joined = lax.optimization_barrier((meta, joined))
    weights["k0"], weights["k1"] = _stage_weights(("k0", "k1"), later_meta, out_weight)
    joined, weights["k0"], ctx1, ctx3 = lax.optimization_barrier((joined, weights["k0"], ctx1, ctx3))
    y2, x2 = _pass_rows(joined, weights)
    y2, x2 = _add(y2, x1p), _add(x2, y1p)
    meta, y2, x2 = lax.optimization_barrier((meta, y2, x2))
    y2, x2 = _flip(y2, "head", 2), _flip(x2, "head", 1)

    xf, xp, yf, yp, joined2 = _leaving_rows(meta, ctx1, ctx3, weights)
    xf, xp, yf, yp, x1f, y1f = lax.optimization_barrier((xf, xp, yf, yp, x1f, y1f))
    next_x1f, next_x1p = _flip(xf, "head", 1), _flip(xp, "head", 1)
    next_y1f, next_y1p = _flip(yf, "head", 2), _flip(yp, "head", 2)
    keep, next_keep = _keep_rows(joined, joined2, weights)
    rows, tokens = keep.shape
    first, away = _finish(_finish_first_kernel, [
        jax.ShapeDtypeStruct((rows, tokens), jnp.bfloat16),
        jax.ShapeDtypeStruct((rows // 2, tokens), jnp.bfloat16),
    ], (meta, keep, x1f, y1f, y2, x2))
    joined2, away = lax.optimization_barrier((joined2, away))
    away = _flip(away, "ctx", 4)
    y2, x2 = _pass_rows(joined2, weights)
    y2, x2 = _add(y2, next_x1p), _add(x2, next_y1p)
    y2, x2 = _flip(y2, "head", 2), _flip(x2, "head", 1)
    away = _finish(_unpack_kernel, [jax.ShapeDtypeStruct((rows, tokens), jnp.bfloat16)], (meta, away))[0]
    away, next_keep = lax.optimization_barrier((away, next_keep))
    summed = _finish(_sum_first_step_kernel, [jax.ShapeDtypeStruct((rows, tokens), jnp.float32)],
                     (meta, next_keep, next_x1f, next_y1f))[0]
    return _finish_second(meta, first, away, summed, y2, x2)


def solution(mesh):
    in_specs = (P("ctx", "head"), P("ctx", "head"), P("ctx", "head"), P(None, "head"), P(), P())
    out_specs = P("head", "ctx")
    fast = mesh.shape["ctx"] == PIECES and mesh.shape["head"] == N_FAST_HEAD
    return jax.shard_map(
        per_device_fast if fast else per_device, mesh=mesh, in_specs=in_specs, out_specs=out_specs, check_vma=False
    )
```

```python
import functools
import math

import jax
import jax.numpy as jnp
from jax import lax
from jax.experimental import pallas as pl
from jax.experimental.pallas import tpu as pltpu
from jax.sharding import PartitionSpec as P

HEAD_SIZE = 128
PIECES = 8
N_FAST_HEAD = 4


MASKED = -1e30


def document_index(positions, doc_starts):
    return jnp.sum((positions[:, None] >= doc_starts[None, :]).astype(jnp.int32), axis=1) - 1


def attend(query_rows, query_pos, keys, values, doc_starts):
    row_count = query_rows.shape[0]
    key_heads = keys.shape[1] // HEAD_SIZE
    group_length = query_rows.shape[1] // keys.shape[1]
    query_heads = query_rows.reshape(row_count, key_heads, group_length, HEAD_SIZE)
    query_doc = document_index(query_pos, doc_starts)
    score_scale = 1.0 / math.sqrt(HEAD_SIZE)
    initial = (
        jnp.full((row_count, key_heads, group_length), MASKED, jnp.float32),
        jnp.zeros((row_count, key_heads, group_length), jnp.float32),
        jnp.zeros((row_count, key_heads, group_length, HEAD_SIZE), jnp.float32),
    )
    key_piece = lax.all_gather(keys, "ctx", axis=0, tiled=True)
    value_piece = lax.all_gather(values, "ctx", axis=0, tiled=True)
    piece_rows = key_piece.shape[0]
    tile_rows = math.gcd(piece_rows, 512)

    def one_tile(tile_index, running):
        tile_start = tile_index * tile_rows
        key_block = lax.dynamic_slice_in_dim(key_piece, tile_start, tile_rows, 0).reshape(
            tile_rows, key_heads, HEAD_SIZE
        )
        value_block = lax.dynamic_slice_in_dim(value_piece, tile_start, tile_rows, 0).reshape(
            tile_rows, key_heads, HEAD_SIZE
        )
        key_pos = tile_start + jnp.arange(tile_rows, dtype=jnp.int32)
        key_doc = document_index(key_pos, doc_starts)
        allowed = (query_doc[:, None] == key_doc[None, :]) & (
            key_pos[None, :] <= query_pos[:, None]
        )
        running_max, running_sum, weighted = running
        scores = (
            jnp.einsum("rkgd,nkd->rkgn", query_heads, key_block, preferred_element_type=jnp.float32)
            * score_scale
        )
        allowed_all = allowed[:, None, None, :]
        scores = jnp.where(allowed_all, scores, MASKED)
        new_max = jnp.maximum(running_max, jnp.max(scores, axis=-1))
        factor = jnp.exp(running_max - new_max)
        weights = jnp.where(allowed_all, jnp.exp(scores - new_max[..., None]), 0.0)
        new_sum = running_sum * factor + jnp.sum(weights, axis=-1)
        new_weighted = weighted * factor[..., None] + jnp.einsum(
            "rkgn,nkd->rkgd",
            weights.astype(jnp.bfloat16),
            value_block,
            preferred_element_type=jnp.float32,
        )
        return (new_max, new_sum, new_weighted)

    final_max, final_sum, weighted = lax.fori_loop(0, piece_rows // tile_rows, one_tile, initial)
    result = weighted / jnp.maximum(final_sum, 1.0)[..., None]
    return result.reshape(row_count, key_heads * group_length * HEAD_SIZE).astype(jnp.bfloat16)


def project(context, out_weight):
    return lax.psum_scatter(
        lax.dot_general(
            out_weight, context, (((1,), (1,)), ((), ())), preferred_element_type=jnp.float32
        ).astype(jnp.bfloat16),
        "head",
        scatter_dimension=0,
        tiled=True,
    )


def per_device(queries, keys, values, out_weight, doc_lengths, owners):
    place_count = lax.axis_size("ctx")
    own_index = lax.axis_index("ctx")
    token_count = queries.shape[0]
    block_rows = token_count // PIECES
    doc_ends = jnp.cumsum(doc_lengths)
    doc_starts = doc_ends - doc_lengths
    owner_table = owners[:, 0].reshape(place_count, PIECES)
    own_owners = lax.dynamic_index_in_dim(owner_table, own_index, 0, keepdims=False)
    place_ids = jnp.arange(place_count, dtype=jnp.int32)
    send_pick = (own_owners[None, :] == place_ids[:, None]).astype(jnp.bfloat16)
    grouped = queries.reshape(PIECES, block_rows, queries.shape[1])
    outgoing = jnp.einsum(
        "oc,chw->ohw", send_pick, grouped, preferred_element_type=jnp.float32
    ).astype(jnp.bfloat16)
    arrived = lax.all_to_all(outgoing, "ctx", split_axis=0, concat_axis=0, tiled=True)
    slot_hits = (owner_table == own_index).astype(jnp.int32)
    slot_live = jnp.sum(slot_hits, axis=1)
    picked = jnp.sum(slot_hits * jnp.arange(PIECES, dtype=jnp.int32)[None, :], axis=1)
    slot_pos = (place_ids[:, None] * PIECES + picked[:, None]) * block_rows + jnp.arange(
        block_rows, dtype=jnp.int32
    )[None, :]
    query_pos = jnp.where(slot_live[:, None] > 0, slot_pos, -1).reshape(-1)
    context = attend(
        arrived.reshape(place_count * block_rows, queries.shape[1]),
        query_pos,
        keys,
        values,
        doc_starts,
    )
    return project(context, out_weight)


SMEM = pl.BlockSpec(memory_space=pltpu.SMEM)
VMEM = pl.BlockSpec(memory_space=pltpu.VMEM)
HBM = pl.BlockSpec(memory_space=pltpu.HBM)


def _own_ctx():
    return lax.axis_index("ctx")


def _own_z():
    return lax.div(_own_ctx(), 2)


def _find_piece(table_ref, source, owner):
    piece = jnp.int32(0)
    for i in range(PIECES):
        piece = jnp.where(table_ref[source * PIECES + i] == owner, jnp.int32(i), piece)
    return piece


def _rows(start, size):
    return pl.ds(pl.multiple_of(start, size), size)


def _join_keys_values_kernel(keys_ref, values_ref, out_ref, sems):
    rows = keys_ref.shape[0]
    copies = [
        pltpu.make_async_copy(keys_ref, out_ref.at[pl.ds(0, rows)], sems.at[0]),
        pltpu.make_async_copy(values_ref, out_ref.at[pl.ds(rows, rows)], sems.at[1]),
    ]
    for copy in copies:
        copy.start()
    for copy in copies:
        copy.wait()


def _join_keys_values(keys, values):
    return pl.pallas_call(
        _join_keys_values_kernel,
        out_shape=jax.ShapeDtypeStruct((2 * keys.shape[0], keys.shape[1]), keys.dtype),
        in_specs=[HBM] * 2,
        out_specs=VMEM,
        scratch_shapes=[pltpu.SemaphoreType.DMA((2,))],
        compiler_params=pltpu.CompilerParams(vmem_limit_bytes=2 * 2**20),
        cost_estimate=pl.CostEstimate(flops=1, bytes_accessed=1, transcendentals=0),
        name="join_keys_values",
    )(keys, values)


def _queries_for_other_core_kernel(names, meta_ref, queries_ref, w_ref, out_ref, kept_ref, *rest):
    *w_out, sem, w_sems = rest
    w_copies = _weight_copies(names, w_ref, w_out, w_sems)
    copy = pltpu.make_async_copy(queries_ref, kept_ref, sem)
    copy.start()
    for w_copy in w_copies:
        w_copy.start()
    copy.wait()
    c = _own_ctx()
    core = lax.rem(c, 2)
    rows = queries_ref.shape[0] // PIECES
    for j in range(PIECES // 2):
        piece = _find_piece(meta_ref, c, 2 * j + 1 - core)
        out_ref[j * rows:(j + 1) * rows] = kept_ref[_rows(piece * rows, rows)]
    for w_copy in w_copies:
        w_copy.wait()


def _queries_for_other_core(names, meta, queries, out_weight):
    return pl.pallas_call(
        functools.partial(_queries_for_other_core_kernel, names),
        out_shape=[
            jax.ShapeDtypeStruct((queries.shape[0] // 2, queries.shape[1]), queries.dtype),
            jax.ShapeDtypeStruct(queries.shape, queries.dtype),
        ] + [_eighth(out_weight) for _ in names],
        in_specs=[SMEM, HBM, HBM],
        out_specs=[VMEM] * (2 + len(names)),
        scratch_shapes=[pltpu.SemaphoreType.DMA, pltpu.SemaphoreType.DMA((len(names),))],
        compiler_params=pltpu.CompilerParams(vmem_limit_bytes=2 * 2**20),
        cost_estimate=pl.CostEstimate(flops=1, bytes_accessed=1, transcendentals=0),
        name="queries_for_other_core",
    )(meta, queries, out_weight)


EIGHTHS = {
    "xf": (1, 0), "xp": (3, 0), "yf": (2, 1), "yp": (3, 1), "py": (2, 0), "px": (1, 1), "k0": (0, 0), "k1": (0, 1),
}


def _weight_copies(names, w_ref, out_refs, sems):
    half = w_ref.shape[0] // (2 * N_FAST_HEAD)
    copies = []
    for n, name in enumerate(names):
        flip, side = EIGHTHS[name]
        row = (lax.axis_index("head") ^ flip) * (2 * half) + side * half
        copies.append(pltpu.make_async_copy(w_ref.at[_rows(row, half)], out_refs[n], sems.at[n]))
    return copies


def _eighth(out_weight):
    return jax.ShapeDtypeStruct((out_weight.shape[0] // (2 * N_FAST_HEAD), out_weight.shape[1]), out_weight.dtype)


def _stage_kernel(names, w_ref, after_ref, *rest):
    copies = _weight_copies(names, w_ref, rest[:-1], rest[-1])
    for copy in copies:
        copy.start()
    for copy in copies:
        copy.wait()


def _stage_weights(names, out_weight, after):
    return pl.pallas_call(
        functools.partial(_stage_kernel, names),
        out_shape=[_eighth(out_weight) for _ in names],
        in_specs=[HBM, VMEM],
        out_specs=[VMEM] * len(names),
        scratch_shapes=[pltpu.SemaphoreType.DMA((len(names),))],
        compiler_params=pltpu.CompilerParams(vmem_limit_bytes=8 * 2**20),
        cost_estimate=pl.CostEstimate(flops=1, bytes_accessed=1, transcendentals=0),
        name="stage_weights",
    )(out_weight, after)


def _attend_kernel(
    groups, names, meta_ref, queries_ref, other_ref,
    kv0_ref, kv1_ref, kv2_ref, kv3_ref, w_ref,
    *rest,
):
    count = len(groups)
    out_refs, w_out = rest[:count], rest[count:count + len(names)]
    kbuf, vbuf, qbuf, ctxbuf, w_sems = rest[count + len(names):]
    w_copies = _weight_copies(names, w_ref, w_out, w_sems)
    for copy in w_copies:
        copy.start()
    c = _own_ctx()
    core = lax.rem(c, 2)
    z = lax.div(c, 2)
    rows = kv0_ref.shape[0] // 2
    piece_rows = rows // PIECES
    tile = 128
    heads = kv0_ref.shape[1] // HEAD_SIZE
    slots = (2 + core, 3 - core, core, 1 - core)
    for b, kv_ref in enumerate((kv0_ref, kv1_ref, kv2_ref, kv3_ref)):
        at = _rows(slots[b] * rows, rows)
        kbuf[at] = kv_ref[:rows]
        for kv in range(heads):
            vbuf[at, 2 * kv * HEAD_SIZE:(2 * kv + 1) * HEAD_SIZE] = (
                kv_ref[rows:, kv * HEAD_SIZE:(kv + 1) * HEAD_SIZE])
            vbuf[at, (2 * kv + 1) * HEAD_SIZE:(2 * kv + 2) * HEAD_SIZE] = jnp.ones((rows, HEAD_SIZE), jnp.bfloat16)
    starts = []
    for n, k in enumerate(groups):
        zdest = z ^ k
        owner = 2 * zdest + core
        mine = _find_piece(meta_ref, c, owner)
        theirs = _find_piece(meta_ref, c + 1 - 2 * core, owner)
        qbuf[2 * n + core] = queries_ref[_rows(mine * piece_rows, piece_rows)]
        qbuf[2 * n + 1 - core] = other_ref[_rows(zdest * piece_rows, piece_rows)]
        at0 = jnp.where(core == 0, mine, theirs)
        at1 = jnp.where(core == 0, theirs, mine)
        starts.append((at0 * piece_rows, rows + at1 * piece_rows))
    doc_start = []
    running = jnp.int32(0)
    lengths_at = PIECES * PIECES
    for d in range(lengths_at, meta_ref.shape[0]):
        doc_start.append(running)
        running = running + meta_ref[d]
    base = 2 * rows * (z - 1)
    group = queries_ref.shape[1] // kv0_ref.shape[1]
    scale = math.log2(math.e) / math.sqrt(HEAD_SIZE)

    def tiles_needed(p0):
        low = jnp.int32(0)
        for start in doc_start:
            low = jnp.where(2 * rows * z + p0 >= start, start, low)
        return lax.div(2 * rows * z + p0, tile) - lax.div(low, tile) + 1

    def piece_keys(p0, span):
        first = pl.multiple_of(lax.div(p0, tile) * tile + 2 * rows + tile - span, tile)
        pos = 2 * rows * z + p0 + lax.broadcasted_iota(jnp.int32, (piece_rows, 1), 0)
        low = jnp.zeros((piece_rows, 1), jnp.int32)
        for start in doc_start:
            low = jnp.where(pos >= start, start, low)
        key_pos = base + first + lax.broadcasted_iota(jnp.int32, (piece_rows, span), 1)
        return first, (key_pos >= low) & (key_pos <= pos)

    def some_pieces(pieces, span):
        units, scores, weights = [], [], []
        for n, p0 in pieces:
            first, allowed = piece_keys(p0, span)
            units += [(n, kv, first, allowed) for kv in range(heads)]
        for n, kv, first, allowed in units:
            q = jnp.concatenate(
                [qbuf[n, :, pl.ds((kv * group + g) * HEAD_SIZE, HEAD_SIZE)] for g in range(group)], axis=0)
            k = kbuf[pl.ds(first, span), pl.ds(kv * HEAD_SIZE, HEAD_SIZE)]
            scores.append(lax.dot_general(q, k, (((1,), (1,)), ((), ())), preferred_element_type=jnp.float32))
        for (n, kv, first, allowed), s in zip(units, scores):
            s = jnp.where(allowed[None], s.reshape(group, piece_rows, span), MASKED)
            w = jnp.exp2((s - jnp.max(s, axis=2, keepdims=True)) * scale)
            weights.append(w.astype(jnp.bfloat16).reshape(group * piece_rows, span))
        for (n, kv, first, allowed), w in zip(units, weights):
            o = jnp.dot(w, vbuf[pl.ds(first, span), pl.ds(kv * 2 * HEAD_SIZE, 2 * HEAD_SIZE)],
                        preferred_element_type=jnp.float32)
            o = (o[:, :HEAD_SIZE] / o[:, HEAD_SIZE:]).astype(jnp.bfloat16)
            for g in range(group):
                ctxbuf[n, :, pl.ds((kv * group + g) * HEAD_SIZE, HEAD_SIZE)] = o[g * piece_rows:(g + 1) * piece_rows]

    together = 2
    most_tiles = 5

    def step(i, carry):
        pieces = []
        for j in range(together):
            n = i * together + j
            p0 = starts[0][0]
            for m in range(1, 2 * count):
                p0 = jnp.where(n == m, starts[m // 2][m % 2], p0)
            pieces.append((n, p0))
        needed = functools.reduce(jnp.maximum, [tiles_needed(p0) for n, p0 in pieces])
        least = 0
        for tiles in (2, 3, most_tiles):
            fits = needed > least if tiles == most_tiles else (needed > least) & (needed <= tiles)
            pl.when(fits)(functools.partial(some_pieces, pieces, tiles * tile))
            least = tiles
        return carry

    lax.fori_loop(0, 2 * count // together, step, 0)
    for n, out_ref in enumerate(out_refs):
        out_ref[...] = ctxbuf[2 * n:2 * n + 2].reshape(out_ref.shape)
    for copy in w_copies:
        copy.wait()


def _attend_groups(groups, names, meta, queries, other, kv, out_weight):
    piece = queries.shape[0] // PIECES
    rows = kv[0].shape[0] // 2
    return pl.pallas_call(
        functools.partial(_attend_kernel, groups, names),
        out_shape=[jax.ShapeDtypeStruct((2 * piece, queries.shape[1]), jnp.bfloat16) for _ in groups]
        + [_eighth(out_weight) for _ in names],
        in_specs=[SMEM] + [VMEM] * 6 + [HBM],
        out_specs=[VMEM] * (len(groups) + len(names)),
        scratch_shapes=[
            pltpu.VMEM((4 * rows, kv[0].shape[1]), jnp.bfloat16),
            pltpu.VMEM((4 * rows, 2 * kv[0].shape[1]), jnp.bfloat16),
            pltpu.VMEM((2 * len(groups), piece, queries.shape[1]), jnp.bfloat16),
            pltpu.VMEM((2 * len(groups), piece, queries.shape[1]), jnp.bfloat16),
            pltpu.SemaphoreType.DMA((len(names),)),
        ],
        compiler_params=pltpu.CompilerParams(vmem_limit_bytes=12 * 2**20),
        cost_estimate=pl.CostEstimate(flops=1, bytes_accessed=1, transcendentals=0),
        name="attend_groups",
    )(meta, queries, other, *kv, out_weight)


def _dot_to(out_ref, weight_ref, tokens):
    out_ref[...] = jnp.dot(weight_ref[...], tokens, preferred_element_type=jnp.float32).astype(out_ref.dtype)


def _join_kernel(a_ref, b_ref, wx_ref, wy_ref, x_ref, y_ref, joined_ref, catbuf):
    second = lax.rem(_own_z(), 2)
    mid = a_ref.shape[0]
    catbuf[_rows(second * mid, mid)] = a_ref[...]
    catbuf[_rows((1 - second) * mid, mid)] = b_ref[...]
    joined = catbuf[...].T
    joined_ref[...] = joined
    _dot_to(x_ref, wx_ref, joined)
    _dot_to(y_ref, wy_ref, joined)


def _two_rows_kernel(joined_ref, w0_ref, w1_ref, out0_ref, out1_ref):
    joined = joined_ref[...]
    _dot_to(out0_ref, w0_ref, joined)
    _dot_to(out1_ref, w1_ref, joined)


def _keep_rows_kernel(first_ref, second_ref, w0_ref, w1_ref, first_out, second_out):
    half, tokens = w0_ref.shape[0], first_ref.shape[1]
    both = jnp.concatenate([first_ref[...], second_ref[...]], axis=1)
    for i, w_ref in enumerate((w0_ref, w1_ref)):
        out = jnp.dot(w_ref[...], both, preferred_element_type=jnp.float32).astype(first_out.dtype)
        first_out[i * half:(i + 1) * half] = out[:, :tokens]
        second_out[i * half:(i + 1) * half] = out[:, tokens:]


def _project(kernel, name, out_shape, operands, scratch=()):
    return pl.pallas_call(
        kernel,
        out_shape=out_shape,
        in_specs=[VMEM] * len(operands),
        out_specs=[VMEM] * len(out_shape),
        scratch_shapes=scratch,
        compiler_params=pltpu.CompilerParams(vmem_limit_bytes=8 * 2**20),
        cost_estimate=pl.CostEstimate(flops=1, bytes_accessed=1, transcendentals=0),
        name=name,
    )(*operands)


def _join(a, b, weights):
    (rows, depth), tokens = weights["xp"].shape, a.shape[0] + b.shape[0]
    part = jax.ShapeDtypeStruct((rows, tokens), jnp.bfloat16)
    return _project(
        _join_kernel, "join", [part] * 2 + [jax.ShapeDtypeStruct((depth, tokens), jnp.bfloat16)],
        (a, b, weights["xp"], weights["yp"]), [pltpu.VMEM((tokens, depth), jnp.bfloat16)])


def _two_rows(name, joined, weights, names):
    part = jax.ShapeDtypeStruct((weights[names[0]].shape[0], joined.shape[1]), jnp.bfloat16)
    return _project(_two_rows_kernel, name, [part] * 2, (joined, weights[names[0]], weights[names[1]]))


def _keep_rows(first, second, weights):
    part = jax.ShapeDtypeStruct((2 * weights["k0"].shape[0], first.shape[1]), jnp.bfloat16)
    return _project(_keep_rows_kernel, "keep_rows", [part] * 2, (first, second, weights["k0"], weights["k1"]))


def _add_kernel(a_ref, b_ref, out_ref):
    out_ref[...] = (a_ref[...].astype(jnp.float32) + b_ref[...].astype(jnp.float32)).astype(out_ref.dtype)


def _add(a, b):
    return _project(_add_kernel, "add", [jax.ShapeDtypeStruct(a.shape, jnp.bfloat16)], (a, b))[0]


def _sum_parts(keep_ref, x1_ref, y1_ref, y2_ref, x2_ref):
    half = y2_ref.shape[0]
    f32 = jnp.float32
    first = keep_ref[:half].astype(f32) + x1_ref[...].astype(f32) + y2_ref[...].astype(f32)
    second = keep_ref[half:].astype(f32) + y1_ref[...].astype(f32) + x2_ref[...].astype(f32)
    return first, second


def _own_half(rows, tokens):
    lane = lax.broadcasted_iota(jnp.int32, (rows, tokens), 1)
    return lax.div(lane, tokens // 2) == lax.rem(_own_z(), 2)


def _finish_first_kernel(keep_ref, x1_ref, y1_ref, y2_ref, x2_ref, out_ref, away_ref):
    half, tokens = y2_ref.shape
    top, bottom = _sum_parts(keep_ref, x1_ref, y1_ref, y2_ref, x2_ref)
    out_ref[:half] = top.astype(out_ref.dtype)
    out_ref[half:] = bottom.astype(out_ref.dtype)
    own = _own_half(half, tokens)
    away_ref[...] = jnp.where(own, pltpu.roll(bottom, tokens // 2, 1), top).astype(away_ref.dtype)


def _unpack_kernel(away_ref, out_ref):
    half, tokens = away_ref.shape
    out_ref[:half] = pltpu.roll(away_ref[...].astype(jnp.float32), tokens // 2, 1).astype(out_ref.dtype)
    out_ref[half:] = away_ref[...]


def _half_sum_kernel(side, keep_ref, one_ref, out_ref):
    half = one_ref.shape[0]
    out_ref[...] = keep_ref[side * half:(side + 1) * half].astype(jnp.float32) + one_ref[...].astype(jnp.float32)


def _half_sum(side, keep, one):
    return _finish(functools.partial(_half_sum_kernel, side), [jax.ShapeDtypeStruct(one.shape, jnp.float32)], (keep, one))[0]


def _finish_second_kernel(first_ref, away_ref, top_ref, bottom_ref, y2_ref, x2_ref, out_ref, rows_ref, sems):
    half, tokens = y2_ref.shape
    part = half // 2
    upper = lax.div(_own_z(), 2)
    mine, others = _rows(upper * tokens, tokens), _rows((1 - upper) * tokens, tokens)
    own = _own_half(part, tokens)
    copies = []
    for i in range(4):
        at, inside = pl.ds(i * part, part), pl.ds(i % 2 * part, part)
        one_ref, two_ref = (top_ref, y2_ref) if i < 2 else (bottom_ref, x2_ref)
        sums = one_ref[inside] + two_ref[inside].astype(jnp.float32)
        first, away = first_ref[at].astype(jnp.float32), away_ref[at].astype(jnp.float32)
        rows_ref[at, mine] = jnp.where(own, first, pltpu.roll(sums, tokens // 2, 1)).astype(rows_ref.dtype)
        rows_ref[at, others] = jnp.where(own, away, sums).astype(rows_ref.dtype)
        copies.append(pltpu.make_async_copy(rows_ref.at[at], out_ref.at[at], sems.at[i]))
        copies[-1].start()
    for copy in copies:
        copy.wait()


def _finish_second(first, away, top, bottom, y2, x2):
    rows, tokens = first.shape
    return pl.pallas_call(
        _finish_second_kernel,
        out_shape=jax.ShapeDtypeStruct((rows, 2 * tokens), jnp.bfloat16),
        in_specs=[VMEM] * 6,
        out_specs=HBM,
        scratch_shapes=[pltpu.VMEM((rows, 2 * tokens), jnp.bfloat16), pltpu.SemaphoreType.DMA((4,))],
        compiler_params=pltpu.CompilerParams(vmem_limit_bytes=8 * 2**20),
        cost_estimate=pl.CostEstimate(flops=1, bytes_accessed=1, transcendentals=0),
        name="finish_second",
    )(first, away, top, bottom, y2, x2)


def _finish(kernel, out_shape, operands):
    return pl.pallas_call(
        kernel,
        out_shape=out_shape,
        in_specs=[VMEM] * len(operands),
        out_specs=jax.tree.map(lambda _: VMEM, out_shape),
        compiler_params=pltpu.CompilerParams(vmem_limit_bytes=8 * 2**20),
        cost_estimate=pl.CostEstimate(flops=1, bytes_accessed=1, transcendentals=0),
        name="finish",
    )(*operands)


def _flip(x, axis, bits):
    n = lax.axis_size(axis)
    return lax.ppermute(x, axis, [(i, i ^ bits) for i in range(n)])


def per_device_fast(queries, keys, values, out_weight, doc_lengths, owners):
    places = lax.axis_size("ctx")
    queries, keys, values, out_weight = (
        pltpu.with_memory_space_constraint(x, pltpu.HBM) for x in (queries, keys, values, out_weight))
    kv0 = _join_keys_values(keys, values)
    kv2 = lax.ppermute(kv0, "ctx", [(i, i + 2) for i in range(places - 2)])
    kv1 = _flip(kv0, "ctx", 1)
    meta = jnp.concatenate([owners.reshape(-1), doc_lengths])
    weights = {}
    leaving, queries, weights["xp"] = _queries_for_other_core(("xp",), meta, queries, out_weight)
    other = _flip(leaving, "ctx", 1)
    weights["yp"], weights["xf"] = _stage_weights(("yp", "xf"), out_weight, leaving)
    kv2, weights["xf"] = lax.optimization_barrier((kv2, weights["xf"]))
    kv = (kv0, kv1, kv2, _flip(kv2, "ctx", 1))
    loaded = ("yf", "py", "px")
    ctx0, ctx2, ctx1, ctx3, *loads = _attend_groups((0, 2, 1, 3), loaded, meta, queries, other, kv, out_weight)
    weights.update(zip(loaded, loads))
    ctx1, ctx3 = _flip(ctx1, "ctx", 2), _flip(ctx3, "ctx", 6)

    xp, yp, joined = _join(ctx0, ctx2, weights)
    x1p, y1p = _flip(xp, "head", 1), _flip(yp, "head", 2)
    xf, yf = _two_rows("last_rows", joined, weights, ("xf", "yf"))
    x1f, y1f = _flip(xf, "head", 1), _flip(yf, "head", 2)
    weights["k0"], weights["k1"] = _stage_weights(("k0", "k1"), out_weight, joined)
    joined, weights["k0"], ctx1, ctx3 = lax.optimization_barrier((joined, weights["k0"], ctx1, ctx3))
    y2, x2 = _two_rows("pass_rows", joined, weights, ("py", "px"))
    y2, x2 = _add(y2, x1p), _add(x2, y1p)
    weights["xp"], y2, x2 = lax.optimization_barrier((weights["xp"], y2, x2))
    y2, x2 = _flip(y2, "head", 2), _flip(x2, "head", 1)

    xp, yp, joined2 = _join(ctx1, ctx3, weights)
    xp, yp, x1f, y1f = lax.optimization_barrier((xp, yp, x1f, y1f))
    next_x1p, next_y1p = _flip(xp, "head", 1), _flip(yp, "head", 2)
    xf, yf = _two_rows("last_rows", joined2, weights, ("xf", "yf"))
    next_x1f, next_y1f = _flip(xf, "head", 1), _flip(yf, "head", 2)
    keep, next_keep = _keep_rows(joined, joined2, weights)
    rows, tokens = keep.shape
    first, away = _finish(_finish_first_kernel, [
        jax.ShapeDtypeStruct((rows, tokens), jnp.bfloat16),
        jax.ShapeDtypeStruct((rows // 2, tokens), jnp.bfloat16),
    ], (keep, x1f, y1f, y2, x2))
    joined2, away = lax.optimization_barrier((joined2, away))
    away = _flip(away, "ctx", 4)
    y2, x2 = _two_rows("pass_rows", joined2, weights, ("py", "px"))
    y2, x2 = _add(y2, next_x1p), _add(x2, next_y1p)
    y2, x2 = _flip(y2, "head", 2), _flip(x2, "head", 1)
    away = _finish(_unpack_kernel, [jax.ShapeDtypeStruct((rows, tokens), jnp.bfloat16)], (away,))[0]
    away, next_keep = lax.optimization_barrier((away, next_keep))
    bottom = _half_sum(1, next_keep, next_y1f)
    bottom, next_keep = lax.optimization_barrier((bottom, next_keep))
    top = _half_sum(0, next_keep, next_x1f)
    return _finish_second(first, away, top, bottom, y2, x2)


def solution(mesh):
    in_specs = (P("ctx", "head"), P("ctx", "head"), P("ctx", "head"), P(None, "head"), P(), P())
    out_specs = P("head", "ctx")
    fast = mesh.shape["ctx"] == PIECES and mesh.shape["head"] == N_FAST_HEAD
    return jax.shard_map(
        per_device_fast if fast else per_device, mesh=mesh, in_specs=in_specs, out_specs=out_specs, check_vma=False
    )
```

```python
import functools
import math

import jax
import jax.numpy as jnp
from jax import lax
from jax.experimental import pallas as pl
from jax.experimental.pallas import tpu as pltpu
from jax.sharding import PartitionSpec as P

HEAD_SIZE = 128
PIECES = 8
N_FAST_HEAD = 4


MASKED = -1e30


def document_index(positions, doc_starts):
    return jnp.sum((positions[:, None] >= doc_starts[None, :]).astype(jnp.int32), axis=1) - 1


def attend(query_rows, query_pos, keys, values, doc_starts):
    row_count = query_rows.shape[0]
    key_heads = keys.shape[1] // HEAD_SIZE
    group_length = query_rows.shape[1] // keys.shape[1]
    query_heads = query_rows.reshape(row_count, key_heads, group_length, HEAD_SIZE)
    query_doc = document_index(query_pos, doc_starts)
    score_scale = 1.0 / math.sqrt(HEAD_SIZE)
    initial = (
        jnp.full((row_count, key_heads, group_length), MASKED, jnp.float32),
        jnp.zeros((row_count, key_heads, group_length), jnp.float32),
        jnp.zeros((row_count, key_heads, group_length, HEAD_SIZE), jnp.float32),
    )
    key_piece = lax.all_gather(keys, "ctx", axis=0, tiled=True)
    value_piece = lax.all_gather(values, "ctx", axis=0, tiled=True)
    piece_rows = key_piece.shape[0]
    tile_rows = math.gcd(piece_rows, 512)

    def one_tile(tile_index, running):
        tile_start = tile_index * tile_rows
        key_block = lax.dynamic_slice_in_dim(key_piece, tile_start, tile_rows, 0).reshape(
            tile_rows, key_heads, HEAD_SIZE
        )
        value_block = lax.dynamic_slice_in_dim(value_piece, tile_start, tile_rows, 0).reshape(
            tile_rows, key_heads, HEAD_SIZE
        )
        key_pos = tile_start + jnp.arange(tile_rows, dtype=jnp.int32)
        key_doc = document_index(key_pos, doc_starts)
        allowed = (query_doc[:, None] == key_doc[None, :]) & (
            key_pos[None, :] <= query_pos[:, None]
        )
        running_max, running_sum, weighted = running
        scores = (
            jnp.einsum("rkgd,nkd->rkgn", query_heads, key_block, preferred_element_type=jnp.float32)
            * score_scale
        )
        allowed_all = allowed[:, None, None, :]
        scores = jnp.where(allowed_all, scores, MASKED)
        new_max = jnp.maximum(running_max, jnp.max(scores, axis=-1))
        factor = jnp.exp(running_max - new_max)
        weights = jnp.where(allowed_all, jnp.exp(scores - new_max[..., None]), 0.0)
        new_sum = running_sum * factor + jnp.sum(weights, axis=-1)
        new_weighted = weighted * factor[..., None] + jnp.einsum(
            "rkgn,nkd->rkgd",
            weights.astype(jnp.bfloat16),
            value_block,
            preferred_element_type=jnp.float32,
        )
        return (new_max, new_sum, new_weighted)

    final_max, final_sum, weighted = lax.fori_loop(0, piece_rows // tile_rows, one_tile, initial)
    result = weighted / jnp.maximum(final_sum, 1.0)[..., None]
    return result.reshape(row_count, key_heads * group_length * HEAD_SIZE).astype(jnp.bfloat16)


def project(context, out_weight):
    return lax.psum_scatter(
        lax.dot_general(
            out_weight, context, (((1,), (1,)), ((), ())), preferred_element_type=jnp.float32
        ).astype(jnp.bfloat16),
        "head",
        scatter_dimension=0,
        tiled=True,
    )


def per_device(queries, keys, values, out_weight, doc_lengths, owners):
    place_count = lax.axis_size("ctx")
    own_index = lax.axis_index("ctx")
    token_count = queries.shape[0]
    block_rows = token_count // PIECES
    doc_ends = jnp.cumsum(doc_lengths)
    doc_starts = doc_ends - doc_lengths
    owner_table = owners[:, 0].reshape(place_count, PIECES)
    own_owners = lax.dynamic_index_in_dim(owner_table, own_index, 0, keepdims=False)
    place_ids = jnp.arange(place_count, dtype=jnp.int32)
    send_pick = (own_owners[None, :] == place_ids[:, None]).astype(jnp.bfloat16)
    grouped = queries.reshape(PIECES, block_rows, queries.shape[1])
    outgoing = jnp.einsum(
        "oc,chw->ohw", send_pick, grouped, preferred_element_type=jnp.float32
    ).astype(jnp.bfloat16)
    arrived = lax.all_to_all(outgoing, "ctx", split_axis=0, concat_axis=0, tiled=True)
    slot_hits = (owner_table == own_index).astype(jnp.int32)
    slot_live = jnp.sum(slot_hits, axis=1)
    picked = jnp.sum(slot_hits * jnp.arange(PIECES, dtype=jnp.int32)[None, :], axis=1)
    slot_pos = (place_ids[:, None] * PIECES + picked[:, None]) * block_rows + jnp.arange(
        block_rows, dtype=jnp.int32
    )[None, :]
    query_pos = jnp.where(slot_live[:, None] > 0, slot_pos, -1).reshape(-1)
    context = attend(
        arrived.reshape(place_count * block_rows, queries.shape[1]),
        query_pos,
        keys,
        values,
        doc_starts,
    )
    return project(context, out_weight)


SMEM = pl.BlockSpec(memory_space=pltpu.SMEM)
VMEM = pl.BlockSpec(memory_space=pltpu.VMEM)
HBM = pl.BlockSpec(memory_space=pltpu.HBM)
ANY = pl.BlockSpec(memory_space=pl.ANY)


def _own_ctx():
    return lax.axis_index("ctx")


def _own_z():
    return lax.div(_own_ctx(), 2)


def _find_piece(table_ref, source, owner):
    piece = jnp.int32(0)
    for i in range(PIECES):
        piece = jnp.where(table_ref[source * PIECES + i] == owner, jnp.int32(i), piece)
    return piece


def _rows(start, size):
    return pl.ds(pl.multiple_of(start, size), size)


def _join_keys_values_kernel(keys_ref, values_ref, out_ref, sems):
    rows = keys_ref.shape[0]
    copies = [
        pltpu.make_async_copy(keys_ref, out_ref.at[pl.ds(0, rows)], sems.at[0]),
        pltpu.make_async_copy(values_ref, out_ref.at[pl.ds(rows, rows)], sems.at[1]),
    ]
    for copy in copies:
        copy.start()
    for copy in copies:
        copy.wait()


def _join_keys_values(keys, values):
    return pl.pallas_call(
        _join_keys_values_kernel,
        out_shape=jax.ShapeDtypeStruct((2 * keys.shape[0], keys.shape[1]), keys.dtype),
        in_specs=[HBM] * 2,
        out_specs=VMEM,
        scratch_shapes=[pltpu.SemaphoreType.DMA((2,))],
        compiler_params=pltpu.CompilerParams(vmem_limit_bytes=2 * 2**20),
        cost_estimate=pl.CostEstimate(flops=1, bytes_accessed=1, transcendentals=0),
        name="join_keys_values",
    )(keys, values)


def _queries_for_other_core_kernel(names, meta_ref, queries_ref, w_ref, out_ref, kept_ref, *rest):
    *w_out, sem, w_sems, table_ref, table_sem = rest
    w_copies = _weight_copies(names, w_ref, w_out, w_sems)
    table_copy = pltpu.make_async_copy(meta_ref, table_ref, table_sem)
    table_copy.start()
    copy = pltpu.make_async_copy(queries_ref, kept_ref, sem)
    copy.start()
    for w_copy in w_copies:
        w_copy.start()
    copy.wait()
    table_copy.wait()
    c = _own_ctx()
    core = lax.rem(c, 2)
    rows = queries_ref.shape[0] // PIECES
    for j in range(PIECES // 2):
        piece = _find_piece(table_ref, c, 2 * j + 1 - core)
        out_ref[j * rows:(j + 1) * rows] = kept_ref[_rows(piece * rows, rows)]
    for w_copy in w_copies:
        w_copy.wait()


def _queries_for_other_core(names, meta, queries, out_weight):
    return pl.pallas_call(
        functools.partial(_queries_for_other_core_kernel, names),
        out_shape=[
            jax.ShapeDtypeStruct((queries.shape[0] // 2, queries.shape[1]), queries.dtype),
            jax.ShapeDtypeStruct(queries.shape, queries.dtype),
        ] + [_eighth(out_weight) for _ in names],
        in_specs=[ANY, HBM, HBM],
        out_specs=[VMEM] * (2 + len(names)),
        scratch_shapes=[
            pltpu.SemaphoreType.DMA, pltpu.SemaphoreType.DMA((len(names),)),
            pltpu.SMEM(meta.shape, meta.dtype), pltpu.SemaphoreType.DMA],
        compiler_params=pltpu.CompilerParams(vmem_limit_bytes=2 * 2**20),
        cost_estimate=pl.CostEstimate(flops=1, bytes_accessed=1, transcendentals=0),
        name="queries_for_other_core",
    )(meta, queries, out_weight)


EIGHTHS = {
    "xf": (1, 0), "xp": (3, 0), "yf": (2, 1), "yp": (3, 1), "py": (2, 0), "px": (1, 1), "k0": (0, 0), "k1": (0, 1),
}


def _weight_copies(names, w_ref, out_refs, sems):
    half = w_ref.shape[0] // (2 * N_FAST_HEAD)
    copies = []
    for n, name in enumerate(names):
        flip, side = EIGHTHS[name]
        row = (lax.axis_index("head") ^ flip) * (2 * half) + side * half
        copies.append(pltpu.make_async_copy(w_ref.at[_rows(row, half)], out_refs[n], sems.at[n]))
    return copies


def _eighth(out_weight):
    return jax.ShapeDtypeStruct((out_weight.shape[0] // (2 * N_FAST_HEAD), out_weight.shape[1]), out_weight.dtype)


def _stage_kernel(names, w_ref, after_ref, *rest):
    copies = _weight_copies(names, w_ref, rest[:-1], rest[-1])
    for copy in copies:
        copy.start()
    for copy in copies:
        copy.wait()


def _stage_weights(names, out_weight, after):
    return pl.pallas_call(
        functools.partial(_stage_kernel, names),
        out_shape=[_eighth(out_weight) for _ in names],
        in_specs=[HBM, VMEM],
        out_specs=[VMEM] * len(names),
        scratch_shapes=[pltpu.SemaphoreType.DMA((len(names),))],
        compiler_params=pltpu.CompilerParams(vmem_limit_bytes=8 * 2**20),
        cost_estimate=pl.CostEstimate(flops=1, bytes_accessed=1, transcendentals=0),
        name="stage_weights",
    )(out_weight, after)


def _attend_kernel(
    groups, names, documents, meta_ref, queries_ref, other_ref,
    kv0_ref, kv1_ref, kv2_ref, kv3_ref, w_ref,
    *rest,
):
    count = len(groups)
    out_refs, w_out = rest[:count], rest[count:count + len(names)]
    kbuf, vbuf, qbuf, ctxbuf, w_sems, table_ref, table_sem = rest[count + len(names):]
    table_copy = pltpu.make_async_copy(meta_ref, table_ref, table_sem)
    table_copy.start()
    w_copies = _weight_copies(names, w_ref, w_out, w_sems)
    for copy in w_copies:
        copy.start()
    c = _own_ctx()
    core = lax.rem(c, 2)
    z = lax.div(c, 2)
    rows = kv0_ref.shape[0] // 2
    piece_rows = rows // PIECES
    tile = 128
    heads = kv0_ref.shape[1] // HEAD_SIZE
    slots = (2 + core, 3 - core, core, 1 - core)
    for b, kv_ref in enumerate((kv0_ref, kv1_ref, kv2_ref, kv3_ref)):
        at = _rows(slots[b] * rows, rows)
        kbuf[at] = kv_ref[:rows]
        for kv in range(heads):
            vbuf[at, 2 * kv * HEAD_SIZE:(2 * kv + 1) * HEAD_SIZE] = (
                kv_ref[rows:, kv * HEAD_SIZE:(kv + 1) * HEAD_SIZE])
            vbuf[at, (2 * kv + 1) * HEAD_SIZE:(2 * kv + 2) * HEAD_SIZE] = jnp.ones((rows, HEAD_SIZE), jnp.bfloat16)
    table_copy.wait()
    starts = []
    for n, k in enumerate(groups):
        zdest = z ^ k
        owner = 2 * zdest + core
        mine = _find_piece(table_ref, c, owner)
        theirs = _find_piece(table_ref, c + 1 - 2 * core, owner)
        qbuf[2 * n + core] = queries_ref[_rows(mine * piece_rows, piece_rows)]
        qbuf[2 * n + 1 - core] = other_ref[_rows(zdest * piece_rows, piece_rows)]
        at0 = jnp.where(core == 0, mine, theirs)
        at1 = jnp.where(core == 0, theirs, mine)
        starts.append((at0 * piece_rows, rows + at1 * piece_rows))
    doc_start = []
    running = jnp.int32(0)
    lengths_at = PIECES * PIECES
    for d in range(lengths_at, lengths_at + documents):
        doc_start.append(running)
        running = running + table_ref[d]
    base = 2 * rows * (z - 1)
    group = queries_ref.shape[1] // kv0_ref.shape[1]
    scale = math.log2(math.e) / math.sqrt(HEAD_SIZE)

    def tiles_needed(p0):
        low = jnp.int32(0)
        for start in doc_start:
            low = jnp.where(2 * rows * z + p0 >= start, start, low)
        return lax.div(2 * rows * z + p0, tile) - lax.div(low, tile) + 1

    def piece_keys(p0, span):
        first = pl.multiple_of(lax.div(p0, tile) * tile + 2 * rows + tile - span, tile)
        pos = 2 * rows * z + p0 + lax.broadcasted_iota(jnp.int32, (piece_rows, 1), 0)
        low = jnp.zeros((piece_rows, 1), jnp.int32)
        for start in doc_start:
            low = jnp.where(pos >= start, start, low)
        key_pos = base + first + lax.broadcasted_iota(jnp.int32, (piece_rows, span), 1)
        return first, (key_pos >= low) & (key_pos <= pos)

    def some_pieces(pieces, span):
        units, scores, weights = [], [], []
        for n, p0 in pieces:
            first, allowed = piece_keys(p0, span)
            units += [(n, kv, first, allowed) for kv in range(heads)]
        for n, kv, first, allowed in units:
            q = jnp.concatenate(
                [qbuf[n, :, pl.ds((kv * group + g) * HEAD_SIZE, HEAD_SIZE)] for g in range(group)], axis=0)
            k = kbuf[pl.ds(first, span), pl.ds(kv * HEAD_SIZE, HEAD_SIZE)]
            scores.append(lax.dot_general(q, k, (((1,), (1,)), ((), ())), preferred_element_type=jnp.float32))
        for (n, kv, first, allowed), s in zip(units, scores):
            s = jnp.where(allowed[None], s.reshape(group, piece_rows, span), MASKED)
            w = jnp.exp2((s - jnp.max(s, axis=2, keepdims=True)) * scale)
            weights.append(w.astype(jnp.bfloat16).reshape(group * piece_rows, span))
        for (n, kv, first, allowed), w in zip(units, weights):
            o = jnp.dot(w, vbuf[pl.ds(first, span), pl.ds(kv * 2 * HEAD_SIZE, 2 * HEAD_SIZE)],
                        preferred_element_type=jnp.float32)
            o = (o[:, :HEAD_SIZE] / o[:, HEAD_SIZE:]).astype(jnp.bfloat16)
            for g in range(group):
                ctxbuf[n, :, pl.ds((kv * group + g) * HEAD_SIZE, HEAD_SIZE)] = o[g * piece_rows:(g + 1) * piece_rows]

    together = 2
    most_tiles = 5

    def step(i, carry):
        pieces = []
        for j in range(together):
            n = i * together + j
            p0 = starts[0][0]
            for m in range(1, 2 * count):
                p0 = jnp.where(n == m, starts[m // 2][m % 2], p0)
            pieces.append((n, p0))
        needed = functools.reduce(jnp.maximum, [tiles_needed(p0) for n, p0 in pieces])
        least = 0
        for tiles in (2, 3, most_tiles):
            fits = needed > least if tiles == most_tiles else (needed > least) & (needed <= tiles)
            pl.when(fits)(functools.partial(some_pieces, pieces, tiles * tile))
            least = tiles
        return carry

    lax.fori_loop(0, 2 * count // together, step, 0)
    for n, out_ref in enumerate(out_refs):
        out_ref[...] = ctxbuf[2 * n:2 * n + 2].reshape(out_ref.shape)
    for copy in w_copies:
        copy.wait()


def _attend_groups(groups, names, documents, meta, queries, other, kv, out_weight):
    piece = queries.shape[0] // PIECES
    rows = kv[0].shape[0] // 2
    return pl.pallas_call(
        functools.partial(_attend_kernel, groups, names, documents),
        out_shape=[jax.ShapeDtypeStruct((2 * piece, queries.shape[1]), jnp.bfloat16) for _ in groups]
        + [_eighth(out_weight) for _ in names],
        in_specs=[ANY] + [VMEM] * 6 + [HBM],
        out_specs=[VMEM] * (len(groups) + len(names)),
        scratch_shapes=[
            pltpu.VMEM((4 * rows, kv[0].shape[1]), jnp.bfloat16),
            pltpu.VMEM((4 * rows, 2 * kv[0].shape[1]), jnp.bfloat16),
            pltpu.VMEM((2 * len(groups), piece, queries.shape[1]), jnp.bfloat16),
            pltpu.VMEM((2 * len(groups), piece, queries.shape[1]), jnp.bfloat16),
            pltpu.SemaphoreType.DMA((len(names),)),
            pltpu.SMEM(meta.shape, meta.dtype),
            pltpu.SemaphoreType.DMA,
        ],
        compiler_params=pltpu.CompilerParams(vmem_limit_bytes=12 * 2**20),
        cost_estimate=pl.CostEstimate(flops=1, bytes_accessed=1, transcendentals=0),
        name="attend_groups",
    )(meta, queries, other, *kv, out_weight)


def _dot_to(out_ref, weight_ref, tokens):
    out_ref[...] = jnp.dot(weight_ref[...], tokens, preferred_element_type=jnp.float32).astype(out_ref.dtype)


def _join_kernel(a_ref, b_ref, wx_ref, wy_ref, x_ref, y_ref, joined_ref, catbuf):
    second = lax.rem(_own_z(), 2)
    mid = a_ref.shape[0]
    catbuf[_rows(second * mid, mid)] = a_ref[...]
    catbuf[_rows((1 - second) * mid, mid)] = b_ref[...]
    joined = catbuf[...].T
    joined_ref[...] = joined
    _dot_to(x_ref, wx_ref, joined)
    _dot_to(y_ref, wy_ref, joined)


def _two_rows_kernel(joined_ref, w0_ref, w1_ref, out0_ref, out1_ref):
    joined = joined_ref[...]
    _dot_to(out0_ref, w0_ref, joined)
    _dot_to(out1_ref, w1_ref, joined)


def _keep_rows_kernel(first_ref, second_ref, w0_ref, w1_ref, first_out, second_out):
    half, tokens = w0_ref.shape[0], first_ref.shape[1]
    both = jnp.concatenate([first_ref[...], second_ref[...]], axis=1)
    for i, w_ref in enumerate((w0_ref, w1_ref)):
        out = jnp.dot(w_ref[...], both, preferred_element_type=jnp.float32).astype(first_out.dtype)
        first_out[i * half:(i + 1) * half] = out[:, :tokens]
        second_out[i * half:(i + 1) * half] = out[:, tokens:]


def _project(kernel, name, out_shape, operands, scratch=()):
    return pl.pallas_call(
        kernel,
        out_shape=out_shape,
        in_specs=[VMEM] * len(operands),
        out_specs=[VMEM] * len(out_shape),
        scratch_shapes=scratch,
        compiler_params=pltpu.CompilerParams(vmem_limit_bytes=8 * 2**20),
        cost_estimate=pl.CostEstimate(flops=1, bytes_accessed=1, transcendentals=0),
        name=name,
    )(*operands)


def _join(a, b, weights):
    (rows, depth), tokens = weights["xp"].shape, a.shape[0] + b.shape[0]
    part = jax.ShapeDtypeStruct((rows, tokens), jnp.bfloat16)
    return _project(
        _join_kernel, "join", [part] * 2 + [jax.ShapeDtypeStruct((depth, tokens), jnp.bfloat16)],
        (a, b, weights["xp"], weights["yp"]), [pltpu.VMEM((tokens, depth), jnp.bfloat16)])


def _two_rows(name, joined, weights, names):
    part = jax.ShapeDtypeStruct((weights[names[0]].shape[0], joined.shape[1]), jnp.bfloat16)
    return _project(_two_rows_kernel, name, [part] * 2, (joined, weights[names[0]], weights[names[1]]))


def _keep_rows(first, second, weights):
    part = jax.ShapeDtypeStruct((2 * weights["k0"].shape[0], first.shape[1]), jnp.bfloat16)
    return _project(_keep_rows_kernel, "keep_rows", [part] * 2, (first, second, weights["k0"], weights["k1"]))


def _add_kernel(a_ref, b_ref, out_ref):
    out_ref[...] = (a_ref[...].astype(jnp.float32) + b_ref[...].astype(jnp.float32)).astype(out_ref.dtype)


def _add(a, b):
    return _project(_add_kernel, "add", [jax.ShapeDtypeStruct(a.shape, jnp.bfloat16)], (a, b))[0]


def _sum_parts(keep_ref, x1_ref, y1_ref, y2_ref, x2_ref):
    half = y2_ref.shape[0]
    f32 = jnp.float32
    first = keep_ref[:half].astype(f32) + x1_ref[...].astype(f32) + y2_ref[...].astype(f32)
    second = keep_ref[half:].astype(f32) + y1_ref[...].astype(f32) + x2_ref[...].astype(f32)
    return first, second


def _own_half(rows, tokens):
    lane = lax.broadcasted_iota(jnp.int32, (rows, tokens), 1)
    return lax.div(lane, tokens // 2) == lax.rem(_own_z(), 2)


def _finish_first_kernel(keep_ref, x1_ref, y1_ref, y2_ref, x2_ref, out_ref, away_ref):
    half, tokens = y2_ref.shape
    top, bottom = _sum_parts(keep_ref, x1_ref, y1_ref, y2_ref, x2_ref)
    out_ref[:half] = top.astype(out_ref.dtype)
    out_ref[half:] = bottom.astype(out_ref.dtype)
    own = _own_half(half, tokens)
    away_ref[...] = jnp.where(own, pltpu.roll(bottom, tokens // 2, 1), top).astype(away_ref.dtype)


def _unpack_kernel(away_ref, out_ref):
    half, tokens = away_ref.shape
    out_ref[:half] = pltpu.roll(away_ref[...].astype(jnp.float32), tokens // 2, 1).astype(out_ref.dtype)
    out_ref[half:] = away_ref[...]


def _half_sum_kernel(side, keep_ref, one_ref, out_ref):
    half = one_ref.shape[0]
    out_ref[...] = keep_ref[side * half:(side + 1) * half].astype(jnp.float32) + one_ref[...].astype(jnp.float32)


def _half_sum(side, keep, one):
    return _finish(functools.partial(_half_sum_kernel, side), [jax.ShapeDtypeStruct(one.shape, jnp.float32)], (keep, one))[0]


def _finish_second_kernel(first_ref, away_ref, top_ref, bottom_ref, y2_ref, x2_ref, out_ref, rows_ref, sems):
    half, tokens = y2_ref.shape
    part = half // 2
    upper = lax.div(_own_z(), 2)
    mine, others = _rows(upper * tokens, tokens), _rows((1 - upper) * tokens, tokens)
    own = _own_half(part, tokens)
    copies = []
    for i in range(4):
        at, inside = pl.ds(i * part, part), pl.ds(i % 2 * part, part)
        one_ref, two_ref = (top_ref, y2_ref) if i < 2 else (bottom_ref, x2_ref)
        sums = one_ref[inside] + two_ref[inside].astype(jnp.float32)
        first, away = first_ref[at].astype(jnp.float32), away_ref[at].astype(jnp.float32)
        rows_ref[at, mine] = jnp.where(own, first, pltpu.roll(sums, tokens // 2, 1)).astype(rows_ref.dtype)
        rows_ref[at, others] = jnp.where(own, away, sums).astype(rows_ref.dtype)
        copies.append(pltpu.make_async_copy(rows_ref.at[at], out_ref.at[at], sems.at[i]))
        copies[-1].start()
    for copy in copies:
        copy.wait()


def _finish_second(first, away, top, bottom, y2, x2):
    rows, tokens = first.shape
    return pl.pallas_call(
        _finish_second_kernel,
        out_shape=jax.ShapeDtypeStruct((rows, 2 * tokens), jnp.bfloat16),
        in_specs=[VMEM] * 6,
        out_specs=HBM,
        scratch_shapes=[pltpu.VMEM((rows, 2 * tokens), jnp.bfloat16), pltpu.SemaphoreType.DMA((4,))],
        compiler_params=pltpu.CompilerParams(vmem_limit_bytes=8 * 2**20),
        cost_estimate=pl.CostEstimate(flops=1, bytes_accessed=1, transcendentals=0),
        name="finish_second",
    )(first, away, top, bottom, y2, x2)


def _finish(kernel, out_shape, operands):
    return pl.pallas_call(
        kernel,
        out_shape=out_shape,
        in_specs=[VMEM] * len(operands),
        out_specs=jax.tree.map(lambda _: VMEM, out_shape),
        compiler_params=pltpu.CompilerParams(vmem_limit_bytes=8 * 2**20),
        cost_estimate=pl.CostEstimate(flops=1, bytes_accessed=1, transcendentals=0),
        name="finish",
    )(*operands)


def _flip(x, axis, bits):
    n = lax.axis_size(axis)
    return lax.ppermute(x, axis, [(i, i ^ bits) for i in range(n)])


def per_device_fast(queries, keys, values, out_weight, doc_lengths, owners):
    places = lax.axis_size("ctx")
    queries, keys, values, out_weight = (
        pltpu.with_memory_space_constraint(x, pltpu.HBM) for x in (queries, keys, values, out_weight))
    kv0 = _join_keys_values(keys, values)
    kv2 = lax.ppermute(kv0, "ctx", [(i, i + 2) for i in range(places - 2)])
    kv1 = _flip(kv0, "ctx", 1)
    meta = jnp.concatenate([owners.reshape(-1), doc_lengths])
    weights = {}
    leaving, queries, weights["xp"] = _queries_for_other_core(("xp",), meta, queries, out_weight)
    other = _flip(leaving, "ctx", 1)
    weights["yp"], weights["xf"] = _stage_weights(("yp", "xf"), out_weight, leaving)
    kv2, weights["xf"] = lax.optimization_barrier((kv2, weights["xf"]))
    kv = (kv0, kv1, kv2, _flip(kv2, "ctx", 1))
    loaded = ("yf", "py", "px")
    ctx0, ctx2, ctx1, ctx3, *loads = _attend_groups(
        (0, 2, 1, 3), loaded, doc_lengths.shape[0], meta, queries, other, kv, out_weight)
    weights.update(zip(loaded, loads))
    ctx1, ctx3 = _flip(ctx1, "ctx", 2), _flip(ctx3, "ctx", 6)

    xp, yp, joined = _join(ctx0, ctx2, weights)
    x1p, y1p = _flip(xp, "head", 1), _flip(yp, "head", 2)
    xf, yf = _two_rows("last_rows", joined, weights, ("xf", "yf"))
    x1f, y1f = _flip(xf, "head", 1), _flip(yf, "head", 2)
    weights["k0"], weights["k1"] = _stage_weights(("k0", "k1"), out_weight, joined)
    joined, weights["k0"], ctx1, ctx3 = lax.optimization_barrier((joined, weights["k0"], ctx1, ctx3))
    y2, x2 = _two_rows("pass_rows", joined, weights, ("py", "px"))
    y2, x2 = _add(y2, x1p), _add(x2, y1p)
    weights["xp"], y2, x2 = lax.optimization_barrier((weights["xp"], y2, x2))
    y2, x2 = _flip(y2, "head", 2), _flip(x2, "head", 1)

    xp, yp, joined2 = _join(ctx1, ctx3, weights)
    xp, yp, x1f, y1f = lax.optimization_barrier((xp, yp, x1f, y1f))
    next_x1p, next_y1p = _flip(xp, "head", 1), _flip(yp, "head", 2)
    xf, yf = _two_rows("last_rows", joined2, weights, ("xf", "yf"))
    next_x1f, next_y1f = _flip(xf, "head", 1), _flip(yf, "head", 2)
    keep, next_keep = _keep_rows(joined, joined2, weights)
    rows, tokens = keep.shape
    first, away = _finish(_finish_first_kernel, [
        jax.ShapeDtypeStruct((rows, tokens), jnp.bfloat16),
        jax.ShapeDtypeStruct((rows // 2, tokens), jnp.bfloat16),
    ], (keep, x1f, y1f, y2, x2))
    joined2, away = lax.optimization_barrier((joined2, away))
    away = _flip(away, "ctx", 4)
    y2, x2 = _two_rows("pass_rows", joined2, weights, ("py", "px"))
    y2, x2 = _add(y2, next_x1p), _add(x2, next_y1p)
    y2, x2 = _flip(y2, "head", 2), _flip(x2, "head", 1)
    away = _finish(_unpack_kernel, [jax.ShapeDtypeStruct((rows, tokens), jnp.bfloat16)], (away,))[0]
    away, next_keep = lax.optimization_barrier((away, next_keep))
    bottom = _half_sum(1, next_keep, next_y1f)
    bottom, next_keep = lax.optimization_barrier((bottom, next_keep))
    top = _half_sum(0, next_keep, next_x1f)
    return _finish_second(first, away, top, bottom, y2, x2)


def solution(mesh):
    in_specs = (P("ctx", "head"), P("ctx", "head"), P("ctx", "head"), P(None, "head"), P(), P())
    out_specs = P("head", "ctx")
    fast = mesh.shape["ctx"] == PIECES and mesh.shape["head"] == N_FAST_HEAD
    return jax.shard_map(
        per_device_fast if fast else per_device, mesh=mesh, in_specs=in_specs, out_specs=out_specs, check_vma=False
    )
```

```python
import functools
import math

import jax
import jax.numpy as jnp
from jax import lax
from jax.experimental import pallas as pl
from jax.experimental.pallas import tpu as pltpu
from jax.sharding import PartitionSpec as P

HEAD_SIZE = 128
PIECES = 8
N_FAST_HEAD = 4


MASKED = -1e30


def document_index(positions, doc_starts):
    return jnp.sum((positions[:, None] >= doc_starts[None, :]).astype(jnp.int32), axis=1) - 1


def attend(query_rows, query_pos, keys, values, doc_starts):
    row_count = query_rows.shape[0]
    key_heads = keys.shape[1] // HEAD_SIZE
    group_length = query_rows.shape[1] // keys.shape[1]
    query_heads = query_rows.reshape(row_count, key_heads, group_length, HEAD_SIZE)
    query_doc = document_index(query_pos, doc_starts)
    score_scale = 1.0 / math.sqrt(HEAD_SIZE)
    initial = (
        jnp.full((row_count, key_heads, group_length), MASKED, jnp.float32),
        jnp.zeros((row_count, key_heads, group_length), jnp.float32),
        jnp.zeros((row_count, key_heads, group_length, HEAD_SIZE), jnp.float32),
    )
    key_piece = lax.all_gather(keys, "ctx", axis=0, tiled=True)
    value_piece = lax.all_gather(values, "ctx", axis=0, tiled=True)
    piece_rows = key_piece.shape[0]
    tile_rows = math.gcd(piece_rows, 512)

    def one_tile(tile_index, running):
        tile_start = tile_index * tile_rows
        key_block = lax.dynamic_slice_in_dim(key_piece, tile_start, tile_rows, 0).reshape(
            tile_rows, key_heads, HEAD_SIZE
        )
        value_block = lax.dynamic_slice_in_dim(value_piece, tile_start, tile_rows, 0).reshape(
            tile_rows, key_heads, HEAD_SIZE
        )
        key_pos = tile_start + jnp.arange(tile_rows, dtype=jnp.int32)
        key_doc = document_index(key_pos, doc_starts)
        allowed = (query_doc[:, None] == key_doc[None, :]) & (
            key_pos[None, :] <= query_pos[:, None]
        )
        running_max, running_sum, weighted = running
        scores = (
            jnp.einsum("rkgd,nkd->rkgn", query_heads, key_block, preferred_element_type=jnp.float32)
            * score_scale
        )
        allowed_all = allowed[:, None, None, :]
        scores = jnp.where(allowed_all, scores, MASKED)
        new_max = jnp.maximum(running_max, jnp.max(scores, axis=-1))
        factor = jnp.exp(running_max - new_max)
        weights = jnp.where(allowed_all, jnp.exp(scores - new_max[..., None]), 0.0)
        new_sum = running_sum * factor + jnp.sum(weights, axis=-1)
        new_weighted = weighted * factor[..., None] + jnp.einsum(
            "rkgn,nkd->rkgd",
            weights.astype(jnp.bfloat16),
            value_block,
            preferred_element_type=jnp.float32,
        )
        return (new_max, new_sum, new_weighted)

    final_max, final_sum, weighted = lax.fori_loop(0, piece_rows // tile_rows, one_tile, initial)
    result = weighted / jnp.maximum(final_sum, 1.0)[..., None]
    return result.reshape(row_count, key_heads * group_length * HEAD_SIZE).astype(jnp.bfloat16)


def project(context, out_weight):
    return lax.psum_scatter(
        lax.dot_general(
            out_weight, context, (((1,), (1,)), ((), ())), preferred_element_type=jnp.float32
        ).astype(jnp.bfloat16),
        "head",
        scatter_dimension=0,
        tiled=True,
    )


def per_device(queries, keys, values, out_weight, doc_lengths, owners):
    place_count = lax.axis_size("ctx")
    own_index = lax.axis_index("ctx")
    token_count = queries.shape[0]
    block_rows = token_count // PIECES
    doc_ends = jnp.cumsum(doc_lengths)
    doc_starts = doc_ends - doc_lengths
    owner_table = owners[:, 0].reshape(place_count, PIECES)
    own_owners = lax.dynamic_index_in_dim(owner_table, own_index, 0, keepdims=False)
    place_ids = jnp.arange(place_count, dtype=jnp.int32)
    send_pick = (own_owners[None, :] == place_ids[:, None]).astype(jnp.bfloat16)
    grouped = queries.reshape(PIECES, block_rows, queries.shape[1])
    outgoing = jnp.einsum(
        "oc,chw->ohw", send_pick, grouped, preferred_element_type=jnp.float32
    ).astype(jnp.bfloat16)
    arrived = lax.all_to_all(outgoing, "ctx", split_axis=0, concat_axis=0, tiled=True)
    slot_hits = (owner_table == own_index).astype(jnp.int32)
    slot_live = jnp.sum(slot_hits, axis=1)
    picked = jnp.sum(slot_hits * jnp.arange(PIECES, dtype=jnp.int32)[None, :], axis=1)
    slot_pos = (place_ids[:, None] * PIECES + picked[:, None]) * block_rows + jnp.arange(
        block_rows, dtype=jnp.int32
    )[None, :]
    query_pos = jnp.where(slot_live[:, None] > 0, slot_pos, -1).reshape(-1)
    context = attend(
        arrived.reshape(place_count * block_rows, queries.shape[1]),
        query_pos,
        keys,
        values,
        doc_starts,
    )
    return project(context, out_weight)


SMEM = pl.BlockSpec(memory_space=pltpu.SMEM)
VMEM = pl.BlockSpec(memory_space=pltpu.VMEM)
HBM = pl.BlockSpec(memory_space=pltpu.HBM)
ANY = pl.BlockSpec(memory_space=pl.ANY)


def _own_ctx():
    return lax.axis_index("ctx")


def _own_z():
    return lax.div(_own_ctx(), 2)


def _find_piece(table_ref, source, owner):
    piece = jnp.int32(0)
    for i in range(PIECES):
        piece = jnp.where(table_ref[source * PIECES + i] == owner, jnp.int32(i), piece)
    return piece


def _rows(start, size):
    return pl.ds(pl.multiple_of(start, size), size)


def _join_keys_values_kernel(keys_ref, values_ref, out_ref, sems):
    rows = keys_ref.shape[0]
    copies = [
        pltpu.make_async_copy(keys_ref, out_ref.at[pl.ds(0, rows)], sems.at[0]),
        pltpu.make_async_copy(values_ref, out_ref.at[pl.ds(rows, rows)], sems.at[1]),
    ]
    for copy in copies:
        copy.start()
    for copy in copies:
        copy.wait()


def _join_keys_values(keys, values):
    return pl.pallas_call(
        _join_keys_values_kernel,
        out_shape=jax.ShapeDtypeStruct((2 * keys.shape[0], keys.shape[1]), keys.dtype),
        in_specs=[HBM] * 2,
        out_specs=VMEM,
        scratch_shapes=[pltpu.SemaphoreType.DMA((2,))],
        compiler_params=pltpu.CompilerParams(vmem_limit_bytes=2 * 2**20),
        cost_estimate=pl.CostEstimate(flops=1, bytes_accessed=1, transcendentals=0),
        name="join_keys_values",
    )(keys, values)


def _queries_for_other_core_kernel(names, meta_ref, queries_ref, w_ref, out_ref, kept_ref, *rest):
    *w_out, sem, w_sems, table_ref, table_sem = rest
    w_copies = _weight_copies(names, w_ref, w_out, w_sems)
    table_copy = pltpu.make_async_copy(meta_ref, table_ref, table_sem)
    table_copy.start()
    copy = pltpu.make_async_copy(queries_ref, kept_ref, sem)
    copy.start()
    for w_copy in w_copies:
        w_copy.start()
    copy.wait()
    table_copy.wait()
    c = _own_ctx()
    core = lax.rem(c, 2)
    rows = queries_ref.shape[0] // PIECES
    for j in range(PIECES // 2):
        piece = _find_piece(table_ref, c, 2 * j + 1 - core)
        out_ref[j * rows:(j + 1) * rows] = kept_ref[_rows(piece * rows, rows)]
    for w_copy in w_copies:
        w_copy.wait()


def _queries_for_other_core(names, meta, queries, out_weight):
    return pl.pallas_call(
        functools.partial(_queries_for_other_core_kernel, names),
        out_shape=[
            jax.ShapeDtypeStruct((queries.shape[0] // 2, queries.shape[1]), queries.dtype),
            jax.ShapeDtypeStruct(queries.shape, queries.dtype),
        ] + [_eighth(out_weight) for _ in names],
        in_specs=[ANY, HBM, HBM],
        out_specs=[VMEM] * (2 + len(names)),
        scratch_shapes=[
            pltpu.SemaphoreType.DMA, pltpu.SemaphoreType.DMA((len(names),)),
            pltpu.SMEM(meta.shape, meta.dtype), pltpu.SemaphoreType.DMA],
        compiler_params=pltpu.CompilerParams(vmem_limit_bytes=2 * 2**20),
        cost_estimate=pl.CostEstimate(flops=1, bytes_accessed=1, transcendentals=0),
        name="queries_for_other_core",
    )(meta, queries, out_weight)


EIGHTHS = {
    "xf": ("first", 0), "xp": ("both", 0), "yf": ("second", 1), "yp": ("both", 1),
    "py": ("second", 0), "px": ("first", 1), "k0": ("own", 0), "k1": ("own", 1),
}


def _neighbour(which, core):
    return {"own": 0, "first": 1 + core, "second": 2 - core, "both": 3}[which]


def _weight_copies(names, w_ref, out_refs, sems):
    half = w_ref.shape[0] // (2 * N_FAST_HEAD)
    copies = []
    for n, name in enumerate(names):
        which, side = EIGHTHS[name]
        flip = _neighbour(which, lax.rem(_own_ctx(), 2))
        row = (lax.axis_index("head") ^ flip) * (2 * half) + side * half
        copies.append(pltpu.make_async_copy(w_ref.at[_rows(row, half)], out_refs[n], sems.at[n]))
    return copies


def _eighth(out_weight):
    return jax.ShapeDtypeStruct((out_weight.shape[0] // (2 * N_FAST_HEAD), out_weight.shape[1]), out_weight.dtype)


def _stage_kernel(names, w_ref, after_ref, *rest):
    copies = _weight_copies(names, w_ref, rest[:-1], rest[-1])
    for copy in copies:
        copy.start()
    for copy in copies:
        copy.wait()


def _stage_weights(names, out_weight, after):
    return pl.pallas_call(
        functools.partial(_stage_kernel, names),
        out_shape=[_eighth(out_weight) for _ in names],
        in_specs=[HBM, VMEM],
        out_specs=[VMEM] * len(names),
        scratch_shapes=[pltpu.SemaphoreType.DMA((len(names),))],
        compiler_params=pltpu.CompilerParams(vmem_limit_bytes=8 * 2**20),
        cost_estimate=pl.CostEstimate(flops=1, bytes_accessed=1, transcendentals=0),
        name="stage_weights",
    )(out_weight, after)


def _attend_kernel(
    groups, names, documents, meta_ref, queries_ref, other_ref,
    kv0_ref, kv1_ref, kv2_ref, kv3_ref, w_ref,
    *rest,
):
    count = len(groups)
    out_refs, w_out = rest[:count], rest[count:count + len(names)]
    kbuf, vbuf, qbuf, ctxbuf, w_sems, table_ref, table_sem = rest[count + len(names):]
    table_copy = pltpu.make_async_copy(meta_ref, table_ref, table_sem)
    table_copy.start()
    w_copies = _weight_copies(names, w_ref, w_out, w_sems)
    for copy in w_copies:
        copy.start()
    c = _own_ctx()
    core = lax.rem(c, 2)
    z = lax.div(c, 2)
    rows = kv0_ref.shape[0] // 2
    piece_rows = rows // PIECES
    tile = 128
    heads = kv0_ref.shape[1] // HEAD_SIZE
    slots = (2 + core, 3 - core, core, 1 - core)
    for b, kv_ref in enumerate((kv0_ref, kv1_ref, kv2_ref, kv3_ref)):
        at = _rows(slots[b] * rows, rows)
        kbuf[at] = kv_ref[:rows]
        for kv in range(heads):
            vbuf[at, 2 * kv * HEAD_SIZE:(2 * kv + 1) * HEAD_SIZE] = (
                kv_ref[rows:, kv * HEAD_SIZE:(kv + 1) * HEAD_SIZE])
            vbuf[at, (2 * kv + 1) * HEAD_SIZE:(2 * kv + 2) * HEAD_SIZE] = jnp.ones((rows, HEAD_SIZE), jnp.bfloat16)
    table_copy.wait()
    starts = []
    for n, k in enumerate(groups):
        zdest = z ^ k
        owner = 2 * zdest + core
        mine = _find_piece(table_ref, c, owner)
        theirs = _find_piece(table_ref, c + 1 - 2 * core, owner)
        qbuf[2 * n + core] = queries_ref[_rows(mine * piece_rows, piece_rows)]
        qbuf[2 * n + 1 - core] = other_ref[_rows(zdest * piece_rows, piece_rows)]
        at0 = jnp.where(core == 0, mine, theirs)
        at1 = jnp.where(core == 0, theirs, mine)
        starts.append((at0 * piece_rows, rows + at1 * piece_rows))
    doc_start = []
    running = jnp.int32(0)
    lengths_at = PIECES * PIECES
    for d in range(lengths_at, lengths_at + documents):
        doc_start.append(running)
        running = running + table_ref[d]
    base = 2 * rows * (z - 1)
    group = queries_ref.shape[1] // kv0_ref.shape[1]
    scale = math.log2(math.e) / math.sqrt(HEAD_SIZE)

    def tiles_needed(p0):
        low = jnp.int32(0)
        for start in doc_start:
            low = jnp.where(2 * rows * z + p0 >= start, start, low)
        return lax.div(2 * rows * z + p0, tile) - lax.div(low, tile) + 1

    def piece_keys(p0, span):
        first = pl.multiple_of(lax.div(p0, tile) * tile + 2 * rows + tile - span, tile)
        pos = 2 * rows * z + p0 + lax.broadcasted_iota(jnp.int32, (piece_rows, 1), 0)
        low = jnp.zeros((piece_rows, 1), jnp.int32)
        for start in doc_start:
            low = jnp.where(pos >= start, start, low)
        key_pos = base + first + lax.broadcasted_iota(jnp.int32, (piece_rows, span), 1)
        return first, (key_pos >= low) & (key_pos <= pos)

    def some_pieces(pieces, span):
        units, scores, weights = [], [], []
        for n, p0 in pieces:
            first, allowed = piece_keys(p0, span)
            units += [(n, kv, first, allowed) for kv in range(heads)]
        for n, kv, first, allowed in units:
            q = jnp.concatenate(
                [qbuf[n, :, pl.ds((kv * group + g) * HEAD_SIZE, HEAD_SIZE)] for g in range(group)], axis=0)
            k = kbuf[pl.ds(first, span), pl.ds(kv * HEAD_SIZE, HEAD_SIZE)]
            scores.append(lax.dot_general(q, k, (((1,), (1,)), ((), ())), preferred_element_type=jnp.float32))
        for (n, kv, first, allowed), s in zip(units, scores):
            s = jnp.where(allowed[None], s.reshape(group, piece_rows, span), MASKED)
            w = jnp.exp2((s - jnp.max(s, axis=2, keepdims=True)) * scale)
            weights.append(w.astype(jnp.bfloat16).reshape(group * piece_rows, span))
        for (n, kv, first, allowed), w in zip(units, weights):
            o = jnp.dot(w, vbuf[pl.ds(first, span), pl.ds(kv * 2 * HEAD_SIZE, 2 * HEAD_SIZE)],
                        preferred_element_type=jnp.float32)
            o = (o[:, :HEAD_SIZE] / o[:, HEAD_SIZE:]).astype(jnp.bfloat16)
            for g in range(group):
                ctxbuf[n, :, pl.ds((kv * group + g) * HEAD_SIZE, HEAD_SIZE)] = o[g * piece_rows:(g + 1) * piece_rows]

    together = 2
    most_tiles = 5

    def step(i, carry):
        pieces = []
        for j in range(together):
            n = i * together + j
            p0 = starts[0][0]
            for m in range(1, 2 * count):
                p0 = jnp.where(n == m, starts[m // 2][m % 2], p0)
            pieces.append((n, p0))
        needed = functools.reduce(jnp.maximum, [tiles_needed(p0) for n, p0 in pieces])
        least = 0
        for tiles in range(1, most_tiles + 1):
            fits = needed > least if tiles == most_tiles else (needed > least) & (needed <= tiles)
            pl.when(fits)(functools.partial(some_pieces, pieces, tiles * tile))
            least = tiles
        return carry

    lax.fori_loop(0, 2 * count // together, step, 0)
    for n, out_ref in enumerate(out_refs):
        out_ref[...] = ctxbuf[2 * n:2 * n + 2].reshape(out_ref.shape)
    for copy in w_copies:
        copy.wait()


def _attend_groups(groups, names, documents, meta, queries, other, kv, out_weight):
    piece = queries.shape[0] // PIECES
    rows = kv[0].shape[0] // 2
    return pl.pallas_call(
        functools.partial(_attend_kernel, groups, names, documents),
        out_shape=[jax.ShapeDtypeStruct((2 * piece, queries.shape[1]), jnp.bfloat16) for _ in groups]
        + [_eighth(out_weight) for _ in names],
        in_specs=[ANY] + [VMEM] * 6 + [HBM],
        out_specs=[VMEM] * (len(groups) + len(names)),
        scratch_shapes=[
            pltpu.VMEM((4 * rows, kv[0].shape[1]), jnp.bfloat16),
            pltpu.VMEM((4 * rows, 2 * kv[0].shape[1]), jnp.bfloat16),
            pltpu.VMEM((2 * len(groups), piece, queries.shape[1]), jnp.bfloat16),
            pltpu.VMEM((2 * len(groups), piece, queries.shape[1]), jnp.bfloat16),
            pltpu.SemaphoreType.DMA((len(names),)),
            pltpu.SMEM(meta.shape, meta.dtype),
            pltpu.SemaphoreType.DMA,
        ],
        compiler_params=pltpu.CompilerParams(vmem_limit_bytes=12 * 2**20),
        cost_estimate=pl.CostEstimate(flops=1, bytes_accessed=1, transcendentals=0),
        name="attend_groups",
    )(meta, queries, other, *kv, out_weight)


def _dot_to(out_ref, weight_ref, tokens):
    out_ref[...] = jnp.dot(weight_ref[...], tokens, preferred_element_type=jnp.float32).astype(out_ref.dtype)


def _join_kernel(a_ref, b_ref, wx_ref, wy_ref, x_ref, y_ref, joined_ref, catbuf):
    second = lax.rem(_own_z(), 2)
    mid = a_ref.shape[0]
    catbuf[_rows(second * mid, mid)] = a_ref[...]
    catbuf[_rows((1 - second) * mid, mid)] = b_ref[...]
    joined = catbuf[...].T
    joined_ref[...] = joined
    _dot_to(x_ref, wx_ref, joined)
    _dot_to(y_ref, wy_ref, joined)


def _two_rows_kernel(joined_ref, w0_ref, w1_ref, out0_ref, out1_ref):
    joined = joined_ref[...]
    _dot_to(out0_ref, w0_ref, joined)
    _dot_to(out1_ref, w1_ref, joined)


def _keep_rows_kernel(first_ref, second_ref, w0_ref, w1_ref, first_out, second_out):
    half, tokens = w0_ref.shape[0], first_ref.shape[1]
    both = jnp.concatenate([first_ref[...], second_ref[...]], axis=1)
    for i, w_ref in enumerate((w0_ref, w1_ref)):
        out = jnp.dot(w_ref[...], both, preferred_element_type=jnp.float32).astype(first_out.dtype)
        first_out[i * half:(i + 1) * half] = out[:, :tokens]
        second_out[i * half:(i + 1) * half] = out[:, tokens:]


def _project(kernel, name, out_shape, operands, scratch=()):
    return pl.pallas_call(
        kernel,
        out_shape=out_shape,
        in_specs=[VMEM] * len(operands),
        out_specs=[VMEM] * len(out_shape),
        scratch_shapes=scratch,
        compiler_params=pltpu.CompilerParams(vmem_limit_bytes=8 * 2**20),
        cost_estimate=pl.CostEstimate(flops=1, bytes_accessed=1, transcendentals=0),
        name=name,
    )(*operands)


def _join(a, b, weights):
    (rows, depth), tokens = weights["xp"].shape, a.shape[0] + b.shape[0]
    part = jax.ShapeDtypeStruct((rows, tokens), jnp.bfloat16)
    return _project(
        _join_kernel, "join", [part] * 2 + [jax.ShapeDtypeStruct((depth, tokens), jnp.bfloat16)],
        (a, b, weights["xp"], weights["yp"]), [pltpu.VMEM((tokens, depth), jnp.bfloat16)])


def _two_rows(name, joined, weights, names):
    part = jax.ShapeDtypeStruct((weights[names[0]].shape[0], joined.shape[1]), jnp.bfloat16)
    return _project(_two_rows_kernel, name, [part] * 2, (joined, weights[names[0]], weights[names[1]]))


def _keep_rows(first, second, weights):
    part = jax.ShapeDtypeStruct((2 * weights["k0"].shape[0], first.shape[1]), jnp.bfloat16)
    return _project(_keep_rows_kernel, "keep_rows", [part] * 2, (first, second, weights["k0"], weights["k1"]))


def _add_kernel(a_ref, b_ref, out_ref):
    out_ref[...] = (a_ref[...].astype(jnp.float32) + b_ref[...].astype(jnp.float32)).astype(out_ref.dtype)


def _add(a, b):
    return _project(_add_kernel, "add", [jax.ShapeDtypeStruct(a.shape, jnp.bfloat16)], (a, b))[0]


def _sum_parts(keep_ref, x1_ref, y1_ref, y2_ref, x2_ref):
    half = y2_ref.shape[0]
    f32 = jnp.float32
    first = keep_ref[:half].astype(f32) + x1_ref[...].astype(f32) + y2_ref[...].astype(f32)
    second = keep_ref[half:].astype(f32) + y1_ref[...].astype(f32) + x2_ref[...].astype(f32)
    return first, second


def _own_half(rows, tokens):
    lane = lax.broadcasted_iota(jnp.int32, (rows, tokens), 1)
    return lax.div(lane, tokens // 2) == lax.rem(_own_z(), 2)


def _finish_first_kernel(keep_ref, x1_ref, y1_ref, y2_ref, x2_ref, out_ref, away_ref):
    half, tokens = y2_ref.shape
    top, bottom = _sum_parts(keep_ref, x1_ref, y1_ref, y2_ref, x2_ref)
    out_ref[:half] = top.astype(out_ref.dtype)
    out_ref[half:] = bottom.astype(out_ref.dtype)
    own = _own_half(half, tokens)
    away_ref[...] = jnp.where(own, pltpu.roll(bottom, tokens // 2, 1), top).astype(away_ref.dtype)


def _unpack_kernel(away_ref, out_ref):
    half, tokens = away_ref.shape
    out_ref[:half] = pltpu.roll(away_ref[...].astype(jnp.float32), tokens // 2, 1).astype(out_ref.dtype)
    out_ref[half:] = away_ref[...]


def _half_sum_kernel(side, keep_ref, one_ref, out_ref):
    half = one_ref.shape[0]
    out_ref[...] = keep_ref[side * half:(side + 1) * half].astype(jnp.float32) + one_ref[...].astype(jnp.float32)


def _half_sum(side, keep, one):
    return _finish(functools.partial(_half_sum_kernel, side), [jax.ShapeDtypeStruct(one.shape, jnp.float32)], (keep, one))[0]


def _finish_second_kernel(first_ref, away_ref, top_ref, bottom_ref, y2_ref, x2_ref, out_ref, rows_ref, sems):
    half, tokens = y2_ref.shape
    part = half // 2
    upper = lax.div(_own_z(), 2)
    mine, others = _rows(upper * tokens, tokens), _rows((1 - upper) * tokens, tokens)
    own = _own_half(part, tokens)
    copies = []
    for i in range(4):
        at, inside = pl.ds(i * part, part), pl.ds(i % 2 * part, part)
        one_ref, two_ref = (top_ref, y2_ref) if i < 2 else (bottom_ref, x2_ref)
        sums = one_ref[inside] + two_ref[inside].astype(jnp.float32)
        first, away = first_ref[at].astype(jnp.float32), away_ref[at].astype(jnp.float32)
        rows_ref[at, mine] = jnp.where(own, first, pltpu.roll(sums, tokens // 2, 1)).astype(rows_ref.dtype)
        rows_ref[at, others] = jnp.where(own, away, sums).astype(rows_ref.dtype)
        copies.append(pltpu.make_async_copy(rows_ref.at[at], out_ref.at[at], sems.at[i]))
        copies[-1].start()
    for copy in copies:
        copy.wait()


def _finish_second(first, away, top, bottom, y2, x2):
    rows, tokens = first.shape
    return pl.pallas_call(
        _finish_second_kernel,
        out_shape=jax.ShapeDtypeStruct((rows, 2 * tokens), jnp.bfloat16),
        in_specs=[VMEM] * 6,
        out_specs=HBM,
        scratch_shapes=[pltpu.VMEM((rows, 2 * tokens), jnp.bfloat16), pltpu.SemaphoreType.DMA((4,))],
        compiler_params=pltpu.CompilerParams(vmem_limit_bytes=8 * 2**20),
        cost_estimate=pl.CostEstimate(flops=1, bytes_accessed=1, transcendentals=0),
        name="finish_second",
    )(first, away, top, bottom, y2, x2)


def _finish(kernel, out_shape, operands):
    return pl.pallas_call(
        kernel,
        out_shape=out_shape,
        in_specs=[VMEM] * len(operands),
        out_specs=jax.tree.map(lambda _: VMEM, out_shape),
        compiler_params=pltpu.CompilerParams(vmem_limit_bytes=8 * 2**20),
        cost_estimate=pl.CostEstimate(flops=1, bytes_accessed=1, transcendentals=0),
        name="finish",
    )(*operands)


def _flip(x, axis, bits):
    n = lax.axis_size(axis)
    return lax.ppermute(x, axis, [(i, i ^ bits) for i in range(n)])


def _swap(x, which):
    places, heads = lax.axis_size("ctx"), lax.axis_size("head")
    pairs = [(c * heads + h, c * heads + (h ^ _neighbour(which, c % 2))) for c in range(places) for h in range(heads)]
    return lax.ppermute(x, ("ctx", "head"), pairs)


def per_device_fast(queries, keys, values, out_weight, doc_lengths, owners):
    places = lax.axis_size("ctx")
    queries, keys, values, out_weight = (
        pltpu.with_memory_space_constraint(x, pltpu.HBM) for x in (queries, keys, values, out_weight))
    kv0 = _join_keys_values(keys, values)
    kv2 = lax.ppermute(kv0, "ctx", [(i, i + 2) for i in range(places - 2)])
    kv1 = _flip(kv0, "ctx", 1)
    meta = jnp.concatenate([owners.reshape(-1), doc_lengths])
    weights = {}
    leaving, queries, weights["xp"] = _queries_for_other_core(("xp",), meta, queries, out_weight)
    other = _flip(leaving, "ctx", 1)
    weights["yp"], weights["xf"] = _stage_weights(("yp", "xf"), out_weight, leaving)
    kv2, weights["xf"] = lax.optimization_barrier((kv2, weights["xf"]))
    kv = (kv0, kv1, kv2, _flip(kv2, "ctx", 1))
    loaded = ("yf", "py", "px")
    ctx0, ctx2, ctx1, ctx3, *loads = _attend_groups(
        (0, 2, 1, 3), loaded, doc_lengths.shape[0], meta, queries, other, kv, out_weight)
    weights.update(zip(loaded, loads))
    ctx1, ctx3 = _flip(ctx1, "ctx", 2), _flip(ctx3, "ctx", 6)

    xp, yp, joined = _join(ctx0, ctx2, weights)
    x1p, y1p = _swap(xp, "first"), _swap(yp, "second")
    xf, yf = _two_rows("last_rows", joined, weights, ("xf", "yf"))
    x1f, y1f = _swap(xf, "first"), _swap(yf, "second")
    weights["k0"], weights["k1"] = _stage_weights(("k0", "k1"), out_weight, joined)
    joined, weights["k0"], ctx1, ctx3 = lax.optimization_barrier((joined, weights["k0"], ctx1, ctx3))
    y2, x2 = _two_rows("pass_rows", joined, weights, ("py", "px"))
    y2, x2 = _add(y2, x1p), _add(x2, y1p)
    weights["xp"], y2, x2 = lax.optimization_barrier((weights["xp"], y2, x2))
    y2, x2 = _swap(y2, "second"), _swap(x2, "first")

    xp, yp, joined2 = _join(ctx1, ctx3, weights)
    xp, yp, x1f, y1f = lax.optimization_barrier((xp, yp, x1f, y1f))
    next_x1p, next_y1p = _swap(xp, "first"), _swap(yp, "second")
    xf, yf = _two_rows("last_rows", joined2, weights, ("xf", "yf"))
    next_x1f, next_y1f = _swap(xf, "first"), _swap(yf, "second")
    keep, next_keep = _keep_rows(joined, joined2, weights)
    rows, tokens = keep.shape
    first, away = _finish(_finish_first_kernel, [
        jax.ShapeDtypeStruct((rows, tokens), jnp.bfloat16),
        jax.ShapeDtypeStruct((rows // 2, tokens), jnp.bfloat16),
    ], (keep, x1f, y1f, y2, x2))
    joined2, away = lax.optimization_barrier((joined2, away))
    away = _flip(away, "ctx", 4)
    y2, x2 = _two_rows("pass_rows", joined2, weights, ("py", "px"))
    y2, x2 = _add(y2, next_x1p), _add(x2, next_y1p)
    y2, x2 = _swap(y2, "second"), _swap(x2, "first")
    away = _finish(_unpack_kernel, [jax.ShapeDtypeStruct((rows, tokens), jnp.bfloat16)], (away,))[0]
    away, next_keep = lax.optimization_barrier((away, next_keep))
    bottom = _half_sum(1, next_keep, next_y1f)
    bottom, next_keep = lax.optimization_barrier((bottom, next_keep))
    top = _half_sum(0, next_keep, next_x1f)
    return _finish_second(first, away, top, bottom, y2, x2)


def solution(mesh):
    in_specs = (P("ctx", "head"), P("ctx", "head"), P("ctx", "head"), P(None, "head"), P(), P())
    out_specs = P("head", "ctx")
    fast = mesh.shape["ctx"] == PIECES and mesh.shape["head"] == N_FAST_HEAD
    return jax.shard_map(
        per_device_fast if fast else per_device, mesh=mesh, in_specs=in_specs, out_specs=out_specs, check_vma=False
    )
```

```python
import functools
import math

import jax
import jax.numpy as jnp
from jax import lax
from jax.experimental import pallas as pl
from jax.experimental.pallas import tpu as pltpu
from jax.sharding import PartitionSpec as P

HEAD_SIZE = 128
PIECES = 8
N_FAST_HEAD = 4


MASKED = -1e30


def document_index(positions, doc_starts):
    return jnp.sum((positions[:, None] >= doc_starts[None, :]).astype(jnp.int32), axis=1) - 1


def attend(query_rows, query_pos, keys, values, doc_starts):
    row_count = query_rows.shape[0]
    key_heads = keys.shape[1] // HEAD_SIZE
    group_length = query_rows.shape[1] // keys.shape[1]
    query_heads = query_rows.reshape(row_count, key_heads, group_length, HEAD_SIZE)
    query_doc = document_index(query_pos, doc_starts)
    score_scale = 1.0 / math.sqrt(HEAD_SIZE)
    initial = (
        jnp.full((row_count, key_heads, group_length), MASKED, jnp.float32),
        jnp.zeros((row_count, key_heads, group_length), jnp.float32),
        jnp.zeros((row_count, key_heads, group_length, HEAD_SIZE), jnp.float32),
    )
    key_piece = lax.all_gather(keys, "ctx", axis=0, tiled=True)
    value_piece = lax.all_gather(values, "ctx", axis=0, tiled=True)
    piece_rows = key_piece.shape[0]
    tile_rows = math.gcd(piece_rows, 512)

    def one_tile(tile_index, running):
        tile_start = tile_index * tile_rows
        key_block = lax.dynamic_slice_in_dim(key_piece, tile_start, tile_rows, 0).reshape(
            tile_rows, key_heads, HEAD_SIZE
        )
        value_block = lax.dynamic_slice_in_dim(value_piece, tile_start, tile_rows, 0).reshape(
            tile_rows, key_heads, HEAD_SIZE
        )
        key_pos = tile_start + jnp.arange(tile_rows, dtype=jnp.int32)
        key_doc = document_index(key_pos, doc_starts)
        allowed = (query_doc[:, None] == key_doc[None, :]) & (
            key_pos[None, :] <= query_pos[:, None]
        )
        running_max, running_sum, weighted = running
        scores = (
            jnp.einsum("rkgd,nkd->rkgn", query_heads, key_block, preferred_element_type=jnp.float32)
            * score_scale
        )
        allowed_all = allowed[:, None, None, :]
        scores = jnp.where(allowed_all, scores, MASKED)
        new_max = jnp.maximum(running_max, jnp.max(scores, axis=-1))
        factor = jnp.exp(running_max - new_max)
        weights = jnp.where(allowed_all, jnp.exp(scores - new_max[..., None]), 0.0)
        new_sum = running_sum * factor + jnp.sum(weights, axis=-1)
        new_weighted = weighted * factor[..., None] + jnp.einsum(
            "rkgn,nkd->rkgd",
            weights.astype(jnp.bfloat16),
            value_block,
            preferred_element_type=jnp.float32,
        )
        return (new_max, new_sum, new_weighted)

    final_max, final_sum, weighted = lax.fori_loop(0, piece_rows // tile_rows, one_tile, initial)
    result = weighted / jnp.maximum(final_sum, 1.0)[..., None]
    return result.reshape(row_count, key_heads * group_length * HEAD_SIZE).astype(jnp.bfloat16)


def project(context, out_weight):
    return lax.psum_scatter(
        lax.dot_general(
            out_weight, context, (((1,), (1,)), ((), ())), preferred_element_type=jnp.float32
        ).astype(jnp.bfloat16),
        "head",
        scatter_dimension=0,
        tiled=True,
    )


def per_device(queries, keys, values, out_weight, doc_lengths, owners):
    place_count = lax.axis_size("ctx")
    own_index = lax.axis_index("ctx")
    token_count = queries.shape[0]
    block_rows = token_count // PIECES
    doc_ends = jnp.cumsum(doc_lengths)
    doc_starts = doc_ends - doc_lengths
    owner_table = owners[:, 0].reshape(place_count, PIECES)
    own_owners = lax.dynamic_index_in_dim(owner_table, own_index, 0, keepdims=False)
    place_ids = jnp.arange(place_count, dtype=jnp.int32)
    send_pick = (own_owners[None, :] == place_ids[:, None]).astype(jnp.bfloat16)
    grouped = queries.reshape(PIECES, block_rows, queries.shape[1])
    outgoing = jnp.einsum(
        "oc,chw->ohw", send_pick, grouped, preferred_element_type=jnp.float32
    ).astype(jnp.bfloat16)
    arrived = lax.all_to_all(outgoing, "ctx", split_axis=0, concat_axis=0, tiled=True)
    slot_hits = (owner_table == own_index).astype(jnp.int32)
    slot_live = jnp.sum(slot_hits, axis=1)
    picked = jnp.sum(slot_hits * jnp.arange(PIECES, dtype=jnp.int32)[None, :], axis=1)
    slot_pos = (place_ids[:, None] * PIECES + picked[:, None]) * block_rows + jnp.arange(
        block_rows, dtype=jnp.int32
    )[None, :]
    query_pos = jnp.where(slot_live[:, None] > 0, slot_pos, -1).reshape(-1)
    context = attend(
        arrived.reshape(place_count * block_rows, queries.shape[1]),
        query_pos,
        keys,
        values,
        doc_starts,
    )
    return project(context, out_weight)


SMEM = pl.BlockSpec(memory_space=pltpu.SMEM)
VMEM = pl.BlockSpec(memory_space=pltpu.VMEM)
HBM = pl.BlockSpec(memory_space=pltpu.HBM)
ANY = pl.BlockSpec(memory_space=pl.ANY)


def _own_ctx():
    return lax.axis_index("ctx")


def _own_z():
    return lax.div(_own_ctx(), 2)


def _find_piece(table_ref, source, owner):
    piece = jnp.int32(0)
    for i in range(PIECES):
        piece = jnp.where(table_ref[source * PIECES + i] == owner, jnp.int32(i), piece)
    return piece


def _rows(start, size):
    return pl.ds(pl.multiple_of(start, size), size)


def _join_keys_values_kernel(keys_ref, values_ref, out_ref, sems):
    rows = keys_ref.shape[0]
    copies = [
        pltpu.make_async_copy(keys_ref, out_ref.at[pl.ds(0, rows)], sems.at[0]),
        pltpu.make_async_copy(values_ref, out_ref.at[pl.ds(rows, rows)], sems.at[1]),
    ]
    for copy in copies:
        copy.start()
    for copy in copies:
        copy.wait()


def _join_keys_values(keys, values):
    return pl.pallas_call(
        _join_keys_values_kernel,
        out_shape=jax.ShapeDtypeStruct((2 * keys.shape[0], keys.shape[1]), keys.dtype),
        in_specs=[HBM] * 2,
        out_specs=VMEM,
        scratch_shapes=[pltpu.SemaphoreType.DMA((2,))],
        compiler_params=pltpu.CompilerParams(vmem_limit_bytes=2 * 2**20),
        cost_estimate=pl.CostEstimate(flops=1, bytes_accessed=1, transcendentals=0),
        name="join_keys_values",
    )(keys, values)


def _queries_for_other_core_kernel(names, meta_ref, queries_ref, w_ref, out_ref, kept_ref, *rest):
    *w_out, sem, w_sems, table_ref, table_sem = rest
    w_copies = _weight_copies(names, w_ref, w_out, w_sems)
    table_copy = pltpu.make_async_copy(meta_ref, table_ref, table_sem)
    table_copy.start()
    copy = pltpu.make_async_copy(queries_ref, kept_ref, sem)
    copy.start()
    for w_copy in w_copies:
        w_copy.start()
    copy.wait()
    table_copy.wait()
    c = _own_ctx()
    core = lax.rem(c, 2)
    rows = queries_ref.shape[0] // PIECES
    for j in range(PIECES // 2):
        piece = _find_piece(table_ref, c, 2 * j + 1 - core)
        out_ref[j * rows:(j + 1) * rows] = kept_ref[_rows(piece * rows, rows)]
    for w_copy in w_copies:
        w_copy.wait()


def _queries_for_other_core(names, meta, queries, out_weight):
    return pl.pallas_call(
        functools.partial(_queries_for_other_core_kernel, names),
        out_shape=[
            jax.ShapeDtypeStruct((queries.shape[0] // 2, queries.shape[1]), queries.dtype),
            jax.ShapeDtypeStruct(queries.shape, queries.dtype),
        ] + [_eighth(out_weight) for _ in names],
        in_specs=[ANY, HBM, HBM],
        out_specs=[VMEM] * (2 + len(names)),
        scratch_shapes=[
            pltpu.SemaphoreType.DMA, pltpu.SemaphoreType.DMA((len(names),)),
            pltpu.SMEM(meta.shape, meta.dtype), pltpu.SemaphoreType.DMA],
        compiler_params=pltpu.CompilerParams(vmem_limit_bytes=2 * 2**20),
        cost_estimate=pl.CostEstimate(flops=1, bytes_accessed=1, transcendentals=0),
        name="queries_for_other_core",
    )(meta, queries, out_weight)


EIGHTHS = {
    "xf": (1, 0), "xp": (3, 0), "yf": (2, 1), "yp": (3, 1), "py": (2, 0), "px": (1, 1), "k0": (0, 0), "k1": (0, 1),
}


def _weight_copies(names, w_ref, out_refs, sems):
    half = w_ref.shape[0] // (2 * N_FAST_HEAD)
    copies = []
    for n, name in enumerate(names):
        flip, side = EIGHTHS[name]
        row = (lax.axis_index("head") ^ flip) * (2 * half) + side * half
        copies.append(pltpu.make_async_copy(w_ref.at[_rows(row, half)], out_refs[n], sems.at[n]))
    return copies


def _eighth(out_weight):
    return jax.ShapeDtypeStruct((out_weight.shape[0] // (2 * N_FAST_HEAD), out_weight.shape[1]), out_weight.dtype)


def _stage_kernel(names, w_ref, after_ref, *rest):
    copies = _weight_copies(names, w_ref, rest[:-1], rest[-1])
    for copy in copies:
        copy.start()
    for copy in copies:
        copy.wait()


def _stage_weights(names, out_weight, after):
    return pl.pallas_call(
        functools.partial(_stage_kernel, names),
        out_shape=[_eighth(out_weight) for _ in names],
        in_specs=[HBM, VMEM],
        out_specs=[VMEM] * len(names),
        scratch_shapes=[pltpu.SemaphoreType.DMA((len(names),))],
        compiler_params=pltpu.CompilerParams(vmem_limit_bytes=8 * 2**20),
        cost_estimate=pl.CostEstimate(flops=1, bytes_accessed=1, transcendentals=0),
        name="stage_weights",
    )(out_weight, after)


def _attend_kernel(
    groups, names, documents, meta_ref, queries_ref, other_ref,
    kv0_ref, kv1_ref, kv2_ref, kv3_ref, w_ref,
    *rest,
):
    count = len(groups)
    out_refs, w_out = rest[:count], rest[count:count + len(names)]
    kbuf, vbuf, qbuf, ctxbuf, w_sems, table_ref, table_sem = rest[count + len(names):]
    table_copy = pltpu.make_async_copy(meta_ref, table_ref, table_sem)
    table_copy.start()
    w_copies = _weight_copies(names, w_ref, w_out, w_sems)
    for copy in w_copies:
        copy.start()
    c = _own_ctx()
    core = lax.rem(c, 2)
    z = lax.div(c, 2)
    rows = kv0_ref.shape[0] // 2
    piece_rows = rows // PIECES
    tile = 128
    heads = kv0_ref.shape[1] // HEAD_SIZE
    slots = (2 + core, 3 - core, core, 1 - core)
    for b, kv_ref in enumerate((kv0_ref, kv1_ref, kv2_ref, kv3_ref)):
        at = _rows(slots[b] * rows, rows)
        kbuf[at] = kv_ref[:rows]
        for kv in range(heads):
            vbuf[at, 2 * kv * HEAD_SIZE:(2 * kv + 1) * HEAD_SIZE] = (
                kv_ref[rows:, kv * HEAD_SIZE:(kv + 1) * HEAD_SIZE])
            vbuf[at, (2 * kv + 1) * HEAD_SIZE:(2 * kv + 2) * HEAD_SIZE] = jnp.ones((rows, HEAD_SIZE), jnp.bfloat16)
    table_copy.wait()
    starts = []
    for n, k in enumerate(groups):
        zdest = z ^ k
        owner = 2 * zdest + core
        mine = _find_piece(table_ref, c, owner)
        theirs = _find_piece(table_ref, c + 1 - 2 * core, owner)
        qbuf[2 * n + core] = queries_ref[_rows(mine * piece_rows, piece_rows)]
        qbuf[2 * n + 1 - core] = other_ref[_rows(zdest * piece_rows, piece_rows)]
        at0 = jnp.where(core == 0, mine, theirs)
        at1 = jnp.where(core == 0, theirs, mine)
        starts.append((at0 * piece_rows, rows + at1 * piece_rows))
    doc_start = []
    running = jnp.int32(0)
    lengths_at = PIECES * PIECES
    for d in range(lengths_at, lengths_at + documents):
        doc_start.append(running)
        running = running + table_ref[d]
    base = 2 * rows * (z - 1)
    group = queries_ref.shape[1] // kv0_ref.shape[1]
    scale = math.log2(math.e) / math.sqrt(HEAD_SIZE)

    def tiles_needed(p0):
        low = jnp.int32(0)
        for start in doc_start:
            low = jnp.where(2 * rows * z + p0 >= start, start, low)
        return lax.div(2 * rows * z + p0, tile) - lax.div(low, tile) + 1

    def piece_keys(p0, span):
        first = pl.multiple_of(lax.div(p0, tile) * tile + 2 * rows + tile - span, tile)
        pos = 2 * rows * z + p0 + lax.broadcasted_iota(jnp.int32, (piece_rows, 1), 0)
        low = jnp.zeros((piece_rows, 1), jnp.int32)
        for start in doc_start:
            low = jnp.where(pos >= start, start, low)
        key_pos = base + first + lax.broadcasted_iota(jnp.int32, (piece_rows, span), 1)
        return first, (key_pos >= low) & (key_pos <= pos)

    def some_pieces(pieces, span):
        units, scores, weights = [], [], []
        for n, p0 in pieces:
            first, allowed = piece_keys(p0, span)
            units += [(n, kv, first, allowed) for kv in range(heads)]
        for n, kv, first, allowed in units:
            q = jnp.concatenate(
                [qbuf[n, :, pl.ds((kv * group + g) * HEAD_SIZE, HEAD_SIZE)] for g in range(group)], axis=0)
            k = kbuf[pl.ds(first, span), pl.ds(kv * HEAD_SIZE, HEAD_SIZE)]
            scores.append(lax.dot_general(q, k, (((1,), (1,)), ((), ())), preferred_element_type=jnp.float32))
        for (n, kv, first, allowed), s in zip(units, scores):
            s = jnp.where(allowed[None], s.reshape(group, piece_rows, span), MASKED)
            w = jnp.exp2((s - jnp.max(s, axis=2, keepdims=True)) * scale)
            weights.append(w.astype(jnp.bfloat16).reshape(group * piece_rows, span))
        for (n, kv, first, allowed), w in zip(units, weights):
            o = jnp.dot(w, vbuf[pl.ds(first, span), pl.ds(kv * 2 * HEAD_SIZE, 2 * HEAD_SIZE)],
                        preferred_element_type=jnp.float32)
            o = (o[:, :HEAD_SIZE] / o[:, HEAD_SIZE:]).astype(jnp.bfloat16)
            for g in range(group):
                ctxbuf[n, :, pl.ds((kv * group + g) * HEAD_SIZE, HEAD_SIZE)] = o[g * piece_rows:(g + 1) * piece_rows]

    together = 2
    most_tiles = 5

    def step(i, carry):
        pieces = []
        for j in range(together):
            n = i * together + j
            p0 = starts[0][0]
            for m in range(1, 2 * count):
                p0 = jnp.where(n == m, starts[m // 2][m % 2], p0)
            pieces.append((n, p0))
        needed = functools.reduce(jnp.maximum, [tiles_needed(p0) for n, p0 in pieces])
        least = 0
        for tiles in (2, 3, most_tiles):
            fits = needed > least if tiles == most_tiles else (needed > least) & (needed <= tiles)
            pl.when(fits)(functools.partial(some_pieces, pieces, tiles * tile))
            least = tiles
        return carry

    lax.fori_loop(0, 2 * count // together, step, 0)
    for n, out_ref in enumerate(out_refs):
        out_ref[...] = ctxbuf[2 * n:2 * n + 2].reshape(out_ref.shape)
    for copy in w_copies:
        copy.wait()


def _attend_groups(groups, names, documents, meta, queries, other, kv, out_weight):
    piece = queries.shape[0] // PIECES
    rows = kv[0].shape[0] // 2
    return pl.pallas_call(
        functools.partial(_attend_kernel, groups, names, documents),
        out_shape=[jax.ShapeDtypeStruct((2 * piece, queries.shape[1]), jnp.bfloat16) for _ in groups]
        + [_eighth(out_weight) for _ in names],
        in_specs=[ANY] + [VMEM] * 6 + [HBM],
        out_specs=[VMEM] * (len(groups) + len(names)),
        scratch_shapes=[
            pltpu.VMEM((4 * rows, kv[0].shape[1]), jnp.bfloat16),
            pltpu.VMEM((4 * rows, 2 * kv[0].shape[1]), jnp.bfloat16),
            pltpu.VMEM((2 * len(groups), piece, queries.shape[1]), jnp.bfloat16),
            pltpu.VMEM((2 * len(groups), piece, queries.shape[1]), jnp.bfloat16),
            pltpu.SemaphoreType.DMA((len(names),)),
            pltpu.SMEM(meta.shape, meta.dtype),
            pltpu.SemaphoreType.DMA,
        ],
        compiler_params=pltpu.CompilerParams(vmem_limit_bytes=12 * 2**20),
        cost_estimate=pl.CostEstimate(flops=1, bytes_accessed=1, transcendentals=0),
        name="attend_groups",
    )(meta, queries, other, *kv, out_weight)


def _dot_to(out_ref, weight_ref, tokens):
    out_ref[...] = jnp.dot(weight_ref[...], tokens, preferred_element_type=jnp.float32).astype(out_ref.dtype)


def _join_kernel(a_ref, b_ref, wx_ref, wy_ref, x_ref, y_ref, joined_ref, catbuf):
    second = lax.rem(_own_z(), 2)
    mid = a_ref.shape[0]
    catbuf[_rows(second * mid, mid)] = a_ref[...]
    catbuf[_rows((1 - second) * mid, mid)] = b_ref[...]
    joined = catbuf[...].T
    joined_ref[...] = joined
    _dot_to(x_ref, wx_ref, joined)
    _dot_to(y_ref, wy_ref, joined)


def _two_rows_kernel(joined_ref, w0_ref, w1_ref, out0_ref, out1_ref):
    joined = joined_ref[...]
    _dot_to(out0_ref, w0_ref, joined)
    _dot_to(out1_ref, w1_ref, joined)


def _keep_rows_kernel(first_ref, second_ref, w0_ref, w1_ref, first_out, second_out):
    half, tokens = w0_ref.shape[0], first_ref.shape[1]
    both = jnp.concatenate([first_ref[...], second_ref[...]], axis=1)
    for i, w_ref in enumerate((w0_ref, w1_ref)):
        out = jnp.dot(w_ref[...], both, preferred_element_type=jnp.float32).astype(first_out.dtype)
        first_out[i * half:(i + 1) * half] = out[:, :tokens]
        second_out[i * half:(i + 1) * half] = out[:, tokens:]


def _project(kernel, name, out_shape, operands, scratch=()):
    return pl.pallas_call(
        kernel,
        out_shape=out_shape,
        in_specs=[VMEM] * len(operands),
        out_specs=[VMEM] * len(out_shape),
        scratch_shapes=scratch,
        compiler_params=pltpu.CompilerParams(vmem_limit_bytes=8 * 2**20),
        cost_estimate=pl.CostEstimate(flops=1, bytes_accessed=1, transcendentals=0),
        name=name,
    )(*operands)


def _join(a, b, weights):
    (rows, depth), tokens = weights["xp"].shape, a.shape[0] + b.shape[0]
    part = jax.ShapeDtypeStruct((rows, tokens), jnp.bfloat16)
    return _project(
        _join_kernel, "join", [part] * 2 + [jax.ShapeDtypeStruct((depth, tokens), jnp.bfloat16)],
        (a, b, weights["xp"], weights["yp"]), [pltpu.VMEM((tokens, depth), jnp.bfloat16)])


def _two_rows(name, joined, weights, names):
    part = jax.ShapeDtypeStruct((weights[names[0]].shape[0], joined.shape[1]), jnp.bfloat16)
    return _project(_two_rows_kernel, name, [part] * 2, (joined, weights[names[0]], weights[names[1]]))


def _keep_rows(first, second, weights):
    part = jax.ShapeDtypeStruct((2 * weights["k0"].shape[0], first.shape[1]), jnp.bfloat16)
    return _project(_keep_rows_kernel, "keep_rows", [part] * 2, (first, second, weights["k0"], weights["k1"]))


def _add_kernel(a_ref, b_ref, out_ref):
    out_ref[...] = (a_ref[...].astype(jnp.float32) + b_ref[...].astype(jnp.float32)).astype(out_ref.dtype)


def _add(a, b):
    return _project(_add_kernel, "add", [jax.ShapeDtypeStruct(a.shape, jnp.bfloat16)], (a, b))[0]


def _sum_parts(keep_ref, x1_ref, y1_ref, y2_ref, x2_ref):
    half = y2_ref.shape[0]
    f32 = jnp.float32
    first = keep_ref[:half].astype(f32) + x1_ref[...].astype(f32) + y2_ref[...].astype(f32)
    second = keep_ref[half:].astype(f32) + y1_ref[...].astype(f32) + x2_ref[...].astype(f32)
    return first, second


def _own_half(rows, tokens):
    lane = lax.broadcasted_iota(jnp.int32, (rows, tokens), 1)
    return lax.div(lane, tokens // 2) == lax.rem(_own_z(), 2)


def _finish_first_kernel(keep_ref, x1_ref, y1_ref, y2_ref, x2_ref, out_ref, away_ref):
    half, tokens = y2_ref.shape
    top, bottom = _sum_parts(keep_ref, x1_ref, y1_ref, y2_ref, x2_ref)
    out_ref[:half] = top.astype(out_ref.dtype)
    out_ref[half:] = bottom.astype(out_ref.dtype)
    own = _own_half(half, tokens)
    away_ref[...] = jnp.where(own, pltpu.roll(bottom, tokens // 2, 1), top).astype(away_ref.dtype)


def _unpack_kernel(away_ref, out_ref):
    half, tokens = away_ref.shape
    out_ref[:half] = pltpu.roll(away_ref[...].astype(jnp.float32), tokens // 2, 1).astype(out_ref.dtype)
    out_ref[half:] = away_ref[...]


def _half_sum_kernel(side, keep_ref, one_ref, out_ref):
    half = one_ref.shape[0]
    out_ref[...] = keep_ref[side * half:(side + 1) * half].astype(jnp.float32) + one_ref[...].astype(jnp.float32)


def _half_sum(side, keep, one):
    return _finish(functools.partial(_half_sum_kernel, side), [jax.ShapeDtypeStruct(one.shape, jnp.float32)], (keep, one))[0]


def _finish_second_kernel(first_ref, away_ref, top_ref, bottom_ref, y2_ref, x2_ref, out_ref, rows_ref, sems):
    half, tokens = y2_ref.shape
    part = half // 4
    upper = lax.div(_own_z(), 2)
    mine, others = _rows(upper * tokens, tokens), _rows((1 - upper) * tokens, tokens)
    own = _own_half(part, tokens)
    copies = []
    for i in range(8):
        at, inside = pl.ds(i * part, part), pl.ds(i % 4 * part, part)
        one_ref, two_ref = (top_ref, y2_ref) if i < 4 else (bottom_ref, x2_ref)
        sums = one_ref[inside] + two_ref[inside].astype(jnp.float32)
        first, away = first_ref[at].astype(jnp.float32), away_ref[at].astype(jnp.float32)
        rows_ref[at, mine] = jnp.where(own, first, pltpu.roll(sums, tokens // 2, 1)).astype(rows_ref.dtype)
        rows_ref[at, others] = jnp.where(own, away, sums).astype(rows_ref.dtype)
        copies.append(pltpu.make_async_copy(rows_ref.at[at], out_ref.at[at], sems.at[i]))
        copies[-1].start()
    for copy in copies:
        copy.wait()


def _finish_second(first, away, top, bottom, y2, x2):
    rows, tokens = first.shape
    return pl.pallas_call(
        _finish_second_kernel,
        out_shape=jax.ShapeDtypeStruct((rows, 2 * tokens), jnp.bfloat16),
        in_specs=[VMEM] * 6,
        out_specs=HBM,
        scratch_shapes=[pltpu.VMEM((rows, 2 * tokens), jnp.bfloat16), pltpu.SemaphoreType.DMA((8,))],
        compiler_params=pltpu.CompilerParams(vmem_limit_bytes=8 * 2**20),
        cost_estimate=pl.CostEstimate(flops=1, bytes_accessed=1, transcendentals=0),
        name="finish_second",
    )(first, away, top, bottom, y2, x2)


def _finish(kernel, out_shape, operands):
    return pl.pallas_call(
        kernel,
        out_shape=out_shape,
        in_specs=[VMEM] * len(operands),
        out_specs=jax.tree.map(lambda _: VMEM, out_shape),
        compiler_params=pltpu.CompilerParams(vmem_limit_bytes=8 * 2**20),
        cost_estimate=pl.CostEstimate(flops=1, bytes_accessed=1, transcendentals=0),
        name="finish",
    )(*operands)


def _flip(x, axis, bits):
    n = lax.axis_size(axis)
    return lax.ppermute(x, axis, [(i, i ^ bits) for i in range(n)])


def per_device_fast(queries, keys, values, out_weight, doc_lengths, owners):
    places = lax.axis_size("ctx")
    queries, keys, values, out_weight = (
        pltpu.with_memory_space_constraint(x, pltpu.HBM) for x in (queries, keys, values, out_weight))
    kv0 = _join_keys_values(keys, values)
    kv2 = lax.ppermute(kv0, "ctx", [(i, i + 2) for i in range(places - 2)])
    kv1 = _flip(kv0, "ctx", 1)
    meta = jnp.concatenate([owners.reshape(-1), doc_lengths])
    weights = {}
    leaving, queries, weights["xp"] = _queries_for_other_core(("xp",), meta, queries, out_weight)
    other = _flip(leaving, "ctx", 1)
    weights["yp"], weights["xf"] = _stage_weights(("yp", "xf"), out_weight, leaving)
    kv2, weights["xf"] = lax.optimization_barrier((kv2, weights["xf"]))
    kv = (kv0, kv1, kv2, _flip(kv2, "ctx", 1))
    loaded = ("yf", "py", "px")
    ctx0, ctx2, ctx1, ctx3, *loads = _attend_groups(
        (0, 2, 1, 3), loaded, doc_lengths.shape[0], meta, queries, other, kv, out_weight)
    weights.update(zip(loaded, loads))
    ctx1, ctx3 = _flip(ctx1, "ctx", 2), _flip(ctx3, "ctx", 6)

    xp, yp, joined = _join(ctx0, ctx2, weights)
    x1p, y1p = _flip(xp, "head", 1), _flip(yp, "head", 2)
    xf, yf = _two_rows("last_rows", joined, weights, ("xf", "yf"))
    x1f, y1f = _flip(xf, "head", 1), _flip(yf, "head", 2)
    weights["k0"], weights["k1"] = _stage_weights(("k0", "k1"), out_weight, joined)
    joined, weights["k0"], ctx1, ctx3 = lax.optimization_barrier((joined, weights["k0"], ctx1, ctx3))
    y2, x2 = _two_rows("pass_rows", joined, weights, ("py", "px"))
    y2, x2 = _add(y2, x1p), _add(x2, y1p)
    weights["xp"], y2, x2 = lax.optimization_barrier((weights["xp"], y2, x2))
    y2, x2 = _flip(y2, "head", 2), _flip(x2, "head", 1)

    xp, yp, joined2 = _join(ctx1, ctx3, weights)
    xp, yp, x1f, y1f = lax.optimization_barrier((xp, yp, x1f, y1f))
    next_x1p, next_y1p = _flip(xp, "head", 1), _flip(yp, "head", 2)
    xf, yf = _two_rows("last_rows", joined2, weights, ("xf", "yf"))
    next_x1f, next_y1f = _flip(xf, "head", 1), _flip(yf, "head", 2)
    keep, next_keep = _keep_rows(joined, joined2, weights)
    rows, tokens = keep.shape
    first, away = _finish(_finish_first_kernel, [
        jax.ShapeDtypeStruct((rows, tokens), jnp.bfloat16),
        jax.ShapeDtypeStruct((rows // 2, tokens), jnp.bfloat16),
    ], (keep, x1f, y1f, y2, x2))
    joined2, away = lax.optimization_barrier((joined2, away))
    away = _flip(away, "ctx", 4)
    y2, x2 = _two_rows("pass_rows", joined2, weights, ("py", "px"))
    y2, x2 = _add(y2, next_x1p), _add(x2, next_y1p)
    y2, x2 = _flip(y2, "head", 2), _flip(x2, "head", 1)
    away = _finish(_unpack_kernel, [jax.ShapeDtypeStruct((rows, tokens), jnp.bfloat16)], (away,))[0]
    away, next_keep = lax.optimization_barrier((away, next_keep))
    bottom = _half_sum(1, next_keep, next_y1f)
    bottom, next_keep = lax.optimization_barrier((bottom, next_keep))
    top = _half_sum(0, next_keep, next_x1f)
    return _finish_second(first, away, top, bottom, y2, x2)


def solution(mesh):
    in_specs = (P("ctx", "head"), P("ctx", "head"), P("ctx", "head"), P(None, "head"), P(), P())
    out_specs = P("head", "ctx")
    fast = mesh.shape["ctx"] == PIECES and mesh.shape["head"] == N_FAST_HEAD
    return jax.shard_map(
        per_device_fast if fast else per_device, mesh=mesh, in_specs=in_specs, out_specs=out_specs, check_vma=False
    )
```
